32 devices in a mesh: section: 2 (over x), dp: 16 (over z, y, core).
Axes of the slice: x: 2, y: 2, z: 4, core: 2. Of those that a mesh axis runs over, the one named last changes fastest.
Arguments:
- text_in: bfloat16 [10240, 768], P('dp'), may hold values from -6 to 6
- cotangent: bfloat16 [10240, 768], P('dp'), may hold values from -6 to 6
- images: bfloat16 [256, 145, 1024], P('dp'), may hold values from -6 to 6
- segment_ids: int32 [256, 40], P('dp'), may hold values from 0 to 2, never falling along the last dimension, each value on 1 to 24 neighbouring positions
- row_image: int32 [64, 4], P('dp'), may hold values from 0 to 3, each once within a row
- self_qkv: bfloat16 [2, 768, 2304], P('section'), may hold values from -0.21875 to 0.21875
- self_out: bfloat16 [2, 768, 768], P('section'), may hold values from -0.75 to 0.75
- ffn_up: bfloat16 [2, 768, 3072], P('section'), may hold values from -0.21875 to 0.21875
- ffn_down: bfloat16 [2, 3072, 768], P('section'), may hold values from -0.109375 to 0.109375
- norm_gain: float32 [2, 2, 768], P('section'), may hold values from 0.25 to 1.75
- norm_bias: float32 [2, 2, 768], P('section'), may hold values from -1.75 to 1.75
- image_kv: bfloat16 [1024, 1536], P(None, 'section'), may hold values from -0.1875 to 0.1875
- cross_query: bfloat16 [768, 768], replicated, may hold values from -0.21875 to 0.21875
- cross_out: bfloat16 [768, 768], replicated, may hold values from -2.5 to 2.5
- cross_gain: float32 [768], replicated, may hold values from 0.25 to 1.75
- cross_bias: float32 [768], replicated, may hold values from -1.75 to 1.75
Outputs:
- layer_outputs: bfloat16 [2, 10240, 768], P('section', 'dp')
- input_grads: float32 [2, 10240, 768], P('section', 'dp')
- image_grad: float32 [256, 145, 1024], P('dp', None, 'section')
- grad_self_qkv: float32 [2, 768, 2304], P('section', 'dp')
- grad_self_out: float32 [2, 768, 768], P('section', 'dp')
- grad_ffn_up: float32 [2, 768, 3072], P('section', 'dp')
- grad_ffn_down: float32 [2, 3072, 768], P('section', 'dp')
- grad_norm_gain: float32 [2, 2, 768], P('section', None, 'dp')
- grad_norm_bias: float32 [2, 2, 768], P('section', None, 'dp')
- grad_image_kv: float32 [1024, 1536], P('dp', 'section')
- grad_cross_query: float32 [768, 768], P(None, ('section', 'dp'))
- grad_cross_out: float32 [768, 768], P(None, ('section', 'dp'))
- grad_cross_gain: float32 [768], P(('section', 'dp'))
- grad_cross_bias: float32 [768], P(('section', 'dp'))
The draws below stay inside these ranges and needn't reach their ends.
Inputs may be any that keep to these rules, and one draw needn't show every extreme that they name: `segment_ids`: each row of 40 tokens holds 3 texts in order, each of 1 to 24 tokens, one of exactly 24. row_image[b] names each of the 4 images of rows b * 4 to (b + 1) * 4 - 1 once.
All inputs are finite; a program needn't handle non-finite values.
Results may differ from the reference program's by a relative error of at most 0.035.
Values may be sent and summed in bfloat16 or wider, within the bound.
A program may use at most 832 MiB of HBM per device.

```python
import math
import jax
import jax.numpy as jnp
import numpy as np
from jax import lax

D = 768
HEADS = 12
FF = 3072
IMGW = 1024
PATCH = 145
LEN = 40
SEGS = 3
SEGMOST = 24
ROWS_MB = 4
ROWS = 256
TOKENS = 10240


def levels(own_key, extent, cuts, low, high):
    gain, own = 1.0, jax.random.fold_in(own_key, 6)
    for axis_at, shards_of in cuts:
        heights = jnp.exp(jax.random.uniform(jax.random.fold_in(own, axis_at), (shards_of,), jnp.float32, low / len(cuts), high / len(cuts)))
        gain = gain * jnp.repeat(heights, extent[axis_at] // shards_of).reshape([-1 if axis == axis_at else 1 for axis in range(len(extent))])
    return gain


def length_profile(count, total, limit, lean):
    weights = [(1 << 20) // math.isqrt(standing ** lean) + 1 for standing in range(2, count + 1)]
    rest, holding = total - limit - (count - 1), [1] * (count - 1)
    while rest > 0:
        free = [i for i in range(count - 1) if holding[i] < limit]
        pool, remaining = sum([weights[i] for i in free]), rest
        for i in free:
            extra = min(limit - holding[i], max(1, remaining * weights[i] // pool), rest)
            holding[i] = holding[i] + extra
            rest = rest - extra
    return np.array([limit] + holding)


def uneven_parts(stream_key, amount, total, bound, lean):
    if amount == 2:
        one = jax.random.randint(stream_key, (), max(1, total - bound), min(bound, total - 1) + 1)
        return jnp.stack([one, total - one])
    sizes = jnp.asarray(length_profile(amount, total, bound, lean), jnp.int32)
    pairs = (amount - 1) // 2
    source_of, taker = sizes[1:1 + 2 * pairs:2], sizes[2:2 + 2 * pairs:2]
    room = jnp.minimum(source_of - 1, bound - taker)
    moved = jax.random.randint(jax.random.fold_in(stream_key, 1), (pairs,), 0, 1 << 20) % (room + 1)
    sizes = sizes.at[1:1 + 2 * pairs:2].set(source_of - moved).at[2:2 + 2 * pairs:2].set(taker + moved)
    return sizes[jax.random.permutation(jax.random.fold_in(stream_key, 2), amount)]


def gaussian(key, extent, scale, reach, cuts=(), kind=jnp.bfloat16):
    factor_of = levels(key, extent, cuts, -0.22, 0.18) if cuts else 1.0
    drawn = jax.random.normal(key, extent, jnp.float32) * scale * factor_of
    return jnp.minimum(jnp.maximum(drawn, -reach), reach).astype(kind)


def setup_inputs(seed: int = 0) -> dict:
    keys = jax.random.split(jax.random.key(seed), 17)
    text_in = gaussian(keys[0], (TOKENS, D), 1.0, 6.0, ((0, 16),))
    cotangent = gaussian(keys[1], (TOKENS, D), 1.0, 6.0, ((0, 16),))
    images = gaussian(keys[2], (ROWS, PATCH, IMGW), 1.0, 6.0, ((0, 16),))
    segment_ids = jax.vmap(lambda own: jnp.searchsorted(jnp.cumsum(uneven_parts(own, SEGS, LEN, SEGMOST, 0)), jnp.arange(LEN), side="right"))(jax.random.split(keys[3], ROWS)).reshape((ROWS, LEN)).astype(jnp.int32)
    row_image = jax.vmap(lambda own: jax.random.permutation(own, ROWS_MB))(jax.random.split(keys[4], (ROWS // ROWS_MB))).reshape((ROWS // ROWS_MB, ROWS_MB)).astype(jnp.int32)
    self_qkv = gaussian(keys[5], (2, D, 3 * D), D ** -0.5, 0.21875, ((0, 2),))
    self_out = gaussian(keys[6], (2, D, D), (max(D * SEGS // LEN, 1)) ** -0.5, 0.75, ((0, 2),))
    ffn_up = gaussian(keys[7], (2, D, FF), D ** -0.5, 0.21875, ((0, 2),))
    ffn_down = gaussian(keys[8], (2, FF, D), FF ** -0.5, 0.109375, ((0, 2),))
    norm_gain = jnp.clip(1.0 + 0.15 * jax.random.normal(keys[9], (2, 2, D), jnp.float32), 0.25, 1.75)
    norm_bias = gaussian(keys[10], (2, 2, D), 0.3, 1.75, ((0, 2),), jnp.float32)
    image_kv = gaussian(keys[11], (IMGW, 2 * D), IMGW ** -0.5, 0.1875, ((1, 2),))
    cross_query = gaussian(keys[12], (D, D), D ** -0.5, 0.21875)
    cross_out = gaussian(keys[13], (D, D), (max(D // PATCH, 1)) ** -0.5, 2.5)
    cross_gain = jnp.clip(1.0 + 0.15 * jax.random.normal(keys[14], (D,), jnp.float32), 0.25, 1.75)
    cross_bias = gaussian(keys[15], (D,), 0.3, 1.75, (), jnp.float32)
    return dict(text_in=text_in, cotangent=cotangent, images=images, segment_ids=segment_ids, row_image=row_image, self_qkv=self_qkv, self_out=self_out, ffn_up=ffn_up, ffn_down=ffn_down, norm_gain=norm_gain, norm_bias=norm_bias, image_kv=image_kv, cross_query=cross_query, cross_out=cross_out, cross_gain=cross_gain, cross_bias=cross_bias)


EPSILON = 1e-06
MASKED = -1e+30
PRECISE = lax.Precision.HIGHEST

@jax.custom_vjp
def low(v):
    return lax.optimization_barrier(v.astype(jnp.bfloat16)).astype(jnp.float32)

@jax.custom_vjp
def low_back(v):
    return v

def low_keep(v):
    return (low(v), None)

def low_pass(kept, grad):
    return (grad,)

def back_keep(v):
    return (v, None)

def back_low(kept, grad):
    return (low(grad),)
low.defvjp(low_keep, low_pass)
low_back.defvjp(back_keep, back_low)

def matmul(left, right):
    return jnp.dot(left, right, precision=PRECISE, preferred_element_type=jnp.float32)

def layer_norm(summed, gain_vec, bias_vec):
    average = lax.optimization_barrier(jnp.mean(summed, -1, keepdims=True))
    centred = summed - average
    variance = lax.optimization_barrier(jnp.mean(centred * centred, -1, keepdims=True))
    return centred * lax.rsqrt(variance + EPSILON) * gain_vec + bias_vec

def gelu_value(preact):
    return 0.5 * preact * (1.0 + jax.scipy.special.erf(preact * math.sqrt(0.5)))

def attend(queries, key_rows, value_rows, allowed):
    num_rows = queries.shape[0]
    head_q = queries.reshape(num_rows, HEADS, -1)
    head_k = key_rows.reshape(key_rows.shape[0], HEADS, -1)
    head_v = value_rows.reshape(value_rows.shape[0], HEADS, -1)
    scaling = 1.0 / math.sqrt(D // HEADS)
    scores = jnp.einsum('qhd,khd->hqk', head_q, head_k, precision=PRECISE) * scaling
    scores = low_back(jnp.where(allowed[None], scores, MASKED))
    largest = lax.optimization_barrier(jnp.max(scores, -1, keepdims=True))
    unnormed = jnp.exp(scores - largest)
    soft_weights = unnormed / lax.optimization_barrier(jnp.sum(unnormed, -1, keepdims=True))
    attended = jnp.einsum('hqk,khd->qhd', low(soft_weights), head_v, precision=PRECISE)
    return attended.reshape(num_rows, -1)

def self_block(residual, w_qkv, w_out, gain_vec, bias_vec, allowed):
    projected = low_back(low(matmul(low(residual), w_qkv)))
    queries, key_rows, value_rows = jnp.split(projected, 3, axis=-1)
    attended = low_back(low(attend(queries, key_rows, value_rows, allowed)))
    return layer_norm(residual + low_back(matmul(attended, w_out)), gain_vec, bias_vec)

def cross_block(residual, key_rows, value_rows, w_query, w_out, gain_vec, bias_vec, allowed):
    queries = low_back(low(matmul(low(residual), w_query)))
    attended = low_back(low(attend(queries, key_rows, value_rows, allowed)))
    return layer_norm(residual + low_back(matmul(attended, w_out)), gain_vec, bias_vec)

def ffn_block(residual, w_up, w_down, gain_vec, bias_vec):
    preact = low_back(matmul(low(residual), w_up))
    branch = low_back(matmul(low(gelu_value(preact)), w_down))
    return layer_norm(residual + branch, gain_vec, bias_vec)

def build_masks(segments, pictures):
    row_count = segments.shape[0]
    token_ids = (segments + LEN * jnp.arange(row_count, dtype=jnp.int32)[:, None]).reshape(-1)
    self_mask = token_ids[:, None] == token_ids[None, :]
    token_image = jnp.repeat(pictures, LEN)
    patch_image = jnp.arange(row_count * PATCH, dtype=jnp.int32) // PATCH
    return (self_mask, token_image[:, None] == patch_image[None, :])

def block_forward(weights, text_rows, boundary_shift, image_rows, self_mask, cross_mask):
    w_qkv, w_out, w_up, w_down, gain_table, bias_table, w_img, w_query, w_cross, cross_gains, cross_shift = weights
    text_mid = self_block(text_rows, w_qkv[0], w_out[0], gain_table[0, 0], bias_table[0, 0], self_mask)
    text_out = ffn_block(text_mid, w_up[0], w_down[0], gain_table[0, 1], bias_table[0, 1])
    boundary = low_back(low(text_out)) + boundary_shift
    key_rows = low_back(low(matmul(low(image_rows), w_img[:, :D])))
    value_rows = low_back(low(matmul(low(image_rows), w_img[:, D:])))
    joined_mid = self_block(boundary, w_qkv[1], w_out[1], gain_table[1, 0], bias_table[1, 0], self_mask)
    joined_cross = cross_block(joined_mid, key_rows, value_rows, w_query, w_cross, cross_gains, cross_shift, cross_mask)
    joined_out = ffn_block(joined_cross, w_up[1], w_down[1], gain_table[1, 1], bias_table[1, 1])
    return (joined_out, text_out)

def add_pair(earlier, increment):
    return earlier + increment

def reference(text_in, cotangent, images, segment_ids, row_image, self_qkv, self_out, ffn_up, ffn_down, norm_gain, norm_bias, image_kv, cross_query, cross_out, cross_gain, cross_bias):
    weights = tuple((tensor.astype(jnp.float32) for tensor in (self_qkv, self_out, ffn_up, ffn_down, norm_gain, norm_bias, image_kv, cross_query, cross_out, cross_gain, cross_bias)))
    blocks_all = ROWS // ROWS_MB
    tokens_mb = ROWS_MB * LEN
    text_blocks = text_in.astype(jnp.float32).reshape(blocks_all, tokens_mb, D)
    grad_blocks = cotangent.astype(jnp.float32).reshape(blocks_all, tokens_mb, D)
    image_blocks = images.astype(jnp.float32).reshape(blocks_all, ROWS_MB * PATCH, IMGW)
    segment_blocks = segment_ids.reshape(blocks_all, ROWS_MB, LEN)

    def one_block(totals, inputs):
        text_rows, grad_rows, image_rows, segments, pictures = inputs
        self_mask, cross_mask = build_masks(segments, pictures)

        def forward(weight_set, text_part, shift_part, image_part):
            return block_forward(weight_set, text_part, shift_part, image_part, self_mask, cross_mask)
        joined_out, pullback, text_out = jax.vjp(forward, weights, text_rows, jnp.zeros_like(text_rows), image_rows, has_aux=True)
        grad_weights, grad_text, grad_shift, grad_image = pullback(grad_rows)
        totals = jax.tree.map(add_pair, totals, grad_weights)
        return (totals, (text_out.astype(jnp.bfloat16), joined_out.astype(jnp.bfloat16), grad_text, grad_shift, grad_image))
    start_totals = tuple((jnp.zeros_like(tensor) for tensor in weights))
    totals, stacked = lax.scan(one_block, start_totals, (text_blocks, grad_blocks, image_blocks, segment_blocks, row_image))
    text_outs, joined_outs, grad_text, grad_shift, grad_image = stacked
    layer_outputs = jnp.stack([text_outs.reshape(TOKENS, D), joined_outs.reshape(TOKENS, D)])
    input_grads = jnp.stack([grad_text.reshape(TOKENS, D), grad_shift.reshape(TOKENS, D)])
    image_grad = grad_image.reshape(ROWS, PATCH, IMGW)
    grad_qkv, grad_out, grad_up, grad_down, grad_gain, grad_bias, grad_img, grad_query, grad_cross, grad_cgain, grad_cbias = totals
    return (layer_outputs, input_grads, image_grad, grad_qkv, grad_out, grad_up, grad_down, grad_gain, grad_bias, grad_img, grad_query, grad_cross, grad_cgain, grad_cbias)
```

```python
import functools
import math

import jax
import jax.numpy as jnp
from jax import lax
from jax.experimental import pallas as pl
from jax.experimental.pallas import tpu as pltpu
from jax.sharding import PartitionSpec as P

HEADS = 12
EPSILON = 1e-06
MASKED = -1e30
BF = jnp.bfloat16
F32 = jnp.float32
PAD = 160
HALVES = 2
CHUNK = 32
LIMIT = 60 * 1024 * 1024
ANY = pl.BlockSpec(memory_space=pl.ANY)
SMEM = pl.BlockSpec(memory_space=pltpu.SMEM)
VMEM = pl.BlockSpec(memory_space=pltpu.VMEM)


def nn(left, right):
    return lax.dot_general(left, right, (((1,), (0,)), ((), ())), preferred_element_type=F32)


def nt(left, right):
    return lax.dot_general(left, right, (((1,), (1,)), ((), ())), preferred_element_type=F32)


def tn(left, right):
    return lax.dot_general(left, right, (((0,), (0,)), ((), ())), preferred_element_type=F32)


class Copies:
    def __init__(self, sems):
        self.sems, self.used, self.open = sems, 0, []

    def load(self, source, target):
        copy = pltpu.make_async_copy(source, target, self.sems.at[self.used])
        self.used += 1
        copy.start()
        return copy

    def store(self, source, target):
        self.open.append(self.load(source, target))

    def finish(self):
        for copy in self.open:
            copy.wait()


def by_rows(count, body):
    @pl.loop(0, count // CHUNK)
    def _(step):
        body(pl.ds(pl.multiple_of(step * CHUNK, CHUNK), CHUNK))


def standard(summed):
    centred = summed - jnp.mean(summed, -1, keepdims=True)
    inv_std = lax.rsqrt(jnp.mean(centred * centred, -1, keepdims=True) + EPSILON)
    return centred * inv_std, inv_std


def fold(value):
    return jnp.sum(value.reshape(value.shape[0] // 8, 8, value.shape[1]), 0)


def norm_back(grad_out, normed, inv_std, gain, sums, slot):
    sums[slot, 0] += fold(grad_out * normed)
    sums[slot, 1] += fold(grad_out)
    grad_normed = grad_out * gain
    return inv_std * (
        grad_normed
        - jnp.mean(grad_normed, -1, keepdims=True)
        - normed * jnp.mean(grad_normed * normed, -1, keepdims=True)
    )


def gelu_both(preact):
    size = jnp.abs(preact)
    bell = jnp.exp(-0.5 * preact * preact)
    t = 1.0 / (1.0 + (0.3275911 * math.sqrt(0.5)) * size)
    series = t * (
        0.5 * 0.254829592
        + t * (-0.5 * 0.284496736 + t * (0.5 * 1.421413741 + t * (-0.5 * 1.453152027 + t * (0.5 * 1.061405429))))
    )
    tail = series * bell
    below = jnp.where(preact >= 0.0, 1.0 - tail, tail)
    return preact * below, below + preact * bell * (1.0 / math.sqrt(2.0 * math.pi))


def head_lanes(width, head_dim):
    lane = lax.broadcasted_iota(jnp.int32, (1, width), 1)
    first = jnp.where(lane < head_dim, 1.0, 0.0)
    return first, 1.0 - first


def self_attend(qkv, mask, probs, att, groups, first_group, span, head_dim):
    width = 2 * head_dim
    model = att.shape[1]
    pairs = model // width
    low, high = head_lanes(width, head_dim)
    scale = 1.0 / math.sqrt(head_dim)
    low_b, high_b = (low * scale).astype(BF), (high * scale).astype(BF)

    @pl.loop(0, groups)
    def _(g):
        rows = pl.ds(pl.multiple_of(g * span, span), span)
        bias = mask[first_group + g]
        bias = jnp.concatenate([bias, bias], 0)
        for p in range(pairs):
            cols = p * width
            q = qkv[rows, cols : cols + width]
            k = qkv[rows, model + cols : model + cols + width]
            v = qkv[rows, 2 * model + cols : 2 * model + cols + width]
            both = jnp.concatenate([q * low_b, q * high_b], 0)
            scores = nt(both, k) + bias
            grown = jnp.exp(scores - jnp.max(scores, -1, keepdims=True))
            weights = (grown / jnp.sum(grown, -1, keepdims=True)).astype(BF)
            probs[g * pairs + p] = weights
            out = nn(weights, v)
            att[rows, cols : cols + width] = (out[:span] * low + out[span:] * high).astype(BF)


def self_attend_back(qkv, probs, grad_att, grad_qkv, groups, span, head_dim):
    width = 2 * head_dim
    model = grad_att.shape[1]
    pairs = model // width
    low, high = head_lanes(width, head_dim)
    scale = 1.0 / math.sqrt(head_dim)
    scaled = ((low * scale).astype(BF), (high * scale).astype(BF))
    plain = (low.astype(BF), high.astype(BF))

    @pl.loop(0, groups)
    def _(g):
        rows = pl.ds(pl.multiple_of(g * span, span), span)
        for p in range(pairs):
            cols = p * width
            q = qkv[rows, cols : cols + width]
            k = qkv[rows, model + cols : model + cols + width]
            v = qkv[rows, 2 * model + cols : 2 * model + cols + width]
            go = grad_att[rows, cols : cols + width]
            both_q = jnp.concatenate([q * scaled[0], q * scaled[1]], 0)
            both_g = jnp.concatenate([go * plain[0], go * plain[1]], 0)
            weights_b = probs[g * pairs + p]
            weights = weights_b.astype(F32)
            grad_w = nt(both_g, v)
            grad_s = (weights * (grad_w - jnp.sum(grad_w * weights, -1, keepdims=True))).astype(BF)
            out = nn(grad_s, k)
            grad_qkv[rows, cols : cols + width] = (
                out[:span] * (low * scale) + out[span:] * (high * scale)
            ).astype(BF)
            grad_qkv[rows, model + cols : model + cols + width] = tn(grad_s, both_q).astype(BF)
            grad_qkv[rows, 2 * model + cols : 2 * model + cols + width] = tn(weights_b, both_g).astype(BF)


def cross_attend(queries, keys, vals, image, first_row, probs, out, row_count, length, patches, head_dim):
    width = 2 * head_dim
    pairs = queries.shape[1] // width
    low, high = head_lanes(width, head_dim)
    scale = 1.0 / math.sqrt(head_dim)
    low_s, high_s = low * scale, high * scale
    shown = lax.broadcasted_iota(jnp.int32, (2 * length, keys.shape[1]), 1) < patches

    @pl.loop(0, row_count)
    def _(r):
        rows = pl.ds(pl.multiple_of(r * length, 8), length)
        picked = image[first_row + r]
        for p in range(pairs):
            cols = slice(p * width, p * width + width)
            q = queries[rows, cols]
            both = jnp.concatenate([q * low_s, q * high_s], 0).astype(BF)
            scores = jnp.where(shown, nt(both, keys[picked, :, cols]), MASKED)
            grown = jnp.exp(scores - jnp.max(scores, -1, keepdims=True))
            weights = (grown / jnp.sum(grown, -1, keepdims=True)).astype(BF)
            probs[r * pairs + p] = weights
            got = nn(weights, vals[picked, :, cols])
            out[rows, cols] = got[:length] * low + got[length:] * high


def cross_attend_back(
    queries, keys, vals, image, first_row, probs, grad_att, grad_q, grad_k, grad_v, row_count, length, head_dim
):
    width = 2 * head_dim
    pairs = queries.shape[1] // width
    low, high = head_lanes(width, head_dim)
    scale = 1.0 / math.sqrt(head_dim)
    low_s, high_s = low * scale, high * scale

    @pl.loop(0, row_count)
    def _(r):
        rows = pl.ds(pl.multiple_of(r * length, 8), length)
        picked = image[first_row + r]
        for p in range(pairs):
            cols = slice(p * width, p * width + width)
            q = queries[rows, cols]
            go = grad_att[rows, cols]
            both_q = jnp.concatenate([q * low_s, q * high_s], 0).astype(BF)
            both_g = jnp.concatenate([go * low, go * high], 0).astype(BF)
            weights_b = probs[r * pairs + p]
            weights = weights_b.astype(F32)
            grad_w = nt(both_g, vals[picked, :, cols])
            grad_s = (weights * (grad_w - jnp.sum(grad_w * weights, -1, keepdims=True))).astype(BF)
            got = nn(grad_s, keys[picked, :, cols])
            grad_q[rows, cols] = got[:length] * low_s + got[length:] * high_s
            grad_k[picked, :, cols] = tn(grad_s, both_q).astype(BF)
            grad_v[picked, :, cols] = tn(weights_b, both_g).astype(BF)


def grow(entry, w_up, preact, hidden, slope):
    tile = preact.shape[1]
    for j in range(hidden.shape[1] // tile):
        cols = slice(j * tile, j * tile + tile)
        preact[...] = nn(entry[...], w_up[:, cols])

        def body(rows):
            value, rise = gelu_both(preact[rows, :])
            hidden[rows, cols] = value.astype(BF)
            slope[rows, cols] = rise.astype(BF)

        by_rows(preact.shape[0], body)


def shrink(branch, w_down, slope, grad_pre):
    tile = branch.shape[1]
    for j in range(slope.shape[1] // tile):
        cols = slice(j * tile, j * tile + tile)
        grad_pre[:, cols] = (nt(branch[...], w_down[cols, :]) * slope[:, cols].astype(F32)).astype(BF)


def text_forward_kernel(half, span, flag, gains, biases, mask, text, wqkv, wo, w1, w2, *refs):
    (lay, zb, hidden, att), refs = refs[4:8] if half else refs[:4], refs[8:] if half else refs[4:]
    (bnd, y1, y3, qkv, probs, slope), refs = refs[:6], refs[6:]
    (x_s, wqkv_s, wo_s, w1_s, w2_s, qkv_s, probs_s, att_s, y1_s, mid_s, zb_s, pre_s, hid_s, slo_s, y3_s, out_s, sems) = refs
    count = x_s.shape[0]
    own = pl.ds(half * count, count)

    @pl.when(flag[0] == 0)
    def _():
        cp = Copies(sems)
        gets = [cp.load(text.at[own], x_s)] + [
            cp.load(a, b) for a, b in ((wqkv, wqkv_s), (wo, wo_s), (w1, w1_s), (w2, w2_s))
        ]
        gets[0].wait()
        gets[1].wait()
        qkv_s[...] = nn(x_s[...], wqkv_s[...]).astype(BF)
        cp.store(qkv_s, qkv)
        groups = count // span
        self_attend(qkv_s, mask, probs_s, att_s, groups, half * groups, span, x_s.shape[1] // HEADS)
        cp.store(probs_s, probs)
        cp.store(att_s, att.at[own])
        gets[2].wait()
        y1_s[...] = x_s[...].astype(F32) + nn(att_s[...], wo_s[...])
        cp.store(y1_s, y1)

        def first(rows):
            value = standard(y1_s[rows, :])[0] * gains[0:1, :] + biases[0:1, :]
            mid_s[rows, :] = value
            zb_s[rows, :] = value.astype(BF)

        by_rows(count, first)
        cp.store(zb_s, zb.at[own])
        gets[3].wait()
        grow(zb_s, w1_s, pre_s, hid_s, slo_s)
        cp.store(hid_s, hidden.at[own])
        cp.store(slo_s, slope)
        gets[4].wait()
        y3_s[...] = mid_s[...] + nn(hid_s[...], w2_s[...])
        cp.store(y3_s, y3)

        def second(rows):
            out_s[rows, :] = (standard(y3_s[rows, :])[0] * gains[1:2, :] + biases[1:2, :]).astype(BF)

        by_rows(count, second)
        cp.store(out_s, bnd)
        cp.store(out_s, lay.at[own])
        cp.finish()


def text_ffn_back_kernel(half, flag, gains, grad, y3, slope, w1, w2, *refs):
    (df, du, sums), refs = refs[3:6], refs[6:]
    dmid, refs = refs[0], refs[1:]
    (g_s, y3_s, slo_s, w1_s, w2_s, dy_s, df_s, du_s, dm_s, sum_s, sems) = refs
    count = g_s.shape[0]
    own = pl.ds(half * count, count)

    @pl.when(flag[0] == 0)
    def _():
        cp = Copies(sems)
        gets = [
            cp.load(a, b) for a, b in ((grad, g_s), (y3, y3_s), (w2, w2_s), (slope, slo_s), (w1, w1_s))
        ]
        sum_s[...] = jnp.zeros_like(sum_s)
        gets[0].wait()
        gets[1].wait()

        def body(rows):
            normed, inv_std = standard(y3_s[rows, :])
            value = norm_back(g_s[rows, :].astype(F32), normed, inv_std, gains[1:2, :], sum_s, 0)
            dy_s[rows, :] = value
            df_s[rows, :] = value.astype(BF)

        by_rows(count, body)
        cp.store(df_s, df.at[own])
        cp.store(sum_s, sums.at[half, pl.ds(1, 1)])
        gets[2].wait()
        gets[3].wait()
        shrink(df_s, w2_s, slo_s, du_s)
        cp.store(du_s, du.at[own])
        gets[4].wait()
        dm_s[...] = dy_s[...] + nt(du_s[...], w1_s[...])
        cp.store(dm_s, dmid)
        cp.finish()


def text_self_back_kernel(half, span, flag, gains, dmid, y1, qkv, probs, wo, wqkv, *refs):
    (da, dqkv, ig, sums), refs = refs[4:8], refs[8:]
    (dm_s, y1_s, qkv_s, probs_s, wo_s, wqkv_s, dy_s, da_s, datt_s, dqkv_s, ig_s, sum_s, sems) = refs
    count = dm_s.shape[0]
    own = pl.ds(half * count, count)

    @pl.when(flag[0] == 0)
    def _():
        cp = Copies(sems)
        gets = [
            cp.load(a, b)
            for a, b in ((dmid, dm_s), (y1, y1_s), (wo, wo_s), (qkv, qkv_s), (probs, probs_s), (wqkv, wqkv_s))
        ]
        sum_s[...] = jnp.zeros_like(sum_s)
        gets[0].wait()
        gets[1].wait()

        def body(rows):
            normed, inv_std = standard(y1_s[rows, :])
            value = norm_back(dm_s[rows, :], normed, inv_std, gains[0:1, :], sum_s, 0)
            dy_s[rows, :] = value
            da_s[rows, :] = value.astype(BF)

        by_rows(count, body)
        cp.store(da_s, da.at[own])
        cp.store(sum_s, sums.at[half, pl.ds(0, 1)])
        gets[2].wait()
        datt_s[...] = nt(da_s[...], wo_s[...]).astype(BF)
        gets[3].wait()
        gets[4].wait()
        self_attend_back(qkv_s, probs_s, datt_s, dqkv_s, count // span, span, dm_s.shape[1] // HEADS)
        cp.store(dqkv_s, dqkv.at[own])
        gets[5].wait()
        ig_s[...] = dy_s[...] + nt(dqkv_s[...], wqkv_s[...])
        cp.store(ig_s, ig.at[own])
        cp.finish()


JOIN_BUFS = 16


def joining_kernel(half, span, length, patches, flag, image, gains, biases, cgain, cbias, mask, bnd, cot,
                   wqkv, wo, w1, w2, wq, wc, keys, vals, *refs):
    refs = refs[JOIN_BUFS:] if half else refs[4:]
    (lay, zb, hidden, att, ig, df, du, da, dqkv, sums, midb, dq, catt, dca, dkey, dval), refs = refs[:16], refs[16:]
    back, refs = refs[0], refs[1:]
    (x_s, wqkv_s, wo_s, w1_s, w2_s, wq_s, wc_s, key_s, val_s, cot_s, qkv_s, probs_s, att_s, y1_s, mid_s, midb_s,
     qc_s, cprobs_s, cat_s, catb_s, y2_s, zb_s, pre_s, hid_s, slo_s, y3_s, lay_s, df_s, dy_s, du_s, dz_s, dca_s,
     dkey_s, dval_s, dqb_s, da_s, datt_s, dqkv_s, sum_s, sems) = refs
    count, model = x_s.shape
    head_dim = model // HEADS
    own = pl.ds(half * count, count)
    row_count = count // length
    groups = count // span
    pictures = pl.ds(half * row_count, row_count)

    @pl.when(flag[0] == 1)
    def _():
        cp = Copies(sems)
        (g_x, g_qkv, g_o, g_q, g_key, g_val, g_c, g_1, g_2, g_cot) = [
            cp.load(a, b)
            for a, b in (
                (bnd, x_s), (wqkv, wqkv_s), (wo, wo_s), (wq, wq_s), (keys.at[pictures], key_s),
                (vals.at[pictures], val_s), (wc, wc_s), (w1, w1_s), (w2, w2_s), (cot.at[own], cot_s),
            )
        ]
        sum_s[...] = jnp.zeros_like(sum_s)
        g_x.wait()
        g_qkv.wait()
        qkv_s[...] = nn(x_s[...], wqkv_s[...]).astype(BF)
        self_attend(qkv_s, mask, probs_s, att_s, groups, half * groups, span, head_dim)
        cp.store(att_s, att.at[own])
        g_o.wait()
        y1_s[...] = x_s[...].astype(F32) + nn(att_s[...], wo_s[...])

        def first(rows):
            value = standard(y1_s[rows, :])[0] * gains[0:1, :] + biases[0:1, :]
            mid_s[rows, :] = value
            midb_s[rows, :] = value.astype(BF)

        by_rows(count, first)
        cp.store(midb_s, midb.at[own])
        g_q.wait()
        qc_s[...] = nn(midb_s[...], wq_s[...]).astype(BF).astype(F32)
        g_key.wait()
        g_val.wait()
        cross_attend(qc_s, key_s, val_s, image, half * row_count, cprobs_s, cat_s, row_count, length, patches, head_dim)
        catb_s[...] = cat_s[...].astype(BF)
        cp.store(catb_s, catt.at[own])
        g_c.wait()
        y2_s[...] = mid_s[...] + nn(catb_s[...], wc_s[...])

        def second(rows):
            value = standard(y2_s[rows, :])[0] * cgain[...] + cbias[...]
            mid_s[rows, :] = value
            zb_s[rows, :] = value.astype(BF)

        by_rows(count, second)
        cp.store(zb_s, zb.at[own])
        g_1.wait()
        grow(zb_s, w1_s, pre_s, hid_s, slo_s)
        cp.store(hid_s, hidden.at[own])
        g_2.wait()
        y3_s[...] = mid_s[...] + nn(hid_s[...], w2_s[...])
        g_cot.wait()

        def third(rows):
            normed, inv_std = standard(y3_s[rows, :])
            lay_s[rows, :] = (normed * gains[1:2, :] + biases[1:2, :]).astype(BF)
            value = norm_back(cot_s[rows, :].astype(F32), normed, inv_std, gains[1:2, :], sum_s, 1)
            dy_s[rows, :] = value
            df_s[rows, :] = value.astype(BF)

        by_rows(count, third)
        cp.store(lay_s, lay.at[own])
        cp.store(df_s, df.at[own])
        shrink(df_s, w2_s, slo_s, du_s)
        cp.store(du_s, du.at[own])
        dz_s[...] = dy_s[...] + nt(du_s[...], w1_s[...])

        def fourth(rows):
            normed, inv_std = standard(y2_s[rows, :])
            value = norm_back(dz_s[rows, :], normed, inv_std, cgain[...], sum_s, 2)
            dy_s[rows, :] = value
            dca_s[rows, :] = value.astype(BF)

        by_rows(count, fourth)
        cp.store(dca_s, dca.at[own])
        cat_s[...] = nt(dca_s[...], wc_s[...]).astype(BF).astype(F32)
        cross_attend_back(qc_s, key_s, val_s, image, half * row_count, cprobs_s, cat_s, pre_s, dkey_s, dval_s,
                          row_count, length, head_dim)
        cp.store(dkey_s, dkey.at[pictures])
        cp.store(dval_s, dval.at[pictures])
        dqb_s[...] = pre_s[...].astype(BF)
        cp.store(dqb_s, dq.at[own])
        dz_s[...] = dy_s[...] + nt(dqb_s[...], wq_s[...])

        def fifth(rows):
            normed, inv_std = standard(y1_s[rows, :])
            value = norm_back(dz_s[rows, :], normed, inv_std, gains[0:1, :], sum_s, 0)
            dy_s[rows, :] = value
            da_s[rows, :] = value.astype(BF)

        by_rows(count, fifth)
        cp.store(da_s, da.at[own])
        cp.store(sum_s, sums.at[half])
        datt_s[...] = nt(da_s[...], wo_s[...]).astype(BF)
        self_attend_back(qkv_s, probs_s, datt_s, dqkv_s, groups, span, head_dim)
        cp.store(dqkv_s, dqkv.at[own])
        dz_s[...] = dy_s[...] + nt(dqkv_s[...], wqkv_s[...])
        x_s[...] = dz_s[...].astype(BF)
        cp.store(x_s, back)
        cp.store(dz_s, ig.at[own])
        cp.finish()


def project_kernel(flag, image, weight, out, packed):
    @pl.when(flag[0] == 1)
    def _():
        each, patches = image.shape[0], image.shape[1]
        packed[...] = jnp.zeros_like(packed)
        for i in range(each):
            packed[i * PAD : i * PAD + patches, :] = image[i]
        got = nn(packed[...], weight[...]).astype(BF)
        for i in range(each):
            out[i] = got[i * PAD : i * PAD + PAD]


def image_back_kernel(flag, image, dkey, dval, wk, wv, own, other, dwk, dwv, packed, sum_k, sum_v):
    step = pl.program_id(0)

    @pl.when(flag[0] == 1)
    def _():
        each, patches, width = image.shape

        @pl.when(step == 0)
        def _():
            packed[...] = jnp.zeros_like(packed)
            sum_k[...] = jnp.zeros_like(sum_k)
            sum_v[...] = jnp.zeros_like(sum_v)

        for i in range(each):
            packed[i * PAD : i * PAD + patches, :] = image[i]
        grad_k = dkey[...].reshape(each * PAD, dkey.shape[2])
        grad_v = dval[...].reshape(each * PAD, dval.shape[2])
        sum_k[...] += tn(packed[...], grad_k)
        sum_v[...] += tn(packed[...], grad_v)
        part = width // 2
        got = nt(grad_k, wk[part:, :]) + nt(grad_v, wv[part:, :])
        for i in range(each):
            own[i] = got[i * PAD : i * PAD + patches]
        got = (nt(grad_k, wk[:part, :]) + nt(grad_v, wv[:part, :])).astype(BF)
        for i in range(each):
            other[i] = got[i * PAD : i * PAD + patches]

        @pl.when(step == pl.num_programs(0) - 1)
        def _():
            dwk[...] = sum_k[...].astype(BF)
            dwv[...] = sum_v[...].astype(BF)


def weight_grad_kernel(left, right, out):
    out[...] = tn(left[...], right[...]).astype(BF)


def weight_grad(left, right, by_left, tile=768):
    tokens, rows = left.shape
    cols = right.shape[1]
    if by_left:
        grid, specs = (rows // tile,), (lambda i: (0, i), lambda i: (0, 0), lambda i: (i, 0))
        shapes = ((tokens, tile), (tokens, cols), (tile, cols))
    else:
        grid, specs = (cols // tile,), (lambda i: (0, 0), lambda i: (0, i), lambda i: (0, i))
        shapes = ((tokens, rows), (tokens, tile), (rows, tile))
    return pl.pallas_call(
        weight_grad_kernel,
        grid=grid,
        in_specs=[pl.BlockSpec(shapes[0], specs[0]), pl.BlockSpec(shapes[1], specs[1])],
        out_specs=pl.BlockSpec(shapes[2], specs[2]),
        out_shape=jax.ShapeDtypeStruct((rows, cols), BF),
        compiler_params=pltpu.CompilerParams(vmem_limit_bytes=LIMIT),
        cost_estimate=pl.CostEstimate(
            flops=2 * tokens * rows * cols, bytes_accessed=2 * (tokens * (rows + cols) + rows * cols), transcendentals=0
        ),
        name="weight_grad",
    )(left, right)


def stage(kernel, name, smem, vmem, hbm, bufs, fresh, scratch, flops):
    arrays = [b for b in bufs if not isinstance(b, jax.ShapeDtypeStruct)]
    first = len(smem) + len(vmem) + len(hbm)
    aliases, at = {}, first
    for i, b in enumerate(bufs):
        if not isinstance(b, jax.ShapeDtypeStruct):
            aliases[at] = i
            at += 1
    outs = [jax.ShapeDtypeStruct(b.shape, b.dtype) for b in list(bufs) + list(fresh)]
    got = pl.pallas_call(
        kernel,
        in_specs=[SMEM] * len(smem) + [VMEM] * len(vmem) + [ANY] * (len(hbm) + len(arrays)),
        out_specs=[ANY] * len(outs),
        out_shape=outs,
        scratch_shapes=list(scratch) + [pltpu.SemaphoreType.DMA((40,))],
        input_output_aliases=aliases,
        compiler_params=pltpu.CompilerParams(vmem_limit_bytes=LIMIT),
        cost_estimate=pl.CostEstimate(flops=flops, bytes_accessed=sum(a.size * 2 for a in hbm), transcendentals=0),
        name=name,
    )(*smem, *vmem, *hbm, *arrays)
    return list(got[: len(bufs)]), list(got[len(bufs) :])


def spread(value, axis_size):
    return value.reshape(axis_size, value.shape[0] // axis_size, value.shape[1])


def reduce_parts(value, only):
    total = lax.axis_size("dp")
    if total != 16:
        return lax.psum_scatter(value, "dp", scatter_dimension=0, tiled=True)[0].astype(F32)
    place = lax.axis_index("dp")
    core, y, z = place % 2, (place // 2) % 2, place // 4
    rows, cols = value.shape[1:]

    def swap(sent, flip):
        perm = [(s * total + i, s * total + (i ^ flip)) for s in only for i in range(total)]
        return lax.ppermute(sent, ("section", "dp"), perm)

    def pick(array, axis, index):
        return lax.dynamic_index_in_dim(array, index, axis, keepdims=False)

    value = value.reshape(8, 2, rows, cols)
    got = swap(pick(value, 1, 1 - core), 1)
    value = (pick(value, 1, core).astype(F32) + got.astype(F32)).astype(BF)
    value = value.reshape(4, 2, rows, cols)
    got = swap(pick(value, 1, 1 - y), 2)
    value = (pick(value, 1, y).astype(F32) + got.astype(F32)).astype(BF)
    others = [swap(pick(value, 0, z ^ step), 4 * step) for step in (1, 2, 3)]
    return pick(value, 0, z).astype(F32) + others[0].astype(F32) + others[1].astype(F32) + others[2].astype(F32)


def per_device(
    text_in, cotangent, images, segment_ids, row_image, self_qkv, self_out, ffn_up, ffn_down,
    norm_gain, norm_bias, image_kv, cross_query, cross_out, cross_gain, cross_bias,
):
    tokens, model = text_in.shape
    row_total, length = segment_ids.shape
    patches, width = images.shape[1:]
    hidden_width = ffn_up.shape[2]
    block_rows = row_image.shape[1]
    head_dim = model // HEADS
    pairs = HEADS // 2
    count = tokens // HALVES
    half_rows = row_total // HALVES
    span = 2 * length
    dp = lax.axis_size("dp")
    section = lax.axis_index("section")
    is_text = section == 0
    flag = section.astype(jnp.int32).reshape(1)
    place = lax.axis_index("dp")
    wqkv, wo, w1, w2 = self_qkv[0], self_out[0], ffn_up[0], ffn_down[0]
    gains, biases = norm_gain[0], norm_bias[0]
    cgain, cbias = cross_gain.reshape(1, model), cross_bias.reshape(1, model)

    marks = (segment_ids + segment_ids.shape[1] * (jnp.arange(row_total, dtype=jnp.int32) % 2)[:, None]).reshape(-1, span)
    mask = jnp.where(marks[:, :, None] == marks[:, None, :], 0.0, MASKED).astype(F32)
    in_block = jnp.arange(row_total, dtype=jnp.int32) // block_rows * block_rows % half_rows
    image = row_image.reshape(-1) + in_block

    def shape(*dims, dtype=BF):
        return jax.ShapeDtypeStruct(dims, dtype)

    core = place % 2
    half_w = width // 2
    sent_w = lax.dynamic_slice_in_dim(image_kv, core * half_w, half_w, 0)
    sent_w = lax.ppermute(sent_w, "section", [(0, 1)])
    swapped = lax.ppermute(sent_w, "dp", [(i, i ^ 1) for i in range(dp)])
    key_w = jnp.where(core == 0, jnp.concatenate([sent_w, swapped], 0), jnp.concatenate([swapped, sent_w], 0))

    each = 4
    grid = row_total // each

    def project(weight):
        return pl.pallas_call(
            project_kernel,
            grid_spec=pltpu.PrefetchScalarGridSpec(
                num_scalar_prefetch=1,
                grid=(grid,),
                in_specs=[
                    pl.BlockSpec((each, patches, width), lambda i, f: (i * f[0], 0, 0)),
                    pl.BlockSpec((width, model), lambda i, f: (0, 0)),
                ],
                out_specs=pl.BlockSpec((each, PAD, model), lambda i, f: (i * f[0], 0, 0)),
                scratch_shapes=[pltpu.VMEM((each * PAD, width), BF)],
            ),
            out_shape=shape(row_total, PAD, model),
            compiler_params=pltpu.CompilerParams(vmem_limit_bytes=LIMIT),
            cost_estimate=pl.CostEstimate(
                flops=2 * row_total * PAD * width * model, bytes_accessed=12_000_000, transcendentals=0
            ),
            name="project",
        )(flag, images, weight)

    vm = pltpu.VMEM
    probs_shape = (count // span * pairs, 2 * span, span)
    text_scratch = [
        vm((count, model), BF), vm(wqkv.shape, BF), vm(wo.shape, BF), vm(w1.shape, BF), vm(w2.shape, BF),
        vm((count, 3 * model), BF), vm(probs_shape, BF), vm((count, model), BF), vm((count, model), F32),
        vm((count, model), F32), vm((count, model), BF), vm((count, model), F32), vm((count, hidden_width), BF),
        vm((count, hidden_width), BF), vm((count, model), F32), vm((count, model), BF),
    ]
    shared = [shape(tokens, model), shape(tokens, model), shape(tokens, hidden_width), shape(tokens, model)]
    linear = model * 3 * model + model * model + 2 * model * hidden_width
    kept, outward = [], []
    for half in range(HALVES):
        shared, fresh = stage(
            functools.partial(text_forward_kernel, half, span), "text_forward", [flag], [gains, biases, mask],
            [text_in, wqkv, wo, w1, w2], shared,
            [
                shape(count, model), shape(count, model, dtype=F32), shape(count, model, dtype=F32),
                shape(count, 3 * model), shape(*probs_shape), shape(count, hidden_width),
            ],
            text_scratch, 2 * count * linear,
        )
        outward.append(lax.ppermute(fresh[0], "section", [(0, 1)]))
        kept.append(fresh[1:])
    values = project(image_kv)
    keys = project(key_w)

    join_scratch = [
        vm((count, model), BF), vm(wqkv.shape, BF), vm(wo.shape, BF), vm(w1.shape, BF), vm(w2.shape, BF),
        vm(cross_query.shape, BF), vm(cross_out.shape, BF), vm((half_rows, PAD, model), BF),
        vm((half_rows, PAD, model), BF), vm((count, model), BF), vm((count, 3 * model), BF), vm(probs_shape, BF),
        vm((count, model), BF), vm((count, model), F32), vm((count, model), F32), vm((count, model), BF),
        vm((count, model), F32), vm((half_rows * pairs, 2 * length, PAD), BF), vm((count, model), F32),
        vm((count, model), BF), vm((count, model), F32), vm((count, model), BF), vm((count, model), F32),
        vm((count, hidden_width), BF), vm((count, hidden_width), BF), vm((count, model), F32), vm((count, model), BF),
        vm((count, model), BF), vm((count, model), F32), vm((count, hidden_width), BF), vm((count, model), F32),
        vm((count, model), BF), vm((half_rows, PAD, model), BF), vm((half_rows, PAD, model), BF),
        vm((count, model), BF), vm((count, model), BF), vm((count, model), BF), vm((count, 3 * model), BF),
        vm((3, 2, 8, model), F32),
    ]
    bufs = shared + [
        shape(tokens, model, dtype=F32), shape(tokens, model), shape(tokens, hidden_width), shape(tokens, model),
        shape(tokens, 3 * model), shape(HALVES, 3, 2, 8, model, dtype=F32), shape(tokens, model), shape(tokens, model),
        shape(tokens, model), shape(tokens, model), shape(row_total, PAD, model), shape(row_total, PAD, model),
    ]
    returned = []
    for half in range(HALVES):
        bufs, fresh = stage(
            functools.partial(joining_kernel, half, span, length, patches), "joining", [flag, image],
            [gains, biases, cgain, cbias, mask],
            [outward[half], cotangent, wqkv, wo, w1, w2, cross_query, cross_out, keys, values],
            bufs, [shape(count, model)], join_scratch, 4 * count * (linear + 2 * model * model),
        )
        returned.append(lax.ppermute(fresh[0], "section", [(1, 0)]))
    lay, zb, hidden, att, ig, df, du, da, dqkv, sums, midb, dq, catt, dca, dkey, dval = bufs

    own_part, other_part, grad_wk, grad_wv = pl.pallas_call(
        image_back_kernel,
        grid_spec=pltpu.PrefetchScalarGridSpec(
            num_scalar_prefetch=1,
            grid=(grid,),
            in_specs=[
                pl.BlockSpec((each, patches, width), lambda i, f: (i * f[0], 0, 0)),
                pl.BlockSpec((each, PAD, model), lambda i, f: (i * f[0], 0, 0)),
                pl.BlockSpec((each, PAD, model), lambda i, f: (i * f[0], 0, 0)),
                pl.BlockSpec((width, model), lambda i, f: (0, 0)),
                pl.BlockSpec((width, model), lambda i, f: (0, 0)),
            ],
            out_specs=[
                pl.BlockSpec((each, patches, width // 2), lambda i, f: (i * f[0], 0, 0)),
                pl.BlockSpec((each, patches, width // 2), lambda i, f: (i * f[0], 0, 0)),
                pl.BlockSpec((width, model), lambda i, f: (0, 0)),
                pl.BlockSpec((width, model), lambda i, f: (0, 0)),
            ],
            scratch_shapes=[vm((each * PAD, width), BF), vm((width, model), F32), vm((width, model), F32)],
        ),
        out_shape=[
            shape(row_total, patches, width // 2, dtype=F32), shape(row_total, patches, width // 2),
            shape(width, model), shape(width, model),
        ],
        compiler_params=pltpu.CompilerParams(vmem_limit_bytes=LIMIT),
        cost_estimate=pl.CostEstimate(
            flops=8 * row_total * PAD * width * model, bytes_accessed=25_000_000, transcendentals=0
        ),
        name="image_back",
    )(flag, images, dkey, dval, key_w, image_kv)
    image_part = lax.ppermute(other_part, "section", [(1, 0)])

    grad_cq = weight_grad(dq, midb, True)
    grad_co = weight_grad(dca, catt, True)
    sections = lax.axis_size("section")
    cross_rows = model // (sections * dp)

    def by_owner(value):
        value = value.reshape(sections, dp, cross_rows, model)
        return jnp.swapaxes(value, 0, 1).reshape(dp, sections * cross_rows, model)

    joint = jnp.concatenate(
        [spread(grad_wk, dp), spread(grad_wv, dp), by_owner(grad_cq), by_owner(grad_co)], 1
    )
    joint = reduce_parts(joint, (1,))
    image_rows = width // dp

    dmids = []
    for half in range(HALVES):
        y1, y3, qkv, probs, slope = kept[half]
        (df, du, sums), fresh = stage(
            functools.partial(text_ffn_back_kernel, half), "text_ffn_back", [flag], [gains],
            [returned[half], y3, slope, w1, w2], [df, du, sums], [shape(count, model, dtype=F32)],
            [
                vm((count, model), BF), vm((count, model), F32), vm((count, hidden_width), BF), vm(w1.shape, BF),
                vm(w2.shape, BF), vm((count, model), F32), vm((count, model), BF), vm((count, hidden_width), BF),
                vm((count, model), F32), vm((1, 2, 8, model), F32),
            ],
            4 * count * model * hidden_width,
        )
        dmids.append(fresh[0])
    down = reduce_parts(spread(weight_grad(hidden, df, True), dp), (0, 1))
    up = reduce_parts(spread(weight_grad(zb, du, False), dp), (0, 1))
    for half in range(HALVES):
        y1, y3, qkv, probs, slope = kept[half]
        (da, dqkv, ig, sums), _ = stage(
            functools.partial(text_self_back_kernel, half, span), "text_self_back", [flag], [gains],
            [dmids[half], y1, qkv, probs, wo, wqkv], [da, dqkv, ig, sums], [],
            [
                vm((count, model), F32), vm((count, model), F32), vm((count, 3 * model), BF), vm(probs_shape, BF),
                vm(wo.shape, BF), vm(wqkv.shape, BF), vm((count, model), F32), vm((count, model), BF),
                vm((count, model), BF), vm((count, 3 * model), BF), vm((count, model), F32), vm((1, 2, 8, model), F32),
            ],
            2 * count * 4 * model * model,
        )
    entry = jnp.where(is_text, text_in, jnp.concatenate(outward, 0))
    qkv_grad = reduce_parts(spread(weight_grad(entry, dqkv, False), dp), (0, 1))

    totals = jnp.sum(sums, (0, 3))
    own_norm = totals[:2].reshape(4, dp, model // dp)
    own_cross = jnp.where(is_text, 0.0, totals[2]).reshape(2, sections, dp, cross_rows)
    small = jnp.concatenate(
        [jnp.moveaxis(own_norm, 1, 0).reshape(dp, -1), jnp.moveaxis(own_cross, 2, 0).reshape(dp, -1)], 1
    )
    small = jnp.pad(small[:, None, :], ((0, 0), (0, 15), (0, model - small.shape[1]))).astype(BF)
    last = reduce_parts(jnp.concatenate([spread(weight_grad(att, da, True), dp), small], 1), (0, 1))
    out_rows = model // dp
    out_grad, small = last[:out_rows], last[out_rows]
    norm_part = small[: 4 * out_rows].reshape(2, 2, out_rows)
    cross_part = small[4 * out_rows : 4 * out_rows + 2 * sections * cross_rows].reshape(2, sections, cross_rows)

    at = 2 * image_rows
    cross_q = joint[at : at + sections * cross_rows]
    cross_o = joint[at + sections * cross_rows :]
    extra = jnp.pad(cross_part[:, 0].reshape(1, -1), ((0, 15), (0, model - 2 * cross_rows)))
    parcel = jnp.concatenate([joint[:image_rows], cross_q[:cross_rows], cross_o[:cross_rows], extra], 0).astype(BF)
    parcel = lax.ppermute(parcel, "section", [(1, 0)]).astype(F32)
    at = image_rows + 2 * cross_rows
    pick = functools.partial(jnp.where, is_text)
    grad_kv = pick(parcel[:image_rows], joint[image_rows : 2 * image_rows])
    grad_cross_q = pick(parcel[image_rows : image_rows + cross_rows], cross_q[cross_rows:]).T
    grad_cross_o = pick(parcel[image_rows + cross_rows : at], cross_o[cross_rows:]).T
    grad_cross_g = pick(parcel[at, :cross_rows], cross_part[0, 1])
    grad_cross_b = pick(parcel[at, cross_rows : 2 * cross_rows], cross_part[1, 1])
    image_grad = pick(image_part.astype(F32), own_part)
    return (
        lay[None], ig[None], image_grad, qkv_grad[None], out_grad[None], up[None], down[None],
        norm_part[:, 0][None], norm_part[:, 1][None], grad_kv, grad_cross_q, grad_cross_o, grad_cross_g, grad_cross_b,
    )


def solution(mesh):
    return jax.shard_map(
        per_device,
        mesh=mesh,
        in_specs=(
            P("dp", None),
            P("dp", None),
            P("dp", None, None),
            P("dp", None),
            P("dp", None),
            P("section", None, None),
            P("section", None, None),
            P("section", None, None),
            P("section", None, None),
            P("section", None, None),
            P("section", None, None),
            P(None, "section"),
            P(),
            P(),
            P(),
            P(),
        ),
        out_specs=(
            P("section", "dp", None),
            P("section", "dp", None),
            P("dp", None, "section"),
            P("section", "dp", None),
            P("section", "dp", None),
            P("section", "dp", None),
            P("section", "dp", None),
            P("section", None, "dp"),
            P("section", None, "dp"),
            P("dp", "section"),
            P(None, ("section", "dp")),
            P(None, ("section", "dp")),
            P(("section", "dp")),
            P(("section", "dp")),
        ),
        check_vma=False,
    )
```

```python
import functools
import math

import jax
import jax.numpy as jnp
from jax import lax
from jax.experimental import pallas as pl
from jax.experimental.pallas import tpu as pltpu
from jax.sharding import PartitionSpec as P

HEADS = 12
EPSILON = 1e-06
MASKED = -1e30
BF = jnp.bfloat16
F32 = jnp.float32
PAD = 160
HALVES = 2
CHUNK = 32
LIMIT = 60 * 1024 * 1024
ANY = pl.BlockSpec(memory_space=pl.ANY)
SMEM = pl.BlockSpec(memory_space=pltpu.SMEM)
VMEM = pl.BlockSpec(memory_space=pltpu.VMEM)


def nn(left, right):
    return lax.dot_general(left, right, (((1,), (0,)), ((), ())), preferred_element_type=F32)


def nt(left, right):
    return lax.dot_general(left, right, (((1,), (1,)), ((), ())), preferred_element_type=F32)


def tn(left, right):
    return lax.dot_general(left, right, (((0,), (0,)), ((), ())), preferred_element_type=F32)


class Copies:
    def __init__(self, sems):
        self.sems, self.used, self.open = sems, 0, []

    def load(self, source, target):
        copy = pltpu.make_async_copy(source, target, self.sems.at[self.used])
        self.used += 1
        copy.start()
        return copy

    def store(self, source, target):
        self.open.append(self.load(source, target))

    def finish(self):
        for copy in self.open:
            copy.wait()


def by_rows(count, body):
    for at in range(0, count, CHUNK):
        body(pl.ds(at, CHUNK))


def standard(summed):
    centred = summed - jnp.mean(summed, -1, keepdims=True)
    inv_std = lax.rsqrt(jnp.mean(centred * centred, -1, keepdims=True) + EPSILON)
    return centred * inv_std, inv_std


def fold(value):
    return jnp.sum(value.reshape(value.shape[0] // 8, 8, value.shape[1]), 0)


def norm_back(grad_out, normed, inv_std, gain, sums, slot):
    sums[slot, 0] += fold(grad_out * normed)
    sums[slot, 1] += fold(grad_out)
    grad_normed = grad_out * gain
    return inv_std * (
        grad_normed
        - jnp.mean(grad_normed, -1, keepdims=True)
        - normed * jnp.mean(grad_normed * normed, -1, keepdims=True)
    )


def gelu_both(preact):
    size = jnp.abs(preact)
    bell = jnp.exp(-0.5 * preact * preact)
    t = 1.0 / (1.0 + (0.3275911 * math.sqrt(0.5)) * size)
    series = t * (
        0.5 * 0.254829592
        + t * (-0.5 * 0.284496736 + t * (0.5 * 1.421413741 + t * (-0.5 * 1.453152027 + t * (0.5 * 1.061405429))))
    )
    tail = series * bell
    below = jnp.where(preact >= 0.0, 1.0 - tail, tail)
    return preact * below, below + preact * bell * (1.0 / math.sqrt(2.0 * math.pi))


def head_lanes(width, head_dim):
    lane = lax.broadcasted_iota(jnp.int32, (1, width), 1)
    first = jnp.where(lane < head_dim, 1.0, 0.0)
    return first, 1.0 - first


def lanes(value, low, high):
    return jnp.concatenate([value * low, value * high], 0)


def weights_of(scores):
    grown = [jnp.exp(s - jnp.max(s, 0, keepdims=True)) for s in scores]
    return [(e * (1.0 / jnp.sum(e, 0, keepdims=True))).astype(BF) for e in grown]


def scores_back(weights_b, grad_w):
    weights = [w.astype(F32) for w in weights_b]
    return [(w * (g - jnp.sum(g * w, 0, keepdims=True))).astype(BF) for w, g in zip(weights, grad_w)]


def self_attend(qkv, mask, probs, att, groups, first_group, span, head_dim):
    width = 2 * head_dim
    model = att.shape[1]
    pairs = model // width
    low, high = head_lanes(width, head_dim)
    scale = 1.0 / math.sqrt(head_dim)
    low_b, high_b = (low * scale).astype(BF), (high * scale).astype(BF)
    at = [p * width for p in range(pairs)]

    @pl.loop(0, groups)
    def _(g):
        rows = pl.ds(pl.multiple_of(g * span, span), span)
        bias = mask[first_group + g]
        both = [lanes(qkv[rows, c : c + width], low_b, high_b) for c in at]
        scores = [nt(qkv[rows, model + c : model + c + width], b) + bias for c, b in zip(at, both)]
        weights = weights_of(scores)
        for p, c in enumerate(at):
            probs[g * pairs + p] = weights[p]
            out = tn(weights[p], qkv[rows, 2 * model + c : 2 * model + c + width])
            att[rows, c : c + width] = (out[:span] * low + out[span:] * high).astype(BF)


def self_attend_back(qkv, probs, grad_att, grad_qkv, groups, span, head_dim):
    width = 2 * head_dim
    model = grad_att.shape[1]
    pairs = model // width
    low, high = head_lanes(width, head_dim)
    scale = 1.0 / math.sqrt(head_dim)
    low_s, high_s = low * scale, high * scale
    scaled, plain = (low_s.astype(BF), high_s.astype(BF)), (low.astype(BF), high.astype(BF))
    at = [p * width for p in range(pairs)]

    @pl.loop(0, groups)
    def _(g):
        rows = pl.ds(pl.multiple_of(g * span, span), span)
        both_g = [lanes(grad_att[rows, c : c + width], *plain) for c in at]
        weights = [probs[g * pairs + p] for p in range(pairs)]
        grad_w = [nt(qkv[rows, 2 * model + c : 2 * model + c + width], b) for c, b in zip(at, both_g)]
        grad_s = scores_back(weights, grad_w)
        for p, c in enumerate(at):
            out = tn(grad_s[p], qkv[rows, model + c : model + c + width])
            both_q = lanes(qkv[rows, c : c + width], *scaled)
            grad_qkv[rows, c : c + width] = (out[:span] * low_s + out[span:] * high_s).astype(BF)
            grad_qkv[rows, model + c : model + c + width] = nn(grad_s[p], both_q).astype(BF)
            grad_qkv[rows, 2 * model + c : 2 * model + c + width] = nn(weights[p], both_g[p]).astype(BF)


def cross_attend(queries, keys, vals, image, first_row, probs, out, row_count, length, patches, head_dim):
    width = 2 * head_dim
    pairs = queries.shape[1] // width
    low, high = head_lanes(width, head_dim)
    scale = 1.0 / math.sqrt(head_dim)
    low_s, high_s = low * scale, high * scale
    shown = lax.broadcasted_iota(jnp.int32, (keys.shape[1], 2 * length), 0) < patches
    at = [slice(p * width, p * width + width) for p in range(pairs)]

    @pl.loop(0, row_count)
    def _(r):
        rows = pl.ds(pl.multiple_of(r * length, 8), length)
        picked = image[first_row + r]
        both = [lanes(queries[rows, c], low_s, high_s).astype(BF) for c in at]
        scores = [jnp.where(shown, nt(keys[picked, :, c], b), MASKED) for c, b in zip(at, both)]
        weights = weights_of(scores)
        for p, c in enumerate(at):
            probs[r * pairs + p] = weights[p]
            got = tn(weights[p], vals[picked, :, c])
            out[rows, c] = got[:length] * low + got[length:] * high


def cross_attend_back(
    queries, keys, vals, image, first_row, probs, grad_att, grad_q, grad_k, grad_v, row_count, length, head_dim
):
    width = 2 * head_dim
    pairs = queries.shape[1] // width
    low, high = head_lanes(width, head_dim)
    scale = 1.0 / math.sqrt(head_dim)
    low_s, high_s = low * scale, high * scale
    at = [slice(p * width, p * width + width) for p in range(pairs)]

    @pl.loop(0, row_count)
    def _(r):
        rows = pl.ds(pl.multiple_of(r * length, 8), length)
        picked = image[first_row + r]
        both_g = [lanes(grad_att[rows, c], low, high).astype(BF) for c in at]
        weights = [probs[r * pairs + p] for p in range(pairs)]
        grad_w = [nt(vals[picked, :, c], b) for c, b in zip(at, both_g)]
        grad_s = scores_back(weights, grad_w)
        for p, c in enumerate(at):
            both_q = lanes(queries[rows, c], low_s, high_s).astype(BF)
            got = tn(grad_s[p], keys[picked, :, c])
            grad_q[rows, c] = got[:length] * low_s + got[length:] * high_s
            grad_k[picked, :, c] = nn(grad_s[p], both_q).astype(BF)
            grad_v[picked, :, c] = nn(weights[p], both_g[p]).astype(BF)


def grow(entry, w_up, preact, hidden, slope):
    tile = preact.shape[1]
    for j in range(hidden.shape[1] // tile):
        cols = slice(j * tile, j * tile + tile)
        preact[...] = nn(entry[...], w_up[:, cols])

        def body(rows):
            value, rise = gelu_both(preact[rows, :])
            hidden[rows, cols] = value.astype(BF)
            slope[rows, cols] = rise.astype(BF)

        by_rows(preact.shape[0], body)


def shrink(branch, w_down, slope, grad_pre):
    tile = branch.shape[1]
    for j in range(slope.shape[1] // tile):
        cols = slice(j * tile, j * tile + tile)
        grad_pre[:, cols] = (nt(branch[...], w_down[cols, :]) * slope[:, cols].astype(F32)).astype(BF)


def text_forward_kernel(half, span, flag, gains, biases, mask, text, wqkv, wo, w1, w2, *refs):
    (lay, zb, hidden, att), refs = refs[4:8] if half else refs[:4], refs[8:] if half else refs[4:]
    (bnd, y1, y3, qkv, probs, slope), refs = refs[:6], refs[6:]
    (x_s, wqkv_s, wo_s, w1_s, w2_s, qkv_s, probs_s, att_s, y1_s, mid_s, zb_s, pre_s, hid_s, slo_s, y3_s, out_s, sems) = refs
    count = x_s.shape[0]
    own = pl.ds(half * count, count)

    @pl.when(flag[0] == 0)
    def _():
        cp = Copies(sems)
        gets = [cp.load(text.at[own], x_s)] + [
            cp.load(a, b) for a, b in ((wqkv, wqkv_s), (wo, wo_s), (w1, w1_s), (w2, w2_s))
        ]
        gets[0].wait()
        gets[1].wait()
        qkv_s[...] = nn(x_s[...], wqkv_s[...]).astype(BF)
        cp.store(qkv_s, qkv)
        groups = count // span
        self_attend(qkv_s, mask, probs_s, att_s, groups, half * groups, span, x_s.shape[1] // HEADS)
        cp.store(probs_s, probs)
        cp.store(att_s, att.at[own])
        gets[2].wait()
        y1_s[...] = x_s[...].astype(F32) + nn(att_s[...], wo_s[...])
        cp.store(y1_s, y1)

        def first(rows):
            value = standard(y1_s[rows, :])[0] * gains[0:1, :] + biases[0:1, :]
            mid_s[rows, :] = value
            zb_s[rows, :] = value.astype(BF)

        by_rows(count, first)
        cp.store(zb_s, zb.at[own])
        gets[3].wait()
        grow(zb_s, w1_s, pre_s, hid_s, slo_s)
        cp.store(hid_s, hidden.at[own])
        cp.store(slo_s, slope)
        gets[4].wait()
        y3_s[...] = mid_s[...] + nn(hid_s[...], w2_s[...])
        cp.store(y3_s, y3)

        def second(rows):
            out_s[rows, :] = (standard(y3_s[rows, :])[0] * gains[1:2, :] + biases[1:2, :]).astype(BF)

        by_rows(count, second)
        cp.store(out_s, bnd)
        cp.store(out_s, lay.at[own])
        cp.finish()


def text_ffn_back_kernel(half, flag, gains, grad, y3, slope, w1, w2, *refs):
    (df, du, sums), refs = refs[3:6], refs[6:]
    dmid, refs = refs[0], refs[1:]
    (g_s, y3_s, slo_s, w1_s, w2_s, dy_s, df_s, du_s, dm_s, sum_s, sems) = refs
    count = g_s.shape[0]
    own = pl.ds(half * count, count)

    @pl.when(flag[0] == 0)
    def _():
        cp = Copies(sems)
        gets = [
            cp.load(a, b) for a, b in ((grad, g_s), (y3, y3_s), (w2, w2_s), (slope, slo_s), (w1, w1_s))
        ]
        sum_s[...] = jnp.zeros_like(sum_s)
        gets[0].wait()
        gets[1].wait()

        def body(rows):
            normed, inv_std = standard(y3_s[rows, :])
            value = norm_back(g_s[rows, :].astype(F32), normed, inv_std, gains[1:2, :], sum_s, 0)
            dy_s[rows, :] = value
            df_s[rows, :] = value.astype(BF)

        by_rows(count, body)
        cp.store(df_s, df.at[own])
        cp.store(sum_s, sums.at[half, pl.ds(1, 1)])
        gets[2].wait()
        gets[3].wait()
        shrink(df_s, w2_s, slo_s, du_s)
        cp.store(du_s, du.at[own])
        gets[4].wait()
        dm_s[...] = dy_s[...] + nt(du_s[...], w1_s[...])
        cp.store(dm_s, dmid)
        cp.finish()


def text_self_back_kernel(half, span, flag, gains, dmid, y1, qkv, probs, wo, wqkv, *refs):
    (da, dqkv, ig, sums), refs = refs[4:8], refs[8:]
    (dm_s, y1_s, qkv_s, probs_s, wo_s, wqkv_s, dy_s, da_s, datt_s, dqkv_s, ig_s, sum_s, sems) = refs
    count = dm_s.shape[0]
    own = pl.ds(half * count, count)

    @pl.when(flag[0] == 0)
    def _():
        cp = Copies(sems)
        gets = [
            cp.load(a, b)
            for a, b in ((dmid, dm_s), (y1, y1_s), (wo, wo_s), (qkv, qkv_s), (probs, probs_s), (wqkv, wqkv_s))
        ]
        sum_s[...] = jnp.zeros_like(sum_s)
        gets[0].wait()
        gets[1].wait()

        def body(rows):
            normed, inv_std = standard(y1_s[rows, :])
            value = norm_back(dm_s[rows, :], normed, inv_std, gains[0:1, :], sum_s, 0)
            dy_s[rows, :] = value
            da_s[rows, :] = value.astype(BF)

        by_rows(count, body)
        cp.store(da_s, da.at[own])
        cp.store(sum_s, sums.at[half, pl.ds(0, 1)])
        gets[2].wait()
        datt_s[...] = nt(da_s[...], wo_s[...]).astype(BF)
        gets[3].wait()
        gets[4].wait()
        self_attend_back(qkv_s, probs_s, datt_s, dqkv_s, count // span, span, dm_s.shape[1] // HEADS)
        cp.store(dqkv_s, dqkv.at[own])
        gets[5].wait()
        ig_s[...] = dy_s[...] + nt(dqkv_s[...], wqkv_s[...])
        cp.store(ig_s, ig.at[own])
        cp.finish()


JOIN_BUFS = 16


def joining_kernel(half, span, length, patches, flag, image, gains, biases, cgain, cbias, mask, bnd, cot,
                   wqkv, wo, w1, w2, wq, wc, keys, vals, *refs):
    refs = refs[JOIN_BUFS:] if half else refs[4:]
    (lay, zb, hidden, att, ig, df, du, da, dqkv, sums, midb, dq, catt, dca, dkey, dval), refs = refs[:16], refs[16:]
    back, refs = refs[0], refs[1:]
    (x_s, wqkv_s, wo_s, w1_s, w2_s, wq_s, wc_s, key_s, val_s, cot_s, qkv_s, probs_s, att_s, y1_s, mid_s, midb_s,
     qc_s, cprobs_s, cat_s, catb_s, y2_s, zb_s, pre_s, hid_s, slo_s, y3_s, lay_s, df_s, dy_s, du_s, dz_s, dca_s,
     dkey_s, dval_s, dqb_s, da_s, datt_s, dqkv_s, sum_s, sems) = refs
    count, model = x_s.shape
    head_dim = model // HEADS
    own = pl.ds(half * count, count)
    row_count = count // length
    groups = count // span
    pictures = pl.ds(half * row_count, row_count)

    @pl.when(flag[0] == 1)
    def _():
        cp = Copies(sems)
        (g_x, g_qkv, g_o, g_q, g_key, g_val, g_c, g_1, g_2, g_cot) = [
            cp.load(a, b)
            for a, b in (
                (bnd, x_s), (wqkv, wqkv_s), (wo, wo_s), (wq, wq_s), (keys.at[pictures], key_s),
                (vals.at[pictures], val_s), (wc, wc_s), (w1, w1_s), (w2, w2_s), (cot.at[own], cot_s),
            )
        ]
        sum_s[...] = jnp.zeros_like(sum_s)
        g_x.wait()
        g_qkv.wait()
        qkv_s[...] = nn(x_s[...], wqkv_s[...]).astype(BF)
        self_attend(qkv_s, mask, probs_s, att_s, groups, half * groups, span, head_dim)
        cp.store(att_s, att.at[own])
        g_o.wait()
        y1_s[...] = x_s[...].astype(F32) + nn(att_s[...], wo_s[...])

        def first(rows):
            value = standard(y1_s[rows, :])[0] * gains[0:1, :] + biases[0:1, :]
            mid_s[rows, :] = value
            midb_s[rows, :] = value.astype(BF)

        by_rows(count, first)
        cp.store(midb_s, midb.at[own])
        g_q.wait()
        qc_s[...] = nn(midb_s[...], wq_s[...]).astype(BF).astype(F32)
        g_key.wait()
        g_val.wait()
        cross_attend(qc_s, key_s, val_s, image, half * row_count, cprobs_s, cat_s, row_count, length, patches, head_dim)
        catb_s[...] = cat_s[...].astype(BF)
        cp.store(catb_s, catt.at[own])
        g_c.wait()
        y2_s[...] = mid_s[...] + nn(catb_s[...], wc_s[...])

        def second(rows):
            value = standard(y2_s[rows, :])[0] * cgain[...] + cbias[...]
            mid_s[rows, :] = value
            zb_s[rows, :] = value.astype(BF)

        by_rows(count, second)
        cp.store(zb_s, zb.at[own])
        g_1.wait()
        grow(zb_s, w1_s, pre_s, hid_s, slo_s)
        cp.store(hid_s, hidden.at[own])
        g_2.wait()
        y3_s[...] = mid_s[...] + nn(hid_s[...], w2_s[...])
        g_cot.wait()

        def third(rows):
            normed, inv_std = standard(y3_s[rows, :])
            lay_s[rows, :] = (normed * gains[1:2, :] + biases[1:2, :]).astype(BF)
            value = norm_back(cot_s[rows, :].astype(F32), normed, inv_std, gains[1:2, :], sum_s, 1)
            dy_s[rows, :] = value
            df_s[rows, :] = value.astype(BF)

        by_rows(count, third)
        cp.store(lay_s, lay.at[own])
        cp.store(df_s, df.at[own])
        shrink(df_s, w2_s, slo_s, du_s)
        cp.store(du_s, du.at[own])
        dz_s[...] = dy_s[...] + nt(du_s[...], w1_s[...])

        def fourth(rows):
            normed, inv_std = standard(y2_s[rows, :])
            value = norm_back(dz_s[rows, :], normed, inv_std, cgain[...], sum_s, 2)
            dy_s[rows, :] = value
            dca_s[rows, :] = value.astype(BF)

        by_rows(count, fourth)
        cp.store(dca_s, dca.at[own])
        cat_s[...] = nt(dca_s[...], wc_s[...]).astype(BF).astype(F32)
        cross_attend_back(qc_s, key_s, val_s, image, half * row_count, cprobs_s, cat_s, pre_s, dkey_s, dval_s,
                          row_count, length, head_dim)
        cp.store(dkey_s, dkey.at[pictures])
        cp.store(dval_s, dval.at[pictures])
        dqb_s[...] = pre_s[...].astype(BF)
        cp.store(dqb_s, dq.at[own])
        dz_s[...] = dy_s[...] + nt(dqb_s[...], wq_s[...])

        def fifth(rows):
            normed, inv_std = standard(y1_s[rows, :])
            value = norm_back(dz_s[rows, :], normed, inv_std, gains[0:1, :], sum_s, 0)
            dy_s[rows, :] = value
            da_s[rows, :] = value.astype(BF)

        by_rows(count, fifth)
        cp.store(da_s, da.at[own])
        cp.store(sum_s, sums.at[half])
        datt_s[...] = nt(da_s[...], wo_s[...]).astype(BF)
        self_attend_back(qkv_s, probs_s, datt_s, dqkv_s, groups, span, head_dim)
        cp.store(dqkv_s, dqkv.at[own])
        dz_s[...] = dy_s[...] + nt(dqkv_s[...], wqkv_s[...])
        x_s[...] = dz_s[...].astype(BF)
        cp.store(x_s, back)
        cp.store(dz_s, ig.at[own])
        cp.finish()


def project_kernel(flag, image, weight, out, packed):
    @pl.when(flag[0] == 1)
    def _():
        each, patches = image.shape[0], image.shape[1]
        packed[...] = jnp.zeros_like(packed)
        for i in range(each):
            packed[i * PAD : i * PAD + patches, :] = image[i]
        got = nn(packed[...], weight[...]).astype(BF)
        for i in range(each):
            out[i] = got[i * PAD : i * PAD + PAD]


def image_back_kernel(flag, image, dkey, dval, wk, wv, own, other, dwk, dwv, packed, sum_k, sum_v):
    step = pl.program_id(0)

    @pl.when(flag[0] == 1)
    def _():
        each, patches, width = image.shape

        @pl.when(step == 0)
        def _():
            packed[...] = jnp.zeros_like(packed)
            sum_k[...] = jnp.zeros_like(sum_k)
            sum_v[...] = jnp.zeros_like(sum_v)

        for i in range(each):
            packed[i * PAD : i * PAD + patches, :] = image[i]
        grad_k = dkey[...].reshape(each * PAD, dkey.shape[2])
        grad_v = dval[...].reshape(each * PAD, dval.shape[2])
        sum_k[...] += tn(packed[...], grad_k)
        sum_v[...] += tn(packed[...], grad_v)
        part = width // 2
        got = nt(grad_k, wk[part:, :]) + nt(grad_v, wv[part:, :])
        for i in range(each):
            own[i] = got[i * PAD : i * PAD + patches]
        got = (nt(grad_k, wk[:part, :]) + nt(grad_v, wv[:part, :])).astype(BF)
        for i in range(each):
            other[i] = got[i * PAD : i * PAD + patches]

        @pl.when(step == pl.num_programs(0) - 1)
        def _():
            dwk[...] = sum_k[...].astype(BF)
            dwv[...] = sum_v[...].astype(BF)


def weight_grad_kernel(left, right, out):
    out[...] = tn(left[...], right[...]).astype(BF)


def weight_grad(left, right, by_left, tile=768):
    tokens, rows = left.shape
    cols = right.shape[1]
    if by_left:
        grid, specs = (rows // tile,), (lambda i: (0, i), lambda i: (0, 0), lambda i: (i, 0))
        shapes = ((tokens, tile), (tokens, cols), (tile, cols))
    else:
        grid, specs = (cols // tile,), (lambda i: (0, 0), lambda i: (0, i), lambda i: (0, i))
        shapes = ((tokens, rows), (tokens, tile), (rows, tile))
    return pl.pallas_call(
        weight_grad_kernel,
        grid=grid,
        in_specs=[pl.BlockSpec(shapes[0], specs[0]), pl.BlockSpec(shapes[1], specs[1])],
        out_specs=pl.BlockSpec(shapes[2], specs[2]),
        out_shape=jax.ShapeDtypeStruct((rows, cols), BF),
        compiler_params=pltpu.CompilerParams(vmem_limit_bytes=LIMIT),
        cost_estimate=pl.CostEstimate(
            flops=2 * tokens * rows * cols, bytes_accessed=2 * (tokens * (rows + cols) + rows * cols), transcendentals=0
        ),
        name="weight_grad",
    )(left, right)


TILE = 256
DEEP = 192


class Job:
    def __init__(self, fill, rows, cols, outs):
        self.fill, self.rows, self.cols, self.outs = fill, rows, cols, outs
        self.depth = rows * (cols // TILE)


def reduce_kernel(model, *refs):
    (hidden, df, zb, du, att, da, entry, dqkv, dq, midb, dca, catt, gwk, gwv, small), refs = refs[:15], refs[15:]
    (down, up, qkv, out, norms, wide_k, wide_v, cross_q, cross_o), refs = refs[:9], refs[9:]
    (hidden_s, df_s, zb_s, du_s, att_s, da_s, entry_s, dqkv_s, dq_s, midb_s, dca_s, catt_s, gwk_s, gwv_s, small_s,
     tile, core_in, y_in, z_in, final, load_sems, store_sems, send_sems, recv_sems) = refs
    section, place = lax.axis_index("section"), lax.axis_index("dp")
    core, y, z = place % 2, place // 2 % 2, place // 4
    beside = place + 1 - 2 * core
    across = place + 2 - 4 * y
    along = [place + 4 * (1 - 2 * (z % 2)), place + 4 * (2 - 4 * (z // 2)), place + 4 * (3 - 2 * z)]
    far = [z + 1 - 2 * (z % 2), z + 2 - 4 * (z // 2), 3 - z]
    barrier = pltpu.get_barrier_semaphore()
    for other in [beside, across] + along:
        pl.semaphore_signal(barrier, inc=1, device_id=(section, other), device_id_type=pl.DeviceIdType.MESH)

    def send(number, kind, source, target, other):
        copy = pltpu.make_async_remote_copy(
            src_ref=source, dst_ref=target, send_sem=send_sems.at[number, kind], recv_sem=recv_sems.at[number, kind],
            device_id=(section, other), device_id_type=pl.DeviceIdType.MESH,
        )
        copy.start()
        return copy

    def loads(pairs, first):
        waits = {}
        for i, (source, target) in enumerate(pairs):
            copy = pltpu.make_async_copy(source, target, load_sems.at[first + i])
            copy.start()
            waits[id(target)] = copy
        return waits

    def product(left, right, cols, rows, spare=None):
        def fill(slot, need):
            need(left)
            need(right)
            got = tn(left[...], right[:, cols]).astype(BF)
            count = (cols.stop - cols.start) // TILE
            each = rows + (0 if spare is None else spare.shape[1])
            for k in range(count):
                piece = got[:, k * TILE : k * TILE + TILE].reshape(4, 2, 2, rows, TILE)
                tile[slot, :, :, :, k * each : k * each + rows, :] = piece
            if spare is not None:
                need(spare)
                for k in range(count):
                    extra = spare[:, :, k * TILE : k * TILE + TILE].reshape(4, 2, 2, each - rows, TILE)
                    tile[slot, :, :, :, k * each + rows : k * each + each, :] = extra

        return fill

    def shuffled(left, right, rows):
        def fill(slot, need):
            need(left)
            need(right)
            size = left.shape[1]
            old = lax.broadcasted_iota(jnp.int32, (size, size), 0)
            new = lax.broadcasted_iota(jnp.int32, (size, size), 1)
            own = rows // 2
            source = new % rows // own * (size // 2) + new // rows * own + new % own
            order = jnp.where(old == source, 1.0, 0.0).astype(BF)
            got = tn(nn(left[...], order).astype(BF), right[...]).astype(BF)
            for k in range(size // TILE):
                piece = got[:, k * TILE : k * TILE + TILE].reshape(4, 2, 2, rows, TILE)
                tile[slot, :, :, :, k * rows : k * rows + rows, :] = piece

        return fill

    def copied(source, rows):
        def fill(slot, need):
            need(source)
            for k in range(source.shape[1] // TILE):
                piece = source[:, k * TILE : k * TILE + TILE].reshape(4, 2, 2, rows, TILE)
                tile[slot, :, :, :, k * rows : k * rows + rows, :] = piece

        return fill

    def run(jobs, waits):
        waited = set()

        def need(ref):
            if id(ref) not in waited:
                waited.add(id(ref))
                waits[id(ref)].wait()

        stores, cores, ys, zs = [], {}, {}, {}
        total = len(jobs)
        for i in range(total + 4):
            if i < total:
                if i >= 3:
                    cores[i - 3].wait_send()
                slot, deep = i % 3, pl.ds(0, jobs[i].depth)
                jobs[i].fill(slot, need)
                if i == 0:
                    pl.semaphore_wait(barrier, 5)
                cores[i] = send(i, 0, tile.at[slot, :, :, 1 - core, deep], core_in.at[i, :, :, deep], beside)
            j = i - 1
            if 0 <= j < total:
                cores[j].wait_recv()
                deep = pl.ds(0, jobs[j].depth)

                @pl.loop(0, 4)
                def _(a):
                    for b in range(2):
                        core_in[j, a, b, deep, :] = core_in[j, a, b, deep, :] + tile[j % 3, a, b, core, deep, :]

                ys[j] = send(j, 1, core_in.at[j, :, 1 - y, deep], y_in.at[j, :, deep], across)
            j = i - 3
            if 0 <= j < total:
                ys[j].wait_recv()
                deep = pl.ds(0, jobs[j].depth)

                @pl.loop(0, 4)
                def _(a):
                    y_in[j, a, deep, :] = y_in[j, a, deep, :] + core_in[j, a, y, deep, :]

                for step in range(3):
                    zs[j, step] = send(
                        j, 2 + step, y_in.at[j, far[step], deep], z_in.at[j, step, deep], along[step]
                    )
            j = i - 4
            if 0 <= j < total:
                for step in range(3):
                    zs[j, step].wait_recv()
                deep = pl.ds(0, jobs[j].depth)
                final[j, deep, :] = (
                    y_in[j, z, deep, :].astype(F32) + z_in[j, 0, deep, :].astype(F32)
                ) + (z_in[j, 1, deep, :].astype(F32) + z_in[j, 2, deep, :].astype(F32))
                each = jobs[j].rows
                for k in range(jobs[j].cols // TILE):
                    row = k * each
                    for target, first, rows in jobs[j].outs:
                        copy = pltpu.make_async_copy(
                            final.at[j, pl.ds(row, rows)], target.at[:, pl.ds(first + k * TILE, TILE)],
                            store_sems.at[len(stores)],
                        )
                        copy.start()
                        stores.append(copy)
                        row += rows
        for i in range(total):
            if i >= total - 3:
                cores[i].wait_send()
            ys[i].wait_send()
            for step in range(3):
                zs[i, step].wait_send()
        for copy in stores:
            copy.wait()

    part = model // 16
    high = hidden.shape[1] // 16
    shared = [(hidden, hidden_s), (df, df_s), (zb, zb_s), (du, du_s), (att, att_s), (da, da_s), (small, small_s),
              (entry, entry_s), (dqkv, dqkv_s)]
    jobs = []
    for at in range(0, model, TILE):
        jobs.append(Job(product(hidden_s, df_s, slice(at, at + TILE), high), high, TILE, [(down, at, high)]))
    wide = DEEP // part * TILE
    for at in range(0, hidden.shape[1], wide):
        jobs.append(Job(product(zb_s, du_s, slice(at, at + wide), part), part, wide, [(up, at, part)]))
    for at in range(0, 3 * model, model):
        jobs.append(Job(product(entry_s, dqkv_s, slice(at, at + model), part), part, model, [(qkv, at, part)]))
    tail = Job(product(att_s, da_s, slice(0, model), part, small_s), part + small.shape[1], model,
               [(out, 0, part), (norms, 0, small.shape[1])])
    jobs.append(tail)
    tall = gwk.shape[0] // 16
    joint = [
        Job(shuffled(dq_s, midb_s, part), part, model, [(cross_q, 0, part)]),
        Job(shuffled(dca_s, catt_s, part), part, model, [(cross_o, 0, part)]),
        Job(copied(gwk_s, tall), tall, model, [(wide_k, 0, tall)]),
        Job(copied(gwv_s, tall), tall, model, [(wide_v, 0, tall)]),
    ]

    @pl.when(section == 0)
    def _():
        run(jobs, loads(shared, 0))

    @pl.when(section == 1)
    def _():
        waits = loads([(dq, dq_s), (midb, midb_s), (dca, dca_s), (catt, catt_s), (gwk, gwk_s), (gwv, gwv_s)] + shared, 0)
        run(joint + jobs, waits)


def reduce_all(acts, small, dp):
    hidden, df, zb, du, att, da, entry, dqkv, dq, midb, dca, catt, gwk, gwv = acts
    model, part, tall = df.shape[1], df.shape[1] // dp, gwk.shape[0] // dp
    high = hidden.shape[1] // dp
    jobs = 14
    shapes = [(high, model), (part, hidden.shape[1]), (part, 3 * model), (part, model), (small.shape[1], model),
              (tall, model), (tall, model), (part, model), (part, model)]
    vm = pltpu.VMEM
    return pl.pallas_call(
        functools.partial(reduce_kernel, model),
        in_specs=[ANY] * 15,
        out_specs=[ANY] * 9,
        out_shape=[jax.ShapeDtypeStruct(shape, F32) for shape in shapes],
        scratch_shapes=[vm(a.shape, BF) for a in list(acts) + [small]] + [
            vm((3, 4, 2, 2, DEEP, TILE), BF), vm((jobs, 4, 2, DEEP, TILE), BF), vm((jobs, 4, DEEP, TILE), BF),
            vm((jobs, 3, DEEP, TILE), BF), vm((jobs, DEEP, TILE), F32),
            pltpu.SemaphoreType.DMA((15,)), pltpu.SemaphoreType.DMA((48,)),
            pltpu.SemaphoreType.DMA((jobs, 5)), pltpu.SemaphoreType.DMA((jobs, 5)),
        ],
        compiler_params=pltpu.CompilerParams(vmem_limit_bytes=LIMIT, collective_id=1, has_side_effects=True),
        cost_estimate=pl.CostEstimate(flops=20_000_000_000, bytes_accessed=40_000_000, transcendentals=0),
        name="reduce_all",
    )(*acts, small)


def stage(kernel, name, smem, vmem, hbm, bufs, fresh, scratch, flops):
    arrays = [b for b in bufs if not isinstance(b, jax.ShapeDtypeStruct)]
    first = len(smem) + len(vmem) + len(hbm)
    aliases, at = {}, first
    for i, b in enumerate(bufs):
        if not isinstance(b, jax.ShapeDtypeStruct):
            aliases[at] = i
            at += 1
    outs = [jax.ShapeDtypeStruct(b.shape, b.dtype) for b in list(bufs) + list(fresh)]
    got = pl.pallas_call(
        kernel,
        in_specs=[SMEM] * len(smem) + [VMEM] * len(vmem) + [ANY] * (len(hbm) + len(arrays)),
        out_specs=[ANY] * len(outs),
        out_shape=outs,
        scratch_shapes=list(scratch) + [pltpu.SemaphoreType.DMA((40,))],
        input_output_aliases=aliases,
        compiler_params=pltpu.CompilerParams(vmem_limit_bytes=LIMIT),
        cost_estimate=pl.CostEstimate(flops=flops, bytes_accessed=sum(a.size * 2 for a in hbm), transcendentals=0),
        name=name,
    )(*smem, *vmem, *hbm, *arrays)
    return list(got[: len(bufs)]), list(got[len(bufs) :])


def reduce_plain(acts, small, dp):
    hidden, df, zb, du, att, da, entry, dqkv, dq, midb, dca, catt, gwk, gwv = acts
    model = df.shape[1]

    def total(value):
        return lax.psum_scatter(value, "dp", scatter_dimension=0, tiled=True).astype(F32)

    def by_owner(value):
        own = value.reshape(2, dp, model // (2 * dp), model)
        return jnp.swapaxes(own, 0, 1).reshape(model, model)

    return (
        total(weight_grad(hidden, df, True)), total(weight_grad(zb, du, False)), total(weight_grad(entry, dqkv, False)),
        total(weight_grad(att, da, True)), total(small)[0], total(gwk), total(gwv),
        total(by_owner(weight_grad(dq, midb, True))), total(by_owner(weight_grad(dca, catt, True))),
    )


def per_device(
    text_in, cotangent, images, segment_ids, row_image, self_qkv, self_out, ffn_up, ffn_down,
    norm_gain, norm_bias, image_kv, cross_query, cross_out, cross_gain, cross_bias,
):
    tokens, model = text_in.shape
    row_total, length = segment_ids.shape
    patches, width = images.shape[1:]
    hidden_width = ffn_up.shape[2]
    block_rows = row_image.shape[1]
    head_dim = model // HEADS
    pairs = HEADS // 2
    count = tokens // HALVES
    half_rows = row_total // HALVES
    span = 2 * length
    dp = lax.axis_size("dp")
    section = lax.axis_index("section")
    is_text = section == 0
    flag = section.astype(jnp.int32).reshape(1)
    place = lax.axis_index("dp")
    wqkv, wo, w1, w2 = self_qkv[0], self_out[0], ffn_up[0], ffn_down[0]
    gains, biases = norm_gain[0], norm_bias[0]
    cgain, cbias = cross_gain.reshape(1, model), cross_bias.reshape(1, model)

    marks = (segment_ids + segment_ids.shape[1] * (jnp.arange(row_total, dtype=jnp.int32) % 2)[:, None]).reshape(-1, span)
    mask = jnp.where(marks[:, :, None] == jnp.tile(marks, (1, 2))[:, None, :], 0.0, MASKED).astype(F32)
    in_block = jnp.arange(row_total, dtype=jnp.int32) // block_rows * block_rows % half_rows
    image = row_image.reshape(-1) + in_block

    def shape(*dims, dtype=BF):
        return jax.ShapeDtypeStruct(dims, dtype)

    core = place % 2
    half_w = width // 2
    sent_w = lax.dynamic_slice_in_dim(image_kv, core * half_w, half_w, 0)
    sent_w = lax.ppermute(sent_w, "section", [(0, 1)])
    swapped = lax.ppermute(sent_w, "dp", [(i, i ^ 1) for i in range(dp)])
    key_w = jnp.where(core == 0, jnp.concatenate([sent_w, swapped], 0), jnp.concatenate([swapped, sent_w], 0))

    each = 4
    grid = row_total // each

    def project(weight):
        return pl.pallas_call(
            project_kernel,
            grid_spec=pltpu.PrefetchScalarGridSpec(
                num_scalar_prefetch=1,
                grid=(grid,),
                in_specs=[
                    pl.BlockSpec((each, patches, width), lambda i, f: (i * f[0], 0, 0)),
                    pl.BlockSpec((width, model), lambda i, f: (0, 0)),
                ],
                out_specs=pl.BlockSpec((each, PAD, model), lambda i, f: (i * f[0], 0, 0)),
                scratch_shapes=[pltpu.VMEM((each * PAD, width), BF)],
            ),
            out_shape=shape(row_total, PAD, model),
            compiler_params=pltpu.CompilerParams(vmem_limit_bytes=LIMIT),
            cost_estimate=pl.CostEstimate(
                flops=2 * row_total * PAD * width * model, bytes_accessed=12_000_000, transcendentals=0
            ),
            name="project",
        )(flag, images, weight)

    vm = pltpu.VMEM
    probs_shape = (count // span * pairs, span, 2 * span)
    text_scratch = [
        vm((count, model), BF), vm(wqkv.shape, BF), vm(wo.shape, BF), vm(w1.shape, BF), vm(w2.shape, BF),
        vm((count, 3 * model), BF), vm(probs_shape, BF), vm((count, model), BF), vm((count, model), F32),
        vm((count, model), F32), vm((count, model), BF), vm((count, model), F32), vm((count, hidden_width), BF),
        vm((count, hidden_width), BF), vm((count, model), F32), vm((count, model), BF),
    ]
    shared = [shape(tokens, model), shape(tokens, model), shape(tokens, hidden_width), shape(tokens, model)]
    linear = model * 3 * model + model * model + 2 * model * hidden_width
    kept, outward = [], []
    for half in range(HALVES):
        shared, fresh = stage(
            functools.partial(text_forward_kernel, half, span), "text_forward", [flag], [gains, biases, mask],
            [text_in, wqkv, wo, w1, w2], shared,
            [
                shape(count, model), shape(count, model, dtype=F32), shape(count, model, dtype=F32),
                shape(count, 3 * model), shape(*probs_shape), shape(count, hidden_width),
            ],
            text_scratch, 2 * count * linear,
        )
        outward.append(lax.ppermute(fresh[0], "section", [(0, 1)]))
        kept.append(fresh[1:])
    values = project(image_kv)
    keys = project(key_w)

    join_scratch = [
        vm((count, model), BF), vm(wqkv.shape, BF), vm(wo.shape, BF), vm(w1.shape, BF), vm(w2.shape, BF),
        vm(cross_query.shape, BF), vm(cross_out.shape, BF), vm((half_rows, PAD, model), BF),
        vm((half_rows, PAD, model), BF), vm((count, model), BF), vm((count, 3 * model), BF), vm(probs_shape, BF),
        vm((count, model), BF), vm((count, model), F32), vm((count, model), F32), vm((count, model), BF),
        vm((count, model), F32), vm((half_rows * pairs, PAD, 2 * length), BF), vm((count, model), F32),
        vm((count, model), BF), vm((count, model), F32), vm((count, model), BF), vm((count, model), F32),
        vm((count, hidden_width), BF), vm((count, hidden_width), BF), vm((count, model), F32), vm((count, model), BF),
        vm((count, model), BF), vm((count, model), F32), vm((count, hidden_width), BF), vm((count, model), F32),
        vm((count, model), BF), vm((half_rows, PAD, model), BF), vm((half_rows, PAD, model), BF),
        vm((count, model), BF), vm((count, model), BF), vm((count, model), BF), vm((count, 3 * model), BF),
        vm((3, 2, 8, model), F32),
    ]
    bufs = shared + [
        shape(tokens, model, dtype=F32), shape(tokens, model), shape(tokens, hidden_width), shape(tokens, model),
        shape(tokens, 3 * model), shape(HALVES, 3, 2, 8, model, dtype=F32), shape(tokens, model), shape(tokens, model),
        shape(tokens, model), shape(tokens, model), shape(row_total, PAD, model), shape(row_total, PAD, model),
    ]
    returned = []
    for half in range(HALVES):
        bufs, fresh = stage(
            functools.partial(joining_kernel, half, span, length, patches), "joining", [flag, image],
            [gains, biases, cgain, cbias, mask],
            [outward[half], cotangent, wqkv, wo, w1, w2, cross_query, cross_out, keys, values],
            bufs, [shape(count, model)], join_scratch, 4 * count * (linear + 2 * model * model),
        )
        returned.append(lax.ppermute(fresh[0], "section", [(1, 0)]))
    lay, zb, hidden, att, ig, df, du, da, dqkv, sums, midb, dq, catt, dca, dkey, dval = bufs

    own_part, other_part, grad_wk, grad_wv = pl.pallas_call(
        image_back_kernel,
        grid_spec=pltpu.PrefetchScalarGridSpec(
            num_scalar_prefetch=1,
            grid=(grid,),
            in_specs=[
                pl.BlockSpec((each, patches, width), lambda i, f: (i * f[0], 0, 0)),
                pl.BlockSpec((each, PAD, model), lambda i, f: (i * f[0], 0, 0)),
                pl.BlockSpec((each, PAD, model), lambda i, f: (i * f[0], 0, 0)),
                pl.BlockSpec((width, model), lambda i, f: (0, 0)),
                pl.BlockSpec((width, model), lambda i, f: (0, 0)),
            ],
            out_specs=[
                pl.BlockSpec((each, patches, width // 2), lambda i, f: (i * f[0], 0, 0)),
                pl.BlockSpec((each, patches, width // 2), lambda i, f: (i * f[0], 0, 0)),
                pl.BlockSpec((width, model), lambda i, f: (0, 0)),
                pl.BlockSpec((width, model), lambda i, f: (0, 0)),
            ],
            scratch_shapes=[vm((each * PAD, width), BF), vm((width, model), F32), vm((width, model), F32)],
        ),
        out_shape=[
            shape(row_total, patches, width // 2, dtype=F32), shape(row_total, patches, width // 2),
            shape(width, model), shape(width, model),
        ],
        compiler_params=pltpu.CompilerParams(vmem_limit_bytes=LIMIT),
        cost_estimate=pl.CostEstimate(
            flops=8 * row_total * PAD * width * model, bytes_accessed=25_000_000, transcendentals=0
        ),
        name="image_back",
    )(flag, images, dkey, dval, key_w, image_kv)
    image_part = lax.ppermute(other_part, "section", [(1, 0)])

    sections = lax.axis_size("section")
    cross_rows = model // (sections * dp)
    image_rows, out_rows = width // dp, model // dp

    dmids = []
    for half in range(HALVES):
        y1, y3, qkv, probs, slope = kept[half]
        (df, du, sums), fresh = stage(
            functools.partial(text_ffn_back_kernel, half), "text_ffn_back", [flag], [gains],
            [returned[half], y3, slope, w1, w2], [df, du, sums], [shape(count, model, dtype=F32)],
            [
                vm((count, model), BF), vm((count, model), F32), vm((count, hidden_width), BF), vm(w1.shape, BF),
                vm(w2.shape, BF), vm((count, model), F32), vm((count, model), BF), vm((count, hidden_width), BF),
                vm((count, model), F32), vm((1, 2, 8, model), F32),
            ],
            4 * count * model * hidden_width,
        )
        dmids.append(fresh[0])
    for half in range(HALVES):
        y1, y3, qkv, probs, slope = kept[half]
        (da, dqkv, ig, sums), _ = stage(
            functools.partial(text_self_back_kernel, half, span), "text_self_back", [flag], [gains],
            [dmids[half], y1, qkv, probs, wo, wqkv], [da, dqkv, ig, sums], [],
            [
                vm((count, model), F32), vm((count, model), F32), vm((count, 3 * model), BF), vm(probs_shape, BF),
                vm(wo.shape, BF), vm(wqkv.shape, BF), vm((count, model), F32), vm((count, model), BF),
                vm((count, model), BF), vm((count, 3 * model), BF), vm((count, model), F32), vm((1, 2, 8, model), F32),
            ],
            2 * count * 4 * model * model,
        )
    entry = jnp.where(is_text, text_in, jnp.concatenate(outward, 0))

    totals = jnp.sum(sums, (0, 3))
    own_norm = totals[:2].reshape(4, dp, model // dp)
    own_cross = jnp.where(is_text, 0.0, totals[2]).reshape(2, sections, dp, cross_rows)
    small = jnp.concatenate(
        [jnp.moveaxis(own_norm, 1, 0).reshape(dp, -1), jnp.moveaxis(own_cross, 2, 0).reshape(dp, -1)], 1
    )
    small = jnp.pad(small[:, None, :], ((0, 0), (0, 15), (0, model - small.shape[1]))).astype(BF)
    acts = (hidden, df, zb, du, att, da, entry, dqkv, dq, midb, dca, catt, grad_wk, grad_wv)
    got = reduce_all(acts, small, dp) if dp == 16 else reduce_plain(acts, small, dp)
    down, up, qkv_grad, out_grad, small, wide_k, wide_v, cross_q, cross_o = got
    small = small[0]
    norm_part = small[: 4 * out_rows].reshape(2, 2, out_rows)
    cross_part = small[4 * out_rows : 4 * out_rows + 2 * sections * cross_rows].reshape(2, sections, cross_rows)

    extra = jnp.pad(cross_part[:, 0].reshape(1, -1), ((0, 15), (0, model - 2 * cross_rows)))
    parcel = jnp.concatenate([wide_k, cross_q[:cross_rows], cross_o[:cross_rows], extra], 0).astype(BF)
    parcel = lax.ppermute(parcel, "section", [(1, 0)]).astype(F32)
    at = image_rows + 2 * cross_rows
    pick = functools.partial(jnp.where, is_text)
    grad_kv = pick(parcel[:image_rows], wide_v)
    grad_cross_q = pick(parcel[image_rows : image_rows + cross_rows], cross_q[cross_rows:]).T
    grad_cross_o = pick(parcel[image_rows + cross_rows : at], cross_o[cross_rows:]).T
    grad_cross_g = pick(parcel[at, :cross_rows], cross_part[0, 1])
    grad_cross_b = pick(parcel[at, cross_rows : 2 * cross_rows], cross_part[1, 1])
    image_grad = pick(image_part.astype(F32), own_part)
    return (
        lay[None], ig[None], image_grad, qkv_grad[None], out_grad[None], up[None], down[None],
        norm_part[:, 0][None], norm_part[:, 1][None], grad_kv, grad_cross_q, grad_cross_o, grad_cross_g, grad_cross_b,
    )


def solution(mesh):
    return jax.shard_map(
        per_device,
        mesh=mesh,
        in_specs=(
            P("dp", None),
            P("dp", None),
            P("dp", None, None),
            P("dp", None),
            P("dp", None),
            P("section", None, None),
            P("section", None, None),
            P("section", None, None),
            P("section", None, None),
            P("section", None, None),
            P("section", None, None),
            P(None, "section"),
            P(),
            P(),
            P(),
            P(),
        ),
        out_specs=(
            P("section", "dp", None),
            P("section", "dp", None),
            P("dp", None, "section"),
            P("section", "dp", None),
            P("section", "dp", None),
            P("section", "dp", None),
            P("section", "dp", None),
            P("section", None, "dp"),
            P("section", None, "dp"),
            P("dp", "section"),
            P(None, ("section", "dp")),
            P(None, ("section", "dp")),
            P(("section", "dp")),
            P(("section", "dp")),
        ),
        check_vma=False,
    )
```

```python
import functools
import math

import jax
import jax.numpy as jnp
from jax import lax
from jax.experimental import pallas as pl
from jax.experimental.pallas import tpu as pltpu
from jax.sharding import PartitionSpec as P

HEADS = 12
EPSILON = 1e-06
MASKED = -1e30
BF = jnp.bfloat16
F32 = jnp.float32
PAD = 160
LANES = 128
HALVES = 2
CHUNK = 32
LIMIT = 60 * 1024 * 1024
ANY = pl.BlockSpec(memory_space=pl.ANY)
SMEM = pl.BlockSpec(memory_space=pltpu.SMEM)
VMEM = pl.BlockSpec(memory_space=pltpu.VMEM)


def nn(left, right):
    return lax.dot_general(left, right, (((1,), (0,)), ((), ())), preferred_element_type=F32)


def nt(left, right):
    return lax.dot_general(left, right, (((1,), (1,)), ((), ())), preferred_element_type=F32)


def tn(left, right):
    return lax.dot_general(left, right, (((0,), (0,)), ((), ())), preferred_element_type=F32)


class Copy:
    def __init__(self, source, target, sems, number):
        self.parts = source, target, sems, number

    def make(self):
        source, target, sems, number = self.parts
        return pltpu.make_async_copy(source, target, sems.at[number])

    def wait(self):
        self.make().wait()


class Copies:
    def __init__(self, sems):
        self.sems, self.used, self.open = sems, 0, []

    def load(self, source, target):
        copy = Copy(source, target, self.sems, self.used)
        self.used += 1
        copy.make().start()
        return copy

    def store(self, source, target):
        copy = self.load(source, target)
        self.open.append(copy)
        return copy

    def settle(self, copy):
        self.open = [other for other in self.open if other is not copy]
        copy.wait()

    def finish(self):
        for copy in self.open:
            copy.wait()
        self.open = []


def by_rows(count, body):
    for at in range(0, count, CHUNK):
        body(pl.ds(at, CHUNK))


def standard(summed):
    centred = summed - jnp.mean(summed, -1, keepdims=True)
    inv_std = lax.rsqrt(jnp.mean(centred * centred, -1, keepdims=True) + EPSILON)
    return centred * inv_std, inv_std


def fold(value):
    return jnp.sum(value.reshape(value.shape[0] // 8, 8, value.shape[1]), 0)


def norm_back(grad_out, normed, inv_std, gain, sums, slot):
    sums[slot, 0] += fold(grad_out * normed)
    sums[slot, 1] += fold(grad_out)
    grad_normed = grad_out * gain
    return inv_std * (
        grad_normed
        - jnp.mean(grad_normed, -1, keepdims=True)
        - normed * jnp.mean(grad_normed * normed, -1, keepdims=True)
    )


def gelu_both(preact):
    size = jnp.abs(preact)
    bell = jnp.exp(-0.5 * preact * preact)
    t = 1.0 / (1.0 + (0.3275911 * math.sqrt(0.5)) * size)
    series = t * (
        0.5 * 0.254829592
        + t * (-0.5 * 0.284496736 + t * (0.5 * 1.421413741 + t * (-0.5 * 1.453152027 + t * (0.5 * 1.061405429))))
    )
    tail = series * bell
    below = jnp.where(preact >= 0.0, 1.0 - tail, tail)
    return preact * below, below + preact * bell * (1.0 / math.sqrt(2.0 * math.pi))


def head_lanes(width, head_dim):
    lane = lax.broadcasted_iota(jnp.int32, (1, width), 1)
    first = jnp.where(lane < head_dim, 1.0, 0.0)
    return first, 1.0 - first


def lanes(value, low, high):
    return jnp.concatenate([value * low, value * high], 0)


def weights_of(scores):
    grown = [jnp.exp(s - jnp.max(s, 0, keepdims=True)) for s in scores]
    return [(e * (1.0 / jnp.sum(e, 0, keepdims=True))).astype(BF) for e in grown]


def scores_back(weights_b, grad_w):
    weights = [w.astype(F32) for w in weights_b]
    return [(w * (g - jnp.sum(g * w, 0, keepdims=True))).astype(BF) for w, g in zip(weights, grad_w)]


def self_attend(qkv, mask, probs, att, groups, first_group, span, head_dim):
    width = 2 * head_dim
    model = att.shape[1]
    pairs = model // width
    low, high = head_lanes(width, head_dim)
    scale = 1.0 / math.sqrt(head_dim)
    low_b, high_b = (low * scale).astype(BF), (high * scale).astype(BF)
    at = [p * width for p in range(pairs)]

    @pl.loop(0, groups)
    def _(g):
        rows = pl.ds(pl.multiple_of(g * span, span), span)
        bias = mask[first_group + g]
        both = [lanes(qkv[rows, c : c + width], low_b, high_b) for c in at]
        scores = [nt(qkv[rows, model + c : model + c + width], b) + bias for c, b in zip(at, both)]
        weights = weights_of(scores)
        for p, c in enumerate(at):
            probs[g * pairs + p] = weights[p]
            out = tn(weights[p], qkv[rows, 2 * model + c : 2 * model + c + width])
            att[rows, c : c + width] = (out[:span] * low + out[span:] * high).astype(BF)


def self_attend_back(qkv, probs, grad_att, grad_qkv, groups, span, head_dim):
    width = 2 * head_dim
    model = grad_att.shape[1]
    pairs = model // width
    low, high = head_lanes(width, head_dim)
    scale = 1.0 / math.sqrt(head_dim)
    low_s, high_s = low * scale, high * scale
    scaled, plain = (low_s.astype(BF), high_s.astype(BF)), (low.astype(BF), high.astype(BF))
    at = [p * width for p in range(pairs)]

    @pl.loop(0, groups)
    def _(g):
        rows = pl.ds(pl.multiple_of(g * span, span), span)
        both_g = [lanes(grad_att[rows, c : c + width], *plain) for c in at]
        weights = [probs[g * pairs + p] for p in range(pairs)]
        grad_w = [nt(qkv[rows, 2 * model + c : 2 * model + c + width], b) for c, b in zip(at, both_g)]
        grad_s = scores_back(weights, grad_w)
        for p, c in enumerate(at):
            out = tn(grad_s[p], qkv[rows, model + c : model + c + width])
            both_q = lanes(qkv[rows, c : c + width], *scaled)
            grad_qkv[rows, c : c + width] = (out[:span] * low_s + out[span:] * high_s).astype(BF)
            grad_qkv[rows, model + c : model + c + width] = nn(grad_s[p], both_q).astype(BF)
            grad_qkv[rows, 2 * model + c : 2 * model + c + width] = nn(weights[p], both_g[p]).astype(BF)


def cross_attend(queries, keys, vals, image, first_row, probs, out, row_count, length, patches, head_dim):
    width = 2 * head_dim
    pairs = queries.shape[1] // width
    low, high = head_lanes(width, head_dim)
    scale = 1.0 / math.sqrt(head_dim)
    low_s, high_s = low * scale, high * scale
    shown = lax.broadcasted_iota(jnp.int32, (keys.shape[1], 2 * length), 0) < patches
    at = [slice(p * width, p * width + width) for p in range(pairs)]

    @pl.loop(0, row_count)
    def _(r):
        rows = pl.ds(pl.multiple_of(r * length, 8), length)
        picked = image[first_row + r]
        both = [lanes(queries[rows, c], low_s, high_s).astype(BF) for c in at]
        scores = [jnp.where(shown, nt(keys[picked, :, c], b), MASKED) for c, b in zip(at, both)]
        weights = weights_of(scores)
        for p, c in enumerate(at):
            probs[r * pairs + p] = weights[p]
            got = tn(weights[p], vals[picked, :, c])
            out[rows, c] = got[:length] * low + got[length:] * high


def cross_attend_back(
    queries, keys, vals, image, first_row, probs, grad_att, grad_q, grad_k, grad_v, row_count, length, head_dim
):
    width = 2 * head_dim
    pairs = queries.shape[1] // width
    low, high = head_lanes(width, head_dim)
    scale = 1.0 / math.sqrt(head_dim)
    low_s, high_s = low * scale, high * scale
    at = [slice(p * width, p * width + width) for p in range(pairs)]

    @pl.loop(0, row_count)
    def _(r):
        rows = pl.ds(pl.multiple_of(r * length, 8), length)
        picked = image[first_row + r]
        both_g = [lanes(grad_att[rows, c], low, high).astype(BF) for c in at]
        weights = [probs[r * pairs + p] for p in range(pairs)]
        grad_w = [nt(vals[picked, :, c], b) for c, b in zip(at, both_g)]
        grad_s = scores_back(weights, grad_w)
        for p, c in enumerate(at):
            both_q = lanes(queries[rows, c], low_s, high_s).astype(BF)
            got = tn(grad_s[p], keys[picked, :, c])
            grad_q[rows, c] = got[:length] * low_s + got[length:] * high_s
            grad_k[r, :, c] = nn(grad_s[p], both_q).astype(BF)
            grad_v[r, :, c] = nn(weights[p], both_g[p]).astype(BF)


def grow(entry, w_up, preact, hidden, slope):
    tile = preact.shape[1]
    for j in range(hidden.shape[1] // tile):
        cols = slice(j * tile, j * tile + tile)
        preact[...] = nn(entry[...], w_up[:, cols])

        def body(rows):
            value, rise = gelu_both(preact[rows, :])
            hidden[rows, cols] = value.astype(BF)
            slope[rows, cols] = rise.astype(BF)

        by_rows(preact.shape[0], body)


def shrink(branch, w_down, slope, grad_pre):
    tile = branch.shape[1]
    for j in range(slope.shape[1] // tile):
        cols = slice(j * tile, j * tile + tile)
        grad_pre[:, cols] = (nt(branch[...], w_down[cols, :]) * slope[:, cols].astype(F32)).astype(BF)


class Refs:
    def __init__(self, names, refs):
        for name, ref in zip(names, refs):
            setattr(self, name, ref)


def remote(r, number, source, target, device):
    copy = pltpu.make_async_remote_copy(
        src_ref=source, dst_ref=target, send_sem=r.send_sems.at[number], recv_sem=r.recv_sems.at[number],
        device_id=device, device_id_type=pl.DeviceIdType.MESH,
    )
    copy.start()
    return copy


def greet(device):
    pl.semaphore_signal(
        pltpu.get_barrier_semaphore(), inc=1, device_id=device, device_id_type=pl.DeviceIdType.MESH
    )


def greeted(count):
    pl.semaphore_wait(pltpu.get_barrier_semaphore(), count)


def text_forward(r, cp, half, span, out, send):
    count = r.x_s.shape[0]
    own = pl.ds(half * count, count)
    groups = count // span
    text = cp.load(r.text.at[own], r.x_s)
    gets = weights_in(r, cp) if half == 0 else None
    text.wait()
    cp.store(r.x_s, r.entry.at[own])
    if half == 0:
        gets[0].wait()
    r.qkv_s[...] = nn(r.x_s[...], r.wqkv_s[...]).astype(BF)
    cp.store(r.qkv_s, r.qkv.at[half])
    self_attend(r.qkv_s, r.mask, r.probs_s, r.att_s, groups, half * groups, span, r.x_s.shape[1] // HEADS)
    cp.store(r.probs_s, r.probs.at[half])
    cp.store(r.att_s, r.att.at[own])
    if half == 0:
        gets[1].wait()
    r.y1_s[...] = r.x_s[...].astype(F32) + nn(r.att_s[...], r.wo_s[...])
    cp.store(r.y1_s, r.y1.at[half])

    def first(rows):
        value = standard(r.y1_s[rows, :])[0] * r.gains[0:1, :] + r.biases[0:1, :]
        r.mid_s[rows, :] = value
        r.zb_s[rows, :] = value.astype(BF)

    by_rows(count, first)
    cp.store(r.zb_s, r.zb.at[own])
    if half == 0:
        gets[2].wait()
    grow(r.zb_s, r.w1_s, r.pre_s, r.hid_s, r.slo_s)
    cp.store(r.hid_s, r.hidden.at[own])
    cp.store(r.slo_s, r.slope.at[half])
    if half == 0:
        gets[3].wait()
    r.y3_s[...] = r.mid_s[...] + nn(r.hid_s[...], r.w2_s[...])
    cp.store(r.y3_s, r.y3.at[half])

    def second(rows):
        out[rows, :] = (standard(r.y3_s[rows, :])[0] * r.gains[1:2, :] + r.biases[1:2, :]).astype(BF)

    by_rows(count, second)
    sent = send()
    cp.store(out, r.lay.at[own])
    cp.finish()
    return sent


def weights_in(r, cp):
    return [cp.load(a, b) for a, b in ((r.wqkv, r.wqkv_s), (r.wo, r.wo_s), (r.w1, r.w1_s), (r.w2, r.w2_s))]


def text_back(r, cp, half, span, arrived):
    count, model = r.y1_s.shape
    own = pl.ds(half * count, count)
    groups = count // span
    kept = [
        cp.load(a.at[half], b)
        for a, b in ((r.y3, r.y3_s), (r.slope, r.slo_s), (r.y1, r.y1_s), (r.qkv, r.qkv_s), (r.probs, r.probs_s))
    ]
    r.sum_s[...] = jnp.zeros_like(r.sum_s)
    for copy in kept:
        copy.wait()
    arrived()

    def first(rows):
        normed, inv_std = standard(r.y3_s[rows, :])
        value = norm_back(r.bnd_s[half, rows, :].astype(F32), normed, inv_std, r.gains[1:2, :], r.sum_s, 1)
        r.dy_s[rows, :] = value
        r.df_s[rows, :] = value.astype(BF)

    by_rows(count, first)
    df = cp.store(r.df_s, r.df.at[own])
    shrink(r.df_s, r.w2_s, r.slo_s, r.hid_s)
    cp.store(r.hid_s, r.du.at[own])
    r.mid_s[...] = r.dy_s[...] + nt(r.hid_s[...], r.w1_s[...])
    cp.settle(df)

    def second(rows):
        normed, inv_std = standard(r.y1_s[rows, :])
        value = norm_back(r.mid_s[rows, :], normed, inv_std, r.gains[0:1, :], r.sum_s, 0)
        r.dy_s[rows, :] = value
        r.df_s[rows, :] = value.astype(BF)

    by_rows(count, second)
    cp.store(r.df_s, r.da.at[own])
    cp.store(r.sum_s, r.sums.at[half])
    r.att_s[...] = nt(r.df_s[...], r.wo_s[...]).astype(BF)
    self_attend_back(r.qkv_s, r.probs_s, r.att_s, r.dqkv_s, groups, span, model // HEADS)
    cp.store(r.dqkv_s, r.dqkv.at[own])
    r.pre_s[...] = r.dy_s[...] + nt(r.dqkv_s[...], r.wqkv_s[...])
    cp.store(r.pre_s, r.ig.at[own])
    cp.finish()


def join(r, cp, half, span, length, patches, gets, back, arrived, send):
    count, model = r.mid_s.shape
    head_dim = model // HEADS
    own = pl.ds(half * count, count)
    row_count = count // length
    groups = count // span
    pictures = pl.ds(half * row_count, row_count)
    g_cot = cp.load(r.cot.at[own], r.g_s)

    def ready(number):
        if half == 0:
            gets[number].wait()

    r.sum_s[...] = jnp.zeros_like(r.sum_s)
    ready(0)
    arrived()
    entry = r.bnd_s.at[half]
    cp.store(entry, r.entry.at[own])
    r.qkv_s[...] = nn(entry[...], r.wqkv_s[...]).astype(BF)
    self_attend(r.qkv_s, r.mask, r.probs_s, r.att_s, groups, half * groups, span, head_dim)
    att = cp.store(r.att_s, r.att.at[own])
    ready(1)
    r.y1_s[...] = entry[...].astype(F32) + nn(r.att_s[...], r.wo_s[...])

    def first(rows):
        value = standard(r.y1_s[rows, :])[0] * r.gains[0:1, :] + r.biases[0:1, :]
        r.mid_s[rows, :] = value
        r.midb_s[rows, :] = value.astype(BF)

    by_rows(count, first)
    cp.store(r.midb_s, r.midb.at[own])
    ready(4)
    r.qc_s[...] = nn(r.midb_s[...], r.wq_s[...]).astype(BF).astype(F32)
    cross_attend(r.qc_s, r.key_s, r.val_s, r.image, half * row_count, r.cprobs_s, r.cat_s, row_count, length, patches,
                 head_dim)
    r.catb_s[...] = r.cat_s[...].astype(BF)
    catt = cp.store(r.catb_s, r.catt.at[own])
    ready(5)
    r.y2_s[...] = r.mid_s[...] + nn(r.catb_s[...], r.wc_s[...])

    def second(rows):
        value = standard(r.y2_s[rows, :])[0] * r.cgain[...] + r.cbias[...]
        r.mid_s[rows, :] = value
        r.zb_s[rows, :] = value.astype(BF)

    by_rows(count, second)
    cp.store(r.zb_s, r.zb.at[own])
    ready(2)
    grow(r.zb_s, r.w1_s, r.pre_s, r.hid_s, r.slo_s)
    hidden = cp.store(r.hid_s, r.hidden.at[own])
    ready(3)
    r.y3_s[...] = r.mid_s[...] + nn(r.hid_s[...], r.w2_s[...])
    g_cot.wait()

    def third(rows):
        normed, inv_std = standard(r.y3_s[rows, :])
        r.lay_s[rows, :] = (normed * r.gains[1:2, :] + r.biases[1:2, :]).astype(BF)
        value = norm_back(r.g_s[rows, :].astype(F32), normed, inv_std, r.gains[1:2, :], r.sum_s, 1)
        r.dy_s[rows, :] = value
        r.df_s[rows, :] = value.astype(BF)

    by_rows(count, third)
    cp.store(r.lay_s, r.lay.at[own])
    df = cp.store(r.df_s, r.df.at[own])
    cp.settle(hidden)
    shrink(r.df_s, r.w2_s, r.slo_s, r.hid_s)
    du = cp.store(r.hid_s, r.du.at[own])
    r.mid_s[...] = r.dy_s[...] + nt(r.hid_s[...], r.w1_s[...])
    cp.settle(df)

    def fourth(rows):
        normed, inv_std = standard(r.y2_s[rows, :])
        value = norm_back(r.mid_s[rows, :], normed, inv_std, r.cgain[...], r.sum_s, 2)
        r.dy_s[rows, :] = value
        r.df_s[rows, :] = value.astype(BF)

    by_rows(count, fourth)
    dca = cp.store(r.df_s, r.dca.at[own])
    r.cat_s[...] = nt(r.df_s[...], r.wc_s[...]).astype(BF).astype(F32)
    cross_attend_back(r.qc_s, r.key_s, r.val_s, r.image, half * row_count, r.cprobs_s, r.cat_s, r.pre_s, r.dkey_s,
                      r.dval_s, row_count, length, head_dim)
    cp.store(r.dkey_s, r.dkey.at[pictures])
    cp.store(r.dval_s, r.dval.at[pictures])
    cp.settle(catt)
    r.catb_s[...] = r.pre_s[...].astype(BF)
    cp.store(r.catb_s, r.dq.at[own])
    r.mid_s[...] = r.dy_s[...] + nt(r.catb_s[...], r.wq_s[...])
    cp.settle(dca)

    def fifth(rows):
        normed, inv_std = standard(r.y1_s[rows, :])
        value = norm_back(r.mid_s[rows, :], normed, inv_std, r.gains[0:1, :], r.sum_s, 0)
        r.dy_s[rows, :] = value
        r.df_s[rows, :] = value.astype(BF)

    by_rows(count, fifth)
    cp.store(r.df_s, r.da.at[own])
    cp.store(r.sum_s, r.sums.at[half])
    cp.settle(att)
    r.att_s[...] = nt(r.df_s[...], r.wo_s[...]).astype(BF)
    self_attend_back(r.qkv_s, r.probs_s, r.att_s, r.dqkv_s, groups, span, head_dim)
    cp.store(r.dqkv_s, r.dqkv.at[own])
    r.mid_s[...] = r.dy_s[...] + nt(r.dqkv_s[...], r.wqkv_s[...])
    back[...] = r.mid_s[...].astype(BF)
    send()
    cp.store(r.mid_s, r.ig.at[own])
    cp.finish()


PIECES = 5


def project(r, cp, rows, patches, own, source, beside):
    total, width = r.pix_s.shape
    chunk = total // PIECES
    weight = cp.load(r.wimg, r.wimg_s)
    gets = [cp.load(r.images.at[pl.ds(c * chunk, chunk)], r.pix_s.at[pl.ds(c * chunk, chunk)]) for c in range(PIECES)]
    later = weights_in(r, cp) + [cp.load(r.wq, r.wq_s), cp.load(r.wc, r.wc_s)]

    def spread(source, target):
        target[:, patches - 1 : PAD, :] = jnp.zeros((rows, PAD - patches + 1, target.shape[2]), BF)
        for c in range(PIECES):
            if target is r.val_s:
                gets[c].wait()
            at = slice(c * chunk, c * chunk + chunk)
            got = nn(r.pix_s[at, :], source[...])
            for t in range(r.flat_s.shape[0]):
                r.flat_s[t, at, :] = got[:, t * LANES : t * LANES + LANES]
        for i in range(rows):
            for t in range(r.flat_s.shape[0]):
                target[i, :patches, t * LANES : t * LANES + LANES] = r.flat_s[
                    t, pl.ds(i, patches, stride=rows), :
                ].astype(BF)

    weight.wait()
    spread(r.wimg_s, r.val_s)
    expect(r, 0, r.wk_s.at[own], r.wk_s.at[own], source).wait_recv()
    greeted(2)
    swap = remote(r, 1, r.wk_s.at[own], r.wk_s.at[own], beside)
    swap.wait_recv()
    spread(r.wk_s, r.key_s)
    swap.wait_send()
    return later


def image_back(r, cp):
    total, width = r.pix_s.shape
    rows = r.key_s.shape[0]
    patches = total // rows
    chunk = total // PIECES
    gets = [cp.load(a, b) for a, b in ((r.dkey, r.key_s), (r.dval, r.val_s), (r.images, r.pix_s))]
    for source, flat, get in ((r.key_s, r.fk_s, gets[0]), (r.val_s, r.fv_s, gets[1])):
        get.wait()
        for i in range(rows):
            picked = r.row_of[i]
            for t in range(r.flat_s.shape[0]):
                r.flat_s[t, pl.ds(i, patches, stride=rows), :] = source[
                    picked, :patches, t * LANES : t * LANES + LANES
                ].astype(F32)
        for t in range(r.flat_s.shape[0]):
            flat[:, t * LANES : t * LANES + LANES] = r.flat_s[t].astype(BF)
    part = width // 2
    stores = []
    for c in range(PIECES):
        at = slice(c * chunk, c * chunk + chunk)
        r.other_s[at, :] = (
            nt(r.fk_s[at, :], r.wk_s[:part, :]) + nt(r.fv_s[at, :], r.wimg_s[:part, :])
        ).astype(BF)
        if c > 1:
            cp.settle(stores[c - 2])
        r.own_s[c % 2] = nt(r.fk_s[at, :], r.wk_s[part:, :]) + nt(r.fv_s[at, :], r.wimg_s[part:, :])
        stores.append(cp.store(r.own_s.at[c % 2], r.image_own.at[pl.ds(c * chunk, chunk)]))
    cp.store(r.other_s, r.image_other)
    gets[2].wait()
    r.grad_s[0] = tn(r.pix_s[...], r.fk_s[...]).astype(BF)
    cp.store(r.grad_s.at[0], r.gwk)
    r.grad_s[1] = tn(r.pix_s[...], r.fv_s[...]).astype(BF)
    cp.store(r.grad_s.at[1], r.gwv)
    cp.finish()


def relay_kernel(halves, span, length, patches, names, scopes, *refs):
    r = Refs(names, refs)
    section, place = lax.axis_index("section"), lax.axis_index("dp")
    core = lax.rem(place, jnp.int32(2))
    partner, beside = (1 - section, place), (section, place + 1 - 2 * core)
    half = r.wimg.shape[0] // 2
    own = pl.ds(pl.multiple_of(core * half, half), half)
    layer, first, last = ({n: pltpu.VMEM(*v) for n, v in scope.items()} for scope in scopes)

    def within(scope, body):
        def call(**own):
            for name, ref in own.items():
                setattr(r, name, ref)
            body()

        pl.run_scoped(call, **scope)

    @pl.when(section == 0)
    def _():
        cp = Copies(r.sems)
        greet(partner)
        greeted(1)

        def body():
            sends = [remote(r, 0, r.wimg.at[own], r.wk_s.at[own], partner)]
            for h in range(halves):
                out = (r.lay_s, r.back_s)[h]
                sends.append(
                    text_forward(r, cp, h, span, out, lambda: remote(r, 2 + h, out, r.bnd_s.at[h], partner))
                )
            for h in range(halves):
                text_back(
                    r, cp, h, span, lambda: expect(r, 2 + h, r.back_s, r.bnd_s.at[h], partner).wait_recv()
                )
            for copy in sends:
                copy.wait_send()

        within(layer, body)

    @pl.when(section == 1)
    def _():
        cp = Copies(r.sems)
        greet(partner)
        greet(beside)
        got = []
        within(first, lambda: got.extend(project(r, cp, r.key_s.shape[0], patches, own, partner, beside)))

        def body():
            for h in range(halves):
                back = (r.back_s, r.x_s)[h]
                join(
                    r, cp, h, span, length, patches, got, back,
                    lambda: expect(r, 2 + h, r.lay_s, r.bnd_s.at[h], partner).wait_recv(),
                    lambda: remote(r, 2 + h, back, r.bnd_s.at[h], partner),
                )

        within(layer, body)
        within(last, lambda: image_back(r, cp))
        for h in range(halves):
            expect(r, 2 + h, (r.back_s, r.x_s)[h], r.bnd_s.at[h], partner).wait_send()


def expect(r, number, source, target, device):
    return pltpu.make_async_remote_copy(
        src_ref=source, dst_ref=target, send_sem=r.send_sems.at[number], recv_sem=r.recv_sems.at[number],
        device_id=device, device_id_type=pl.DeviceIdType.MESH,
    )


def relay(world, reads, writes, scratch, scopes, kernel, flops):
    smem, vmem, hbm = reads
    names = smem + vmem + hbm + list(writes) + list(scratch) + ["sems", "send_sems", "recv_sems"]
    got = pl.pallas_call(
        functools.partial(kernel, names, scopes),
        in_specs=[SMEM] * len(smem) + [VMEM] * len(vmem) + [ANY] * len(hbm),
        out_specs=[ANY] * len(writes),
        out_shape=list(writes.values()),
        scratch_shapes=[pltpu.VMEM(shape, dtype) for shape, dtype in scratch.values()]
        + [pltpu.SemaphoreType.DMA((100,)), pltpu.SemaphoreType.DMA((4,)), pltpu.SemaphoreType.DMA((4,))],
        compiler_params=pltpu.CompilerParams(vmem_limit_bytes=LIMIT, collective_id=2, has_side_effects=True),
        cost_estimate=pl.CostEstimate(flops=flops, bytes_accessed=40_000_000, transcendentals=0),
        name="relay",
    )(*[world[n] for n in smem + vmem + hbm])
    world.update(zip(writes, got))


def weight_grad_kernel(left, right, out):
    out[...] = tn(left[...], right[...]).astype(BF)


def weight_grad(left, right, by_left, tile=768):
    tokens, rows = left.shape
    cols = right.shape[1]
    if by_left:
        grid, specs = (rows // tile,), (lambda i: (0, i), lambda i: (0, 0), lambda i: (i, 0))
        shapes = ((tokens, tile), (tokens, cols), (tile, cols))
    else:
        grid, specs = (cols // tile,), (lambda i: (0, 0), lambda i: (0, i), lambda i: (0, i))
        shapes = ((tokens, rows), (tokens, tile), (rows, tile))
    return pl.pallas_call(
        weight_grad_kernel,
        grid=grid,
        in_specs=[pl.BlockSpec(shapes[0], specs[0]), pl.BlockSpec(shapes[1], specs[1])],
        out_specs=pl.BlockSpec(shapes[2], specs[2]),
        out_shape=jax.ShapeDtypeStruct((rows, cols), BF),
        compiler_params=pltpu.CompilerParams(vmem_limit_bytes=LIMIT),
        cost_estimate=pl.CostEstimate(
            flops=2 * tokens * rows * cols, bytes_accessed=2 * (tokens * (rows + cols) + rows * cols), transcendentals=0
        ),
        name="weight_grad",
    )(left, right)


TILE = 256
DEEP = 192


class Job:
    def __init__(self, fill, rows, cols, outs):
        self.fill, self.rows, self.cols, self.outs = fill, rows, cols, outs
        self.depth = rows * (cols // TILE)


def reduce_kernel(model, *refs):
    (hidden, df, zb, du, att, da, entry, dqkv, dq, midb, dca, catt, gwk, gwv, small), refs = refs[:15], refs[15:]
    (down, up, qkv, out, norms, wide_k, wide_v, cross_q, cross_o), refs = refs[:9], refs[9:]
    (hidden_s, df_s, zb_s, du_s, att_s, da_s, entry_s, dqkv_s, dq_s, midb_s, dca_s, catt_s, gwk_s, gwv_s, small_s,
     tile, core_in, y_in, z_in, final, load_sems, store_sems, send_sems, recv_sems) = refs
    section, place = lax.axis_index("section"), lax.axis_index("dp")
    core, y, z = place % 2, place // 2 % 2, place // 4
    beside = place + 1 - 2 * core
    across = place + 2 - 4 * y
    along = [place + 4 * (1 - 2 * (z % 2)), place + 4 * (2 - 4 * (z // 2)), place + 4 * (3 - 2 * z)]
    far = [z + 1 - 2 * (z % 2), z + 2 - 4 * (z // 2), 3 - z]
    barrier = pltpu.get_barrier_semaphore()
    for other in [beside, across] + along:
        pl.semaphore_signal(barrier, inc=1, device_id=(section, other), device_id_type=pl.DeviceIdType.MESH)

    def send(number, kind, source, target, other):
        copy = pltpu.make_async_remote_copy(
            src_ref=source, dst_ref=target, send_sem=send_sems.at[number, kind], recv_sem=recv_sems.at[number, kind],
            device_id=(section, other), device_id_type=pl.DeviceIdType.MESH,
        )
        copy.start()
        return copy

    def loads(pairs, first):
        waits = {}
        for i, (source, target) in enumerate(pairs):
            copy = pltpu.make_async_copy(source, target, load_sems.at[first + i])
            copy.start()
            waits[id(target)] = copy
        return waits

    def product(left, right, cols, rows, spare=None):
        def fill(slot, need):
            need(left)
            need(right)
            got = tn(left[...], right[:, cols]).astype(BF)
            count = (cols.stop - cols.start) // TILE
            each = rows + (0 if spare is None else spare.shape[1])
            for k in range(count):
                piece = got[:, k * TILE : k * TILE + TILE].reshape(4, 2, 2, rows, TILE)
                tile[slot, :, :, :, k * each : k * each + rows, :] = piece
            if spare is not None:
                need(spare)
                for k in range(count):
                    extra = spare[:, :, k * TILE : k * TILE + TILE].reshape(4, 2, 2, each - rows, TILE)
                    tile[slot, :, :, :, k * each + rows : k * each + each, :] = extra

        return fill

    def shuffled(left, right, rows):
        def fill(slot, need):
            need(left)
            need(right)
            size = left.shape[1]
            old = lax.broadcasted_iota(jnp.int32, (size, size), 0)
            new = lax.broadcasted_iota(jnp.int32, (size, size), 1)
            own = rows // 2
            source = new % rows // own * (size // 2) + new // rows * own + new % own
            order = jnp.where(old == source, 1.0, 0.0).astype(BF)
            got = tn(nn(left[...], order).astype(BF), right[...]).astype(BF)
            for k in range(size // TILE):
                piece = got[:, k * TILE : k * TILE + TILE].reshape(4, 2, 2, rows, TILE)
                tile[slot, :, :, :, k * rows : k * rows + rows, :] = piece

        return fill

    def copied(source, rows):
        def fill(slot, need):
            need(source)
            for k in range(source.shape[1] // TILE):
                piece = source[:, k * TILE : k * TILE + TILE].reshape(4, 2, 2, rows, TILE)
                tile[slot, :, :, :, k * rows : k * rows + rows, :] = piece

        return fill

    def run(jobs, waits):
        waited = set()

        def need(ref):
            if id(ref) not in waited:
                waited.add(id(ref))
                waits[id(ref)].wait()

        stores, cores, ys, zs = [], {}, {}, {}
        total = len(jobs)
        for i in range(total + 4):
            if i < total:
                if i >= 3:
                    cores[i - 3].wait_send()
                slot, deep = i % 3, pl.ds(0, jobs[i].depth)
                jobs[i].fill(slot, need)
                if i == 0:
                    pl.semaphore_wait(barrier, 5)
                cores[i] = send(i, 0, tile.at[slot, :, :, 1 - core, deep], core_in.at[i, :, :, deep], beside)
            j = i - 1
            if 0 <= j < total:
                cores[j].wait_recv()
                deep = pl.ds(0, jobs[j].depth)

                @pl.loop(0, 4)
                def _(a):
                    for b in range(2):
                        core_in[j, a, b, deep, :] = core_in[j, a, b, deep, :] + tile[j % 3, a, b, core, deep, :]

                ys[j] = send(j, 1, core_in.at[j, :, 1 - y, deep], y_in.at[j, :, deep], across)
            j = i - 3
            if 0 <= j < total:
                ys[j].wait_recv()
                deep = pl.ds(0, jobs[j].depth)

                @pl.loop(0, 4)
                def _(a):
                    y_in[j, a, deep, :] = y_in[j, a, deep, :] + core_in[j, a, y, deep, :]

                for step in range(3):
                    zs[j, step] = send(
                        j, 2 + step, y_in.at[j, far[step], deep], z_in.at[j, step, deep], along[step]
                    )
            j = i - 4
            if 0 <= j < total:
                for step in range(3):
                    zs[j, step].wait_recv()
                deep = pl.ds(0, jobs[j].depth)
                final[j, deep, :] = (
                    y_in[j, z, deep, :].astype(F32) + z_in[j, 0, deep, :].astype(F32)
                ) + (z_in[j, 1, deep, :].astype(F32) + z_in[j, 2, deep, :].astype(F32))
                each = jobs[j].rows
                for k in range(jobs[j].cols // TILE):
                    row = k * each
                    for target, first, rows in jobs[j].outs:
                        copy = pltpu.make_async_copy(
                            final.at[j, pl.ds(row, rows)], target.at[:, pl.ds(first + k * TILE, TILE)],
                            store_sems.at[len(stores)],
                        )
                        copy.start()
                        stores.append(copy)
                        row += rows
        for i in range(total):
            if i >= total - 3:
                cores[i].wait_send()
            ys[i].wait_send()
            for step in range(3):
                zs[i, step].wait_send()
        for copy in stores:
            copy.wait()

    part = model // 16
    high = hidden.shape[1] // 16
    shared = [(hidden, hidden_s), (df, df_s), (zb, zb_s), (du, du_s), (att, att_s), (da, da_s), (small, small_s),
              (entry, entry_s), (dqkv, dqkv_s)]
    jobs = []
    for at in range(0, model, TILE):
        jobs.append(Job(product(hidden_s, df_s, slice(at, at + TILE), high), high, TILE, [(down, at, high)]))
    wide = DEEP // part * TILE
    for at in range(0, hidden.shape[1], wide):
        jobs.append(Job(product(zb_s, du_s, slice(at, at + wide), part), part, wide, [(up, at, part)]))
    for at in range(0, 3 * model, model):
        jobs.append(Job(product(entry_s, dqkv_s, slice(at, at + model), part), part, model, [(qkv, at, part)]))
    tail = Job(product(att_s, da_s, slice(0, model), part, small_s), part + small.shape[1], model,
               [(out, 0, part), (norms, 0, small.shape[1])])
    jobs.append(tail)
    tall = gwk.shape[0] // 16
    joint = [
        Job(shuffled(dq_s, midb_s, part), part, model, [(cross_q, 0, part)]),
        Job(shuffled(dca_s, catt_s, part), part, model, [(cross_o, 0, part)]),
        Job(copied(gwk_s, tall), tall, model, [(wide_k, 0, tall)]),
        Job(copied(gwv_s, tall), tall, model, [(wide_v, 0, tall)]),
    ]

    @pl.when(section == 0)
    def _():
        run(jobs, loads(shared, 0))

    @pl.when(section == 1)
    def _():
        waits = loads([(dq, dq_s), (midb, midb_s), (dca, dca_s), (catt, catt_s), (gwk, gwk_s), (gwv, gwv_s)] + shared, 0)
        run(joint + jobs, waits)


def reduce_all(acts, small, dp):
    hidden, df, zb, du, att, da, entry, dqkv, dq, midb, dca, catt, gwk, gwv = acts
    model, part, tall = df.shape[1], df.shape[1] // dp, gwk.shape[0] // dp
    high = hidden.shape[1] // dp
    jobs = 14
    shapes = [(high, model), (part, hidden.shape[1]), (part, 3 * model), (part, model), (small.shape[1], model),
              (tall, model), (tall, model), (part, model), (part, model)]
    vm = pltpu.VMEM
    return pl.pallas_call(
        functools.partial(reduce_kernel, model),
        in_specs=[ANY] * 15,
        out_specs=[ANY] * 9,
        out_shape=[jax.ShapeDtypeStruct(shape, F32) for shape in shapes],
        scratch_shapes=[vm(a.shape, BF) for a in list(acts) + [small]] + [
            vm((3, 4, 2, 2, DEEP, TILE), BF), vm((jobs, 4, 2, DEEP, TILE), BF), vm((jobs, 4, DEEP, TILE), BF),
            vm((jobs, 3, DEEP, TILE), BF), vm((jobs, DEEP, TILE), F32),
            pltpu.SemaphoreType.DMA((15,)), pltpu.SemaphoreType.DMA((48,)),
            pltpu.SemaphoreType.DMA((jobs, 5)), pltpu.SemaphoreType.DMA((jobs, 5)),
        ],
        compiler_params=pltpu.CompilerParams(vmem_limit_bytes=LIMIT, collective_id=1, has_side_effects=True),
        cost_estimate=pl.CostEstimate(flops=20_000_000_000, bytes_accessed=40_000_000, transcendentals=0),
        name="reduce_all",
    )(*acts, small)


def reduce_plain(acts, small, dp):
    hidden, df, zb, du, att, da, entry, dqkv, dq, midb, dca, catt, gwk, gwv = acts
    model = df.shape[1]

    def total(value):
        return lax.psum_scatter(value, "dp", scatter_dimension=0, tiled=True).astype(F32)

    def by_owner(value):
        own = value.reshape(2, dp, model // (2 * dp), model)
        return jnp.swapaxes(own, 0, 1).reshape(model, model)

    return (
        total(weight_grad(hidden, df, True)), total(weight_grad(zb, du, False)), total(weight_grad(entry, dqkv, False)),
        total(weight_grad(att, da, True)), total(small)[0], total(gwk), total(gwv),
        total(by_owner(weight_grad(dq, midb, True))), total(by_owner(weight_grad(dca, catt, True))),
    )


def per_device(
    text_in, cotangent, images, segment_ids, row_image, self_qkv, self_out, ffn_up, ffn_down,
    norm_gain, norm_bias, image_kv, cross_query, cross_out, cross_gain, cross_bias,
):
    tokens, model = text_in.shape
    row_total, length = segment_ids.shape
    patches, width = images.shape[1:]
    hidden_width = ffn_up.shape[2]
    block_rows = row_image.shape[1]
    head_dim = model // HEADS
    pairs = HEADS // 2
    count = tokens // HALVES
    half_rows = row_total // HALVES
    span = 2 * length
    dp = lax.axis_size("dp")
    section = lax.axis_index("section")
    is_text = section == 0
    flag = section.astype(jnp.int32).reshape(1)
    place = lax.axis_index("dp")
    wqkv, wo, w1, w2 = self_qkv[0], self_out[0], ffn_up[0], ffn_down[0]
    gains, biases = norm_gain[0], norm_bias[0]
    cgain, cbias = cross_gain.reshape(1, model), cross_bias.reshape(1, model)

    marks = (segment_ids + segment_ids.shape[1] * (jnp.arange(row_total, dtype=jnp.int32) % 2)[:, None]).reshape(-1, span)
    mask = jnp.where(marks[:, :, None] == jnp.tile(marks, (1, 2))[:, None, :], 0.0, MASKED).astype(F32)
    in_block = jnp.arange(row_total, dtype=jnp.int32) // block_rows * block_rows
    image = row_image.reshape(-1) + in_block
    slots = jnp.arange(block_rows, dtype=jnp.int32)
    row_of = jnp.sum(jnp.where(row_image[:, :, None] == slots, slots[:, None], 0), 1).reshape(-1) + in_block

    def shape(*dims, dtype=BF):
        return jax.ShapeDtypeStruct(dims, dtype)

    flat_rows = row_total * patches
    pixels = jnp.swapaxes(images, 0, 1).reshape(flat_rows, width)
    probs_shape = (count // span * pairs, span, 2 * span)
    world = dict(
        image=image, row_of=row_of, gains=gains, biases=biases, cgain=cgain, cbias=cbias, mask=mask, text=text_in,
        cot=cotangent, images=pixels, wqkv=wqkv, wo=wo, w1=w1, w2=w2, wq=cross_query, wc=cross_out, wimg=image_kv,
    )
    small_f, small_b = ((count, model), F32), ((count, model), BF)
    tall_b, wide_b = ((count, hidden_width), BF), ((count, 3 * model), BF)
    picture_b, pictures_b = ((half_rows, PAD, model), BF), ((row_total, PAD, model), BF)
    scratch = dict(
        wqkv_s=(wqkv.shape, BF), wo_s=(wo.shape, BF), w1_s=(w1.shape, BF), w2_s=(w2.shape, BF),
        wq_s=(cross_query.shape, BF), wc_s=(cross_out.shape, BF), wimg_s=(image_kv.shape, BF),
        wk_s=(image_kv.shape, BF), key_s=pictures_b, val_s=pictures_b, bnd_s=((HALVES, count, model), BF),
        x_s=small_b, back_s=small_b,
    )
    layer_s = dict(
        qkv_s=wide_b, probs_s=(probs_shape, BF), att_s=small_b, y1_s=small_f, mid_s=small_f, zb_s=small_b,
        pre_s=small_f, hid_s=tall_b, slo_s=tall_b, y3_s=small_f, lay_s=small_b, g_s=small_b, midb_s=small_b,
        qc_s=small_f, cprobs_s=((half_rows * pairs, PAD, 2 * length), BF), cat_s=small_f, catb_s=small_b,
        y2_s=small_f, df_s=small_b, dy_s=small_f, dkey_s=picture_b, dval_s=picture_b, dqkv_s=wide_b,
        sum_s=((3, 2, 8, model), F32),
    )
    flat_s = ((model // LANES, flat_rows, LANES), F32)
    first_s = dict(pix_s=((flat_rows, width), BF), flat_s=flat_s)
    last_s = dict(
        pix_s=((flat_rows, width), BF), flat_s=flat_s, fk_s=((flat_rows, model), BF), fv_s=((flat_rows, model), BF),
        own_s=((2, flat_rows // PIECES, width // 2), F32), other_s=((flat_rows, width // 2), BF), grad_s=((2, width, model), BF),
    )
    tokens_b = shape(tokens, model)
    writes = dict(
        lay=tokens_b, zb=tokens_b, hidden=shape(tokens, hidden_width), att=tokens_b, entry=tokens_b,
        ig=shape(tokens, model, dtype=F32), df=tokens_b, du=shape(tokens, hidden_width), da=tokens_b,
        dqkv=shape(tokens, 3 * model), sums=shape(HALVES, 3, 2, 8, model, dtype=F32), midb=tokens_b, dq=tokens_b,
        catt=tokens_b, dca=tokens_b, dkey=shape(row_total, PAD, model), dval=shape(row_total, PAD, model),
        image_own=shape(flat_rows, width // 2, dtype=F32), image_other=shape(flat_rows, width // 2),
        gwk=shape(width, model), gwv=shape(width, model), y1=shape(HALVES, count, model, dtype=F32),
        y3=shape(HALVES, count, model, dtype=F32), qkv=shape(HALVES, count, 3 * model),
        probs=shape(HALVES, *probs_shape), slope=shape(HALVES, count, hidden_width),
    )
    linear = model * 3 * model + model * model + 2 * model * hidden_width
    reads = (
        ["image", "row_of"], ["gains", "biases", "mask", "cgain", "cbias"],
        ["text", "cot", "images", "wqkv", "wo", "w1", "w2", "wq", "wc", "wimg"],
    )
    relay(
        world, reads, writes, scratch, (layer_s, first_s, last_s),
        functools.partial(relay_kernel, HALVES, span, length, patches), 8 * count * (linear + 2 * model * model),
    )
    lay, zb, hidden, att, entry, ig, df, du, da, dqkv, sums, midb, dq, catt, dca = (
        world[n] for n in list(writes)[:15]
    )
    own_part, other_part, grad_wk, grad_wv = (world[n] for n in ("image_own", "image_other", "gwk", "gwv"))
    image_part = lax.ppermute(other_part, "section", [(1, 0)])

    sections = lax.axis_size("section")
    cross_rows = model // (sections * dp)
    image_rows, out_rows = width // dp, model // dp

    totals = jnp.sum(sums, (0, 3))
    own_norm = totals[:2].reshape(4, dp, model // dp)
    own_cross = jnp.where(is_text, 0.0, totals[2]).reshape(2, sections, dp, cross_rows)
    small = jnp.concatenate(
        [jnp.moveaxis(own_norm, 1, 0).reshape(dp, -1), jnp.moveaxis(own_cross, 2, 0).reshape(dp, -1)], 1
    )
    small = jnp.pad(small[:, None, :], ((0, 0), (0, 15), (0, model - small.shape[1]))).astype(BF)
    acts = (hidden, df, zb, du, att, da, entry, dqkv, dq, midb, dca, catt, grad_wk, grad_wv)
    got = reduce_all(acts, small, dp) if dp == 16 else reduce_plain(acts, small, dp)
    down, up, qkv_grad, out_grad, small, wide_k, wide_v, cross_q, cross_o = got
    small = small[0]
    norm_part = small[: 4 * out_rows].reshape(2, 2, out_rows)
    cross_part = small[4 * out_rows : 4 * out_rows + 2 * sections * cross_rows].reshape(2, sections, cross_rows)

    extra = jnp.pad(cross_part[:, 0].reshape(1, -1), ((0, 15), (0, model - 2 * cross_rows)))
    parcel = jnp.concatenate([wide_k, cross_q[:cross_rows], cross_o[:cross_rows], extra], 0).astype(BF)
    parcel = lax.ppermute(parcel, "section", [(1, 0)]).astype(F32)
    at = image_rows + 2 * cross_rows
    pick = functools.partial(jnp.where, is_text)
    grad_kv = pick(parcel[:image_rows], wide_v)
    grad_cross_q = pick(parcel[image_rows : image_rows + cross_rows], cross_q[cross_rows:]).T
    grad_cross_o = pick(parcel[image_rows + cross_rows : at], cross_o[cross_rows:]).T
    grad_cross_g = pick(parcel[at, :cross_rows], cross_part[0, 1])
    grad_cross_b = pick(parcel[at, cross_rows : 2 * cross_rows], cross_part[1, 1])
    image_grad = pick(image_part.astype(F32), own_part).reshape(patches, row_total, width // 2)
    image_grad = jnp.swapaxes(image_grad, 0, 1)
    return (
        lay[None], ig[None], image_grad, qkv_grad[None], out_grad[None], up[None], down[None],
        norm_part[:, 0][None], norm_part[:, 1][None], grad_kv, grad_cross_q, grad_cross_o, grad_cross_g, grad_cross_b,
    )


def solution(mesh):
    return jax.shard_map(
        per_device,
        mesh=mesh,
        in_specs=(
            P("dp", None),
            P("dp", None),
            P("dp", None, None),
            P("dp", None),
            P("dp", None),
            P("section", None, None),
            P("section", None, None),
            P("section", None, None),
            P("section", None, None),
            P("section", None, None),
            P("section", None, None),
            P(None, "section"),
            P(),
            P(),
            P(),
            P(),
        ),
        out_specs=(
            P("section", "dp", None),
            P("section", "dp", None),
            P("dp", None, "section"),
            P("section", "dp", None),
            P("section", "dp", None),
            P("section", "dp", None),
            P("section", "dp", None),
            P("section", None, "dp"),
            P("section", None, "dp"),
            P("dp", "section"),
            P(None, ("section", "dp")),
            P(None, ("section", "dp")),
            P(("section", "dp")),
            P(("section", "dp")),
        ),
        check_vma=False,
    )
```

```python
import functools
import math

import jax
import jax.numpy as jnp
from jax import lax
from jax.experimental import pallas as pl
from jax.experimental.pallas import tpu as pltpu
from jax.sharding import PartitionSpec as P

HEADS = 12
EPSILON = 1e-06
MASKED = -1e30
BF = jnp.bfloat16
F32 = jnp.float32
PAD = 160
LANES = 128
HALVES = 2
CHUNK = 32
LIMIT = 60 * 1024 * 1024
ANY = pl.BlockSpec(memory_space=pl.ANY)
SMEM = pl.BlockSpec(memory_space=pltpu.SMEM)
VMEM = pl.BlockSpec(memory_space=pltpu.VMEM)


def nn(left, right):
    return lax.dot_general(left, right, (((1,), (0,)), ((), ())), preferred_element_type=F32)


def nt(left, right):
    return lax.dot_general(left, right, (((1,), (1,)), ((), ())), preferred_element_type=F32)


def tn(left, right):
    return lax.dot_general(left, right, (((0,), (0,)), ((), ())), preferred_element_type=F32)


class Copy:
    def __init__(self, source, target, sems, number):
        self.parts = source, target, sems, number

    def make(self):
        source, target, sems, number = self.parts
        return pltpu.make_async_copy(source, target, sems.at[number])

    def wait(self):
        self.make().wait()


class Copies:
    def __init__(self, sems):
        self.sems, self.used, self.open = sems, 0, []

    def load(self, source, target):
        copy = Copy(source, target, self.sems, self.used)
        self.used += 1
        copy.make().start()
        return copy

    def store(self, source, target):
        copy = self.load(source, target)
        self.open.append(copy)
        return copy

    def settle(self, copy):
        self.open = [other for other in self.open if other is not copy]
        copy.wait()

    def finish(self):
        for copy in self.open:
            copy.wait()
        self.open = []


def by_rows(count, body):
    for at in range(0, count, CHUNK):
        body(pl.ds(at, CHUNK))


def standard(summed):
    centred = summed - jnp.mean(summed, -1, keepdims=True)
    inv_std = lax.rsqrt(jnp.mean(centred * centred, -1, keepdims=True) + EPSILON)
    return centred * inv_std, inv_std


def fold(value):
    return jnp.sum(value.reshape(value.shape[0] // 8, 8, value.shape[1]), 0)


def norm_back(grad_out, normed, inv_std, gain, sums, slot):
    sums[slot, 0] += fold(grad_out * normed)
    sums[slot, 1] += fold(grad_out)
    grad_normed = grad_out * gain
    return inv_std * (
        grad_normed
        - jnp.mean(grad_normed, -1, keepdims=True)
        - normed * jnp.mean(grad_normed * normed, -1, keepdims=True)
    )


def gelu_both(preact):
    size = jnp.abs(preact)
    bell = jnp.exp(-0.5 * preact * preact)
    t = 1.0 / (1.0 + (0.3275911 * math.sqrt(0.5)) * size)
    series = t * (
        0.5 * 0.254829592
        + t * (-0.5 * 0.284496736 + t * (0.5 * 1.421413741 + t * (-0.5 * 1.453152027 + t * (0.5 * 1.061405429))))
    )
    tail = series * bell
    below = jnp.where(preact >= 0.0, 1.0 - tail, tail)
    return preact * below, below + preact * bell * (1.0 / math.sqrt(2.0 * math.pi))


def head_lanes(width, head_dim):
    lane = lax.broadcasted_iota(jnp.int32, (1, width), 1)
    first = jnp.where(lane < head_dim, 1.0, 0.0)
    return first, 1.0 - first


def lanes(value, low, high):
    return jnp.concatenate([value * low, value * high], 0)


def weights_of(scores):
    grown = [jnp.exp(s - jnp.max(s, 0, keepdims=True)) for s in scores]
    return [(e * (1.0 / jnp.sum(e, 0, keepdims=True))).astype(BF) for e in grown]


def scores_back(weights_b, grad_w):
    weights = [w.astype(F32) for w in weights_b]
    return [(w * (g - jnp.sum(g * w, 0, keepdims=True))).astype(BF) for w, g in zip(weights, grad_w)]


def self_attend(qkv, mask, probs, att, groups, first_group, span, head_dim):
    width = 2 * head_dim
    model = att.shape[1]
    pairs = model // width
    low, high = head_lanes(width, head_dim)
    scale = 1.0 / math.sqrt(head_dim)
    low_b, high_b = (low * scale).astype(BF), (high * scale).astype(BF)
    at = [p * width for p in range(pairs)]

    @pl.loop(0, groups)
    def _(g):
        rows = pl.ds(pl.multiple_of(g * span, span), span)
        bias = mask[first_group + g]
        both = [lanes(qkv[rows, c : c + width], low_b, high_b) for c in at]
        scores = [nt(qkv[rows, model + c : model + c + width], b) + bias for c, b in zip(at, both)]
        weights = weights_of(scores)
        for p, c in enumerate(at):
            probs[g * pairs + p] = weights[p]
            out = tn(weights[p], qkv[rows, 2 * model + c : 2 * model + c + width])
            att[rows, c : c + width] = (out[:span] * low + out[span:] * high).astype(BF)


def self_attend_back(qkv, probs, grad_att, grad_qkv, groups, span, head_dim):
    width = 2 * head_dim
    model = grad_att.shape[1]
    pairs = model // width
    low, high = head_lanes(width, head_dim)
    scale = 1.0 / math.sqrt(head_dim)
    low_s, high_s = low * scale, high * scale
    scaled, plain = (low_s.astype(BF), high_s.astype(BF)), (low.astype(BF), high.astype(BF))
    at = [p * width for p in range(pairs)]

    @pl.loop(0, groups)
    def _(g):
        rows = pl.ds(pl.multiple_of(g * span, span), span)
        both_g = [lanes(grad_att[rows, c : c + width], *plain) for c in at]
        weights = [probs[g * pairs + p] for p in range(pairs)]
        grad_w = [nt(qkv[rows, 2 * model + c : 2 * model + c + width], b) for c, b in zip(at, both_g)]
        grad_s = scores_back(weights, grad_w)
        for p, c in enumerate(at):
            out = tn(grad_s[p], qkv[rows, model + c : model + c + width])
            both_q = lanes(qkv[rows, c : c + width], *scaled)
            grad_qkv[rows, c : c + width] = (out[:span] * low_s + out[span:] * high_s).astype(BF)
            grad_qkv[rows, model + c : model + c + width] = nn(grad_s[p], both_q).astype(BF)
            grad_qkv[rows, 2 * model + c : 2 * model + c + width] = nn(weights[p], both_g[p]).astype(BF)


def cross_attend(queries, keys, vals, image, first_row, probs, out, row_count, length, patches, head_dim):
    width = 2 * head_dim
    pairs = queries.shape[1] // width
    low, high = head_lanes(width, head_dim)
    scale = 1.0 / math.sqrt(head_dim)
    low_s, high_s = low * scale, high * scale
    shown = lax.broadcasted_iota(jnp.int32, (keys.shape[1], 2 * length), 0) < patches
    at = [slice(p * width, p * width + width) for p in range(pairs)]

    @pl.loop(0, row_count)
    def _(r):
        rows = pl.ds(pl.multiple_of(r * length, 8), length)
        picked = image[first_row + r]
        both = [lanes(queries[rows, c], low_s, high_s).astype(BF) for c in at]
        scores = [jnp.where(shown, nt(keys[picked, :, c], b), MASKED) for c, b in zip(at, both)]
        weights = weights_of(scores)
        for p, c in enumerate(at):
            probs[r * pairs + p] = weights[p]
            got = tn(weights[p], vals[picked, :, c])
            out[rows, c] = got[:length] * low + got[length:] * high


def cross_attend_back(
    queries, keys, vals, image, first_row, probs, grad_att, grad_q, grad_k, grad_v, row_count, length, head_dim
):
    width = 2 * head_dim
    pairs = queries.shape[1] // width
    low, high = head_lanes(width, head_dim)
    scale = 1.0 / math.sqrt(head_dim)
    low_s, high_s = low * scale, high * scale
    at = [slice(p * width, p * width + width) for p in range(pairs)]

    @pl.loop(0, row_count)
    def _(r):
        rows = pl.ds(pl.multiple_of(r * length, 8), length)
        picked = image[first_row + r]
        both_g = [lanes(grad_att[rows, c], low, high).astype(BF) for c in at]
        weights = [probs[r * pairs + p] for p in range(pairs)]
        grad_w = [nt(vals[picked, :, c], b) for c, b in zip(at, both_g)]
        grad_s = scores_back(weights, grad_w)
        for p, c in enumerate(at):
            both_q = lanes(queries[rows, c], low_s, high_s).astype(BF)
            got = tn(grad_s[p], keys[picked, :, c])
            grad_q[rows, c] = got[:length] * low_s + got[length:] * high_s
            grad_k[r, :, c] = nn(grad_s[p], both_q).astype(BF)
            grad_v[r, :, c] = nn(weights[p], both_g[p]).astype(BF)


def grow(entry, w_up, preact, hidden, slope):
    tile = preact.shape[1]
    for j in range(hidden.shape[1] // tile):
        cols = slice(j * tile, j * tile + tile)
        preact[...] = nn(entry[...], w_up[:, cols])

        def body(rows):
            value, rise = gelu_both(preact[rows, :])
            hidden[rows, cols] = value.astype(BF)
            slope[rows, cols] = rise.astype(BF)

        by_rows(preact.shape[0], body)


def shrink(branch, w_down, slope, grad_pre):
    tile = branch.shape[1]
    for j in range(slope.shape[1] // tile):
        cols = slice(j * tile, j * tile + tile)
        grad_pre[:, cols] = (nt(branch[...], w_down[cols, :]) * slope[:, cols].astype(F32)).astype(BF)


class Refs:
    def __init__(self, names, refs):
        for name, ref in zip(names, refs):
            setattr(self, name, ref)


def remote(r, number, source, target, device):
    copy = pltpu.make_async_remote_copy(
        src_ref=source, dst_ref=target, send_sem=r.send_sems.at[number], recv_sem=r.recv_sems.at[number],
        device_id=device, device_id_type=pl.DeviceIdType.MESH,
    )
    copy.start()
    return copy


def greet(device):
    pl.semaphore_signal(
        pltpu.get_barrier_semaphore(), inc=1, device_id=device, device_id_type=pl.DeviceIdType.MESH
    )


def greeted(count):
    pl.semaphore_wait(pltpu.get_barrier_semaphore(), count)


def text_forward(r, cp, half, span, out, send):
    count = r.x_s.shape[0]
    own = pl.ds(half * count, count)
    groups = count // span
    text = cp.load(r.text.at[own], r.x_s)
    gets = weights_in(r, cp) if half == 0 else None
    text.wait()
    cp.store(r.x_s, r.entry.at[own])
    if half == 0:
        gets[0].wait()
    r.qkv_s[...] = nn(r.x_s[...], r.wqkv_s[...]).astype(BF)
    cp.store(r.qkv_s, r.qkv.at[half])
    self_attend(r.qkv_s, r.mask, r.probs_s, r.att_s, groups, half * groups, span, r.x_s.shape[1] // HEADS)
    cp.store(r.probs_s, r.probs.at[half])
    cp.store(r.att_s, r.att.at[own])
    if half == 0:
        gets[1].wait()
    r.y1_s[...] = r.x_s[...].astype(F32) + nn(r.att_s[...], r.wo_s[...])
    cp.store(r.y1_s, r.y1.at[half])

    def first(rows):
        value = standard(r.y1_s[rows, :])[0] * r.gains[0:1, :] + r.biases[0:1, :]
        r.mid_s[rows, :] = value
        r.zb_s[rows, :] = value.astype(BF)

    by_rows(count, first)
    cp.store(r.zb_s, r.zb.at[own])
    if half == 0:
        gets[2].wait()
    grow(r.zb_s, r.w1_s, r.pre_s, r.hid_s, r.slo_s)
    cp.store(r.hid_s, r.hidden.at[own])
    cp.store(r.slo_s, r.slope.at[half])
    if half == 0:
        gets[3].wait()
    r.y3_s[...] = r.mid_s[...] + nn(r.hid_s[...], r.w2_s[...])
    cp.store(r.y3_s, r.y3.at[half])

    def second(rows):
        out[rows, :] = (standard(r.y3_s[rows, :])[0] * r.gains[1:2, :] + r.biases[1:2, :]).astype(BF)

    by_rows(count, second)
    sent = send()
    cp.store(out, r.lay.at[own])
    cp.finish()
    return sent


def weights_in(r, cp):
    return [cp.load(a, b) for a, b in ((r.wqkv, r.wqkv_s), (r.wo, r.wo_s), (r.w1, r.w1_s), (r.w2, r.w2_s))]


def text_back(r, cp, half, span, arrived):
    count, model = r.y1_s.shape
    own = pl.ds(half * count, count)
    groups = count // span
    kept = [
        cp.load(a.at[half], b)
        for a, b in ((r.y3, r.y3_s), (r.slope, r.slo_s), (r.y1, r.y1_s), (r.qkv, r.qkv_s), (r.probs, r.probs_s))
    ]
    r.sum_s[...] = jnp.zeros_like(r.sum_s)
    for copy in kept:
        copy.wait()
    arrived()

    def first(rows):
        normed, inv_std = standard(r.y3_s[rows, :])
        value = norm_back(r.bnd_s[half, rows, :].astype(F32), normed, inv_std, r.gains[1:2, :], r.sum_s, 1)
        r.dy_s[rows, :] = value
        r.df_s[rows, :] = value.astype(BF)

    by_rows(count, first)
    df = cp.store(r.df_s, r.df.at[own])
    shrink(r.df_s, r.w2_s, r.slo_s, r.hid_s)
    cp.store(r.hid_s, r.du.at[own])
    r.mid_s[...] = r.dy_s[...] + nt(r.hid_s[...], r.w1_s[...])
    cp.settle(df)

    def second(rows):
        normed, inv_std = standard(r.y1_s[rows, :])
        value = norm_back(r.mid_s[rows, :], normed, inv_std, r.gains[0:1, :], r.sum_s, 0)
        r.dy_s[rows, :] = value
        r.df_s[rows, :] = value.astype(BF)

    by_rows(count, second)
    cp.store(r.df_s, r.da.at[own])
    cp.store(r.sum_s, r.sums.at[half])
    r.att_s[...] = nt(r.df_s[...], r.wo_s[...]).astype(BF)
    self_attend_back(r.qkv_s, r.probs_s, r.att_s, r.dqkv_s, groups, span, model // HEADS)
    cp.store(r.dqkv_s, r.dqkv.at[own])
    r.pre_s[...] = r.dy_s[...] + nt(r.dqkv_s[...], r.wqkv_s[...])
    cp.store(r.pre_s, r.ig.at[own])
    cp.finish()


def join(r, cp, half, span, length, patches, gets, back, arrived, send):
    count, model = r.mid_s.shape
    head_dim = model // HEADS
    own = pl.ds(half * count, count)
    row_count = count // length
    groups = count // span
    pictures = pl.ds(half * row_count, row_count)
    g_cot = cp.load(r.cot.at[own], r.g_s)

    def ready(number):
        if half == 0:
            gets[number].wait()

    r.sum_s[...] = jnp.zeros_like(r.sum_s)
    ready(0)
    arrived()
    entry = r.bnd_s.at[half]
    cp.store(entry, r.entry.at[own])
    r.qkv_s[...] = nn(entry[...], r.wqkv_s[...]).astype(BF)
    self_attend(r.qkv_s, r.mask, r.probs_s, r.att_s, groups, half * groups, span, head_dim)
    att = cp.store(r.att_s, r.att.at[own])
    ready(1)
    r.y1_s[...] = entry[...].astype(F32) + nn(r.att_s[...], r.wo_s[...])

    def first(rows):
        value = standard(r.y1_s[rows, :])[0] * r.gains[0:1, :] + r.biases[0:1, :]
        r.mid_s[rows, :] = value
        r.midb_s[rows, :] = value.astype(BF)

    by_rows(count, first)
    cp.store(r.midb_s, r.midb.at[own])
    ready(4)
    r.qc_s[...] = nn(r.midb_s[...], r.wq_s[...]).astype(BF).astype(F32)
    cross_attend(r.qc_s, r.key_s, r.val_s, r.image, half * row_count, r.cprobs_s, r.cat_s, row_count, length, patches,
                 head_dim)
    r.catb_s[...] = r.cat_s[...].astype(BF)
    catt = cp.store(r.catb_s, r.catt.at[own])
    ready(5)
    r.y2_s[...] = r.mid_s[...] + nn(r.catb_s[...], r.wc_s[...])

    def second(rows):
        value = standard(r.y2_s[rows, :])[0] * r.cgain[...] + r.cbias[...]
        r.mid_s[rows, :] = value
        r.zb_s[rows, :] = value.astype(BF)

    by_rows(count, second)
    cp.store(r.zb_s, r.zb.at[own])
    ready(2)
    grow(r.zb_s, r.w1_s, r.pre_s, r.hid_s, r.slo_s)
    hidden = cp.store(r.hid_s, r.hidden.at[own])
    ready(3)
    r.y3_s[...] = r.mid_s[...] + nn(r.hid_s[...], r.w2_s[...])
    g_cot.wait()

    def third(rows):
        normed, inv_std = standard(r.y3_s[rows, :])
        r.lay_s[rows, :] = (normed * r.gains[1:2, :] + r.biases[1:2, :]).astype(BF)
        value = norm_back(r.g_s[rows, :].astype(F32), normed, inv_std, r.gains[1:2, :], r.sum_s, 1)
        r.dy_s[rows, :] = value
        r.df_s[rows, :] = value.astype(BF)

    by_rows(count, third)
    cp.store(r.lay_s, r.lay.at[own])
    df = cp.store(r.df_s, r.df.at[own])
    cp.settle(hidden)
    shrink(r.df_s, r.w2_s, r.slo_s, r.hid_s)
    du = cp.store(r.hid_s, r.du.at[own])
    r.mid_s[...] = r.dy_s[...] + nt(r.hid_s[...], r.w1_s[...])
    cp.settle(df)

    def fourth(rows):
        normed, inv_std = standard(r.y2_s[rows, :])
        value = norm_back(r.mid_s[rows, :], normed, inv_std, r.cgain[...], r.sum_s, 2)
        r.dy_s[rows, :] = value
        r.df_s[rows, :] = value.astype(BF)

    by_rows(count, fourth)
    dca = cp.store(r.df_s, r.dca.at[own])
    r.cat_s[...] = nt(r.df_s[...], r.wc_s[...]).astype(BF).astype(F32)
    cross_attend_back(r.qc_s, r.key_s, r.val_s, r.image, half * row_count, r.cprobs_s, r.cat_s, r.pre_s, r.dkey_s,
                      r.dval_s, row_count, length, head_dim)
    cp.store(r.dkey_s, r.dkey.at[pictures])
    cp.store(r.dval_s, r.dval.at[pictures])
    cp.settle(catt)
    r.catb_s[...] = r.pre_s[...].astype(BF)
    cp.store(r.catb_s, r.dq.at[own])
    r.mid_s[...] = r.dy_s[...] + nt(r.catb_s[...], r.wq_s[...])
    cp.settle(dca)

    def fifth(rows):
        normed, inv_std = standard(r.y1_s[rows, :])
        value = norm_back(r.mid_s[rows, :], normed, inv_std, r.gains[0:1, :], r.sum_s, 0)
        r.dy_s[rows, :] = value
        r.df_s[rows, :] = value.astype(BF)

    by_rows(count, fifth)
    cp.store(r.df_s, r.da.at[own])
    cp.store(r.sum_s, r.sums.at[half])
    cp.settle(att)
    r.att_s[...] = nt(r.df_s[...], r.wo_s[...]).astype(BF)
    self_attend_back(r.qkv_s, r.probs_s, r.att_s, r.dqkv_s, groups, span, head_dim)
    cp.store(r.dqkv_s, r.dqkv.at[own])
    r.mid_s[...] = r.dy_s[...] + nt(r.dqkv_s[...], r.wqkv_s[...])
    back[...] = r.mid_s[...].astype(BF)
    send()
    cp.store(r.mid_s, r.ig.at[own])
    cp.finish()


PIECES = 5


def project(r, cp, rows, patches, own, source, beside):
    total, width = r.pix_s.shape
    chunk = total // PIECES
    weight = cp.load(r.wimg, r.wimg_s)
    gets = [cp.load(r.images.at[pl.ds(c * chunk, chunk)], r.pix_s.at[pl.ds(c * chunk, chunk)]) for c in range(PIECES)]
    later = weights_in(r, cp) + [cp.load(r.wq, r.wq_s), cp.load(r.wc, r.wc_s)]

    def spread(source, target):
        target[:, patches - 1 : PAD, :] = jnp.zeros((rows, PAD - patches + 1, target.shape[2]), BF)
        for c in range(PIECES):
            if target is r.val_s:
                gets[c].wait()
            at = slice(c * chunk, c * chunk + chunk)
            got = nn(r.pix_s[at, :], source[...])
            for t in range(r.flat_s.shape[0]):
                r.flat_s[t, at, :] = got[:, t * LANES : t * LANES + LANES]
        for i in range(rows):
            for t in range(r.flat_s.shape[0]):
                target[i, :patches, t * LANES : t * LANES + LANES] = r.flat_s[
                    t, pl.ds(i, patches, stride=rows), :
                ].astype(BF)

    weight.wait()
    spread(r.wimg_s, r.val_s)
    expect(r, 0, r.wk_s.at[own], r.wk_s.at[own], source).wait_recv()
    greeted(2)
    swap = remote(r, 1, r.wk_s.at[own], r.wk_s.at[own], beside)
    swap.wait_recv()
    cp.store(r.wk_s, r.wk)
    spread(r.wk_s, r.key_s)
    swap.wait_send()
    return later


def relay_kernel(halves, span, length, patches, names, scopes, *refs):
    r = Refs(names, refs)
    section, place = lax.axis_index("section"), lax.axis_index("dp")
    core = lax.rem(place, jnp.int32(2))
    partner, beside = (1 - section, place), (section, place + 1 - 2 * core)
    half = r.wimg.shape[0] // 2
    own = pl.ds(pl.multiple_of(core * half, half), half)
    layer, first = ({n: pltpu.VMEM(*v) for n, v in scope.items()} for scope in scopes)

    def within(scope, body):
        def call(**own):
            for name, ref in own.items():
                setattr(r, name, ref)
            body()

        pl.run_scoped(call, **scope)

    @pl.when(section == 0)
    def _():
        cp = Copies(r.sems)
        greet(partner)
        greeted(1)

        def body():
            sends = [remote(r, 0, r.wimg.at[own], r.wk_s.at[own], partner)]
            for h in range(halves):
                out = (r.lay_s, r.back_s)[h]
                sends.append(
                    text_forward(r, cp, h, span, out, lambda: remote(r, 2 + h, out, r.bnd_s.at[h], partner))
                )
            for h in range(halves):
                text_back(
                    r, cp, h, span, lambda: expect(r, 2 + h, r.back_s, r.bnd_s.at[h], partner).wait_recv()
                )
            for copy in sends:
                copy.wait_send()

        within(layer, body)

    @pl.when(section == 1)
    def _():
        cp = Copies(r.sems)
        greet(partner)
        greet(beside)
        got = []
        within(first, lambda: got.extend(project(r, cp, r.key_s.shape[0], patches, own, partner, beside)))

        def body():
            for h in range(halves):
                back = (r.back_s, r.x_s)[h]
                join(
                    r, cp, h, span, length, patches, got, back,
                    lambda: expect(r, 2 + h, r.lay_s, r.bnd_s.at[h], partner).wait_recv(),
                    lambda: remote(r, 2 + h, back, r.bnd_s.at[h], partner),
                )

        within(layer, body)
        for h in range(halves):
            expect(r, 2 + h, (r.back_s, r.x_s)[h], r.bnd_s.at[h], partner).wait_send()


def expect(r, number, source, target, device):
    return pltpu.make_async_remote_copy(
        src_ref=source, dst_ref=target, send_sem=r.send_sems.at[number], recv_sem=r.recv_sems.at[number],
        device_id=device, device_id_type=pl.DeviceIdType.MESH,
    )


def relay(world, reads, writes, scratch, scopes, kernel, flops):
    smem, vmem, hbm = reads
    names = smem + vmem + hbm + list(writes) + list(scratch) + ["sems", "send_sems", "recv_sems"]
    got = pl.pallas_call(
        functools.partial(kernel, names, scopes),
        in_specs=[SMEM] * len(smem) + [VMEM] * len(vmem) + [ANY] * len(hbm),
        out_specs=[ANY] * len(writes),
        out_shape=list(writes.values()),
        scratch_shapes=[pltpu.VMEM(shape, dtype) for shape, dtype in scratch.values()]
        + [pltpu.SemaphoreType.DMA((100,)), pltpu.SemaphoreType.DMA((4,)), pltpu.SemaphoreType.DMA((4,))],
        compiler_params=pltpu.CompilerParams(vmem_limit_bytes=LIMIT, collective_id=2, has_side_effects=True),
        cost_estimate=pl.CostEstimate(flops=flops, bytes_accessed=40_000_000, transcendentals=0),
        name="relay",
    )(*[world[n] for n in smem + vmem + hbm])
    world.update(zip(writes, got))


TILE = 256
DEEP = 192


class Job:
    def __init__(self, fill, rows, cols, outs, kind=""):
        self.fill, self.rows, self.cols, self.outs, self.kind = fill, rows, cols, outs, kind
        self.depth = rows * (cols // TILE)


class Feed:
    def __init__(self, cp, lefts, rights):
        self.cp, self.lefts, self.rights = cp, lefts, rights
        self.plan, self.at, self.started = [], 0, 0

    def add(self, left, right):
        here = sum(1 for step in self.plan if step[1] is not None) + (right is not None) - 1
        self.plan.append((left, right, len(self.plan) % 2, here % 2))

    def start(self):
        if self.started < len(self.plan):
            left, right, a, b = self.plan[self.started]
            copies = [self.cp.load(left, self.lefts.at[a])]
            if right is not None:
                copies.append(self.cp.load(right, self.rights.at[b, :, pl.ds(0, right.shape[1])]))
            self.plan[self.started] = (copies, right, a, b)
            self.started += 1

    def take(self):
        if self.started == 0:
            self.start()
        self.start()
        copies, _, a, b = self.plan[self.at]
        for copy in copies:
            copy.wait()
        self.at += 1
        return self.lefts.at[a], self.rights.at[b]


def reduce_kernel(names, *refs):
    r = Refs(names, refs)
    section, place = lax.axis_index("section"), lax.axis_index("dp")
    core, y, z = place % 2, place // 2 % 2, place // 4
    partner = (1 - section, place)
    beside = place + 1 - 2 * core
    across = place + 2 - 4 * y
    along = [place + 4 * (1 - 2 * (z % 2)), place + 4 * (2 - 4 * (z // 2)), place + 4 * (3 - 2 * z)]
    far = [z + 1 - 2 * (z % 2), z + 2 - 4 * (z // 2), 3 - z]
    for other in [beside, across] + along:
        greet((section, other))
    tokens, model = r.df.shape
    part, high, tall = model // 16, r.hidden.shape[1] // 16, r.wk.shape[0] // 16
    total_rows, width = r.images.shape
    row_count = r.dkey.shape[0]
    patches = total_rows // row_count
    chunk = total_rows // PIECES
    vm = pltpu.VMEM

    def send(number, kind, source, target, other):
        copy = pltpu.make_async_remote_copy(
            src_ref=source, dst_ref=target, send_sem=r.send_sems.at[number, kind],
            recv_sem=r.recv_sems.at[number, kind], device_id=(section, other), device_id_type=pl.DeviceIdType.MESH,
        )
        copy.start()
        return copy

    def over(number, source, target):
        return pltpu.make_async_remote_copy(
            src_ref=source, dst_ref=target, send_sem=r.far_sends.at[number], recv_sem=r.far_recvs.at[number],
            device_id=partner, device_id_type=pl.DeviceIdType.MESH,
        )

    def lay_out(slot, got, rows, each=None):
        each = each or rows
        for k in range(got.shape[1] // TILE):
            piece = got[:, k * TILE : k * TILE + TILE].reshape(4, 2, 2, rows, TILE)
            r.tile[slot, :, :, :, k * each : k * each + rows, :] = piece

    def norm_rows(slot, rows, each):
        sums = jnp.sum(r.sums[0] + r.sums[1], 2).reshape(6, model)
        sums = jnp.concatenate([sums, jnp.zeros((10, model), F32)], 0)
        row = lax.broadcasted_iota(jnp.int32, (16, TILE), 0)
        for k in range(model // TILE):
            col = lax.broadcasted_iota(jnp.int32, (16, TILE), 1) + k * TILE
            owner = jnp.where(row < 4, col // part, col % (model // 2) // (part // 2))
            value = sums[:, k * TILE : k * TILE + TILE]
            at = pl.ds(k * each + rows, 16)
            for d in range(16):
                r.tile[slot, d // 4, d // 2 % 2, d % 2, at, :] = jnp.where(owner == d, value, 0.0).astype(BF)

    def product(feed, left, right, cols, rows, norms=False, order=False):
        feed.add(left, right.at[:, cols])

        def fill(slot):
            left_s, right_s = feed.take()
            value = left_s[...]
            if order:
                value = nn(value, r.order_s[...]).astype(BF)
            lay_out(slot, tn(value, right_s[:, : cols.size]).astype(BF), rows, rows + 16 if norms else rows)
            if norms:
                norm_rows(slot, rows, rows + 16)

        return fill

    def stacked(feed, left, right, cols, rows):
        for j in range(4):
            feed.add(left.at[:, pl.ds(j * 4 * rows, 4 * rows)], right.at[:, cols] if j == 0 else None)

        def fill(slot):
            for j in range(4):
                left_s, right_s = feed.take()
                got = tn(left_s[...], right_s[:, : cols.size]).astype(BF)
                r.tile[slot, j, :, :, :rows, :] = got.reshape(2, 2, rows, TILE)

        return fill

    def pictured(cp, flat):
        def fill(slot):
            def body(pix_s):
                cp.load(r.images, pix_s).wait()
                lay_out(slot, tn(pix_s[...], flat[...]).astype(BF), tall)

            pl.run_scoped(body, vm((total_rows, width), BF))

        return fill

    def run(cp, jobs, meet, tasks):
        cores, ys, zs = {}, {}, {}
        total = len(jobs)
        sent = []
        for i in range(total + 4):
            kind = jobs[i].kind if i < total else "none"
            if kind in ("", "give"):
                if i >= 3:
                    cores[i - 3].wait_send()
                slot, deep = i % 3, pl.ds(0, jobs[i].depth)
                jobs[i].fill(slot)
                if i == 0:
                    meet()
                cores[i] = send(i, 0, r.tile.at[slot, :, :, 1 - core, deep], r.core_in.at[i, :, :, deep], beside)
            for task in tasks.get(i, ()):
                task()
            if kind in ("", "give"):
                cores[i].wait_recv()

                @pl.loop(0, 4)
                def _(a):
                    for b in range(2):
                        r.core_in[i, a, b, deep, :] = r.core_in[i, a, b, deep, :] + r.tile[slot, a, b, core, deep, :]

            if i < total:
                deep = pl.ds(0, jobs[i].depth)
                if kind:
                    handed = over(marks[3], r.core_in.at[i, :, :, deep], r.core_in.at[handed_to, :, :, deep])
                if kind == "give":
                    handed.start()
                    sent.append(handed)
                else:
                    if kind == "take":
                        handed.wait_recv()
                    ys[i] = send(i, 1, r.core_in.at[i, :, 1 - y, deep], r.y_in.at[i, :, deep], across)
            j = i - 2
            if 0 <= j < total and jobs[j].kind != "give":
                ys[j].wait_recv()
                deep = pl.ds(0, jobs[j].depth)

                @pl.loop(0, 4)
                def _(a):
                    r.y_in[j, a, deep, :] = r.y_in[j, a, deep, :] + r.core_in[j, a, y, deep, :]

                for step in range(3):
                    zs[j, step] = send(
                        j, 2 + step, r.y_in.at[j, far[step], deep], r.z_in.at[j, step, deep], along[step]
                    )
            j = i - 4
            if 0 <= j < total and jobs[j].kind != "give":
                for step in range(3):
                    zs[j, step].wait_recv()
                deep = pl.ds(0, jobs[j].depth)
                r.final[j, deep, :] = (
                    r.y_in[j, z, deep, :].astype(F32) + r.z_in[j, 0, deep, :].astype(F32)
                ) + (r.z_in[j, 1, deep, :].astype(F32) + r.z_in[j, 2, deep, :].astype(F32))
                each = jobs[j].rows
                for k in range(jobs[j].cols // TILE):
                    for row, rows, target, first, number in jobs[j].outs:
                        source = r.final.at[j, pl.ds(k * each + row, rows)]
                        target = target.at[:, pl.ds(first + k * TILE, TILE)]
                        if number is None:
                            cp.store(source, target)
                        else:
                            sent.append(over(number + k, source, target))
                            sent[-1].start()
        for i in range(total):
            if i >= total - 3 and i in cores or i + 3 < total and i + 3 not in cores:
                cores[i].wait_send()
            if i in ys:
                ys[i].wait_send()
                for step in range(3):
                    zs[i, step].wait_send()
        for copy in sent:
            copy.wait_send()
        cp.finish()

    def ffn_jobs(feed):
        jobs = []
        for at in range(0, model, TILE):
            jobs.append(Job(stacked(feed, r.hidden, r.df, pl.ds(at, TILE), high), high, TILE, [(0, high, r.down, at, None)]))
        wide = DEEP // part * TILE
        for at in range(0, r.hidden.shape[1], wide):
            jobs.append(Job(product(feed, r.zb, r.du, pl.ds(at, wide), part), part, wide, [(0, part, r.up, at, None)]))
        return jobs

    def self_jobs(feed, norms):
        jobs = []
        for at in range(0, 3 * model, model):
            jobs.append(Job(product(feed, r.entry, r.dqkv, pl.ds(at, model), part), part, model,
                            [(0, part, r.qkv, at, None)]))
        outs = [(0, part, r.out, 0, None)] + ([(part, 16, r.norms, 0, None)] if norms else [])
        jobs.append(Job(product(feed, r.att, r.da, pl.ds(0, model), part, norms), part + 16 * norms, model, outs))
        return jobs

    parcels, handed_to = model // TILE, 10
    marks = [PIECES + parcels * n for n in range(4)]

    @pl.when(section == 0)
    def _():
        cp = Copies(r.sems)

        def meet():
            greeted(6)
            greet(partner)

        def widen(c):
            over(c, r.far_s.at[c], r.far_s.at[c]).wait_recv()
            if c > 1:
                cp.settle(stores[c - 2])
            r.own_s[c % 2] = r.far_s[c].astype(F32)
            stores.append(cp.store(r.own_s.at[c % 2], r.image_grad.at[pl.ds(c * chunk, chunk)]))

        feed = Feed(cp, r.left_s, r.right_s)
        jobs, stores = ffn_jobs(feed) + self_jobs(feed, True), []
        jobs.append(Job(None, tall, model, [(0, tall, r.wide, 0, None)], "take"))
        last = len(jobs) + 3
        run(cp, jobs, meet, {last - PIECES + c: [functools.partial(widen, c)] for c in range(PIECES)})
        for first, rows, target in ((marks[0], part // 2, r.cross_q), (marks[1], part // 2, r.cross_o),
                                    (marks[2], 16, r.far_norms)):
            for k in range(parcels):
                piece = target.at[:, pl.ds(k * TILE, TILE)]
                over(first + k, r.final.at[0, pl.ds(0, rows)], piece).wait_recv()

    @pl.when(section == 1)
    def _():
        cp = Copies(r.sems)
        feed = Feed(cp, r.left_s, r.right_s)
        first = ffn_jobs(feed)

        def meet():
            greeted(5)
            greet(partner)

        def flatten(source, flat, weight, weight_s):
            def body(grad_s, flat_s):
                copies = [cp.load(source, grad_s), cp.load(weight, weight_s)]
                if weight is r.wk:
                    copies.append(cp.load(r.order, r.order_s))
                for copy in copies:
                    copy.wait()
                for t in range(model // LANES):
                    lanes_at = slice(t * LANES, t * LANES + LANES)
                    for i in range(row_count):
                        flat_s[t % 2, pl.ds(i, patches, stride=row_count), :] = grad_s[
                            r.row_of[i], :patches, lanes_at
                        ].astype(F32)
                    flat[:, lanes_at] = flat_s[t % 2].astype(BF)

            pl.run_scoped(body, vm(r.dkey.shape, BF), vm((2, total_rows, LANES), F32))

        def pixel_grad(c):
            if c > 1:
                cp.settle(stores[c - 2])
            at, half = slice(c * chunk, c * chunk + chunk), width // 2
            r.far_s[c] = (nt(r.fk_s[at, :], r.wk_s[:half, :]) + nt(r.fv_s[at, :], r.wimg_s[:half, :])).astype(BF)
            if c == 0:
                greeted(1)
            over(c, r.far_s.at[c], r.far_s.at[c]).start()
            r.own_s[c % 2] = nt(r.fk_s[at, :], r.wk_s[half:, :]) + nt(r.fv_s[at, :], r.wimg_s[half:, :])
            stores.append(cp.store(r.own_s.at[c % 2], r.image_grad.at[pl.ds(c * chunk, chunk)]))

        stores = []
        own = part // 2
        joint = [
            Job(product(feed, r.dq, r.midb, pl.ds(0, model), part, False, True), part, model,
                [(0, own, r.cross_q, 0, marks[0]), (own, own, r.cross_q, 0, None)]),
            Job(pictured(cp, r.fk_s), tall, model, [], "give"),
            Job(product(feed, r.dca, r.catt, pl.ds(0, model), part, True, True), part + 16, model,
                [(0, own, r.cross_o, 0, marks[1]), (own, own, r.cross_o, 0, None), (part, 16, r.norms, 0, None),
                 (part, 16, r.far_norms, 0, marks[2])]),
            Job(pictured(cp, r.fv_s), tall, model, [(0, tall, r.wide, 0, None)]),
        ]
        tasks = {1: [lambda: flatten(r.dkey, r.fk_s, r.wk, r.wk_s)], 2: [lambda: flatten(r.dval, r.fv_s, r.wimg, r.wimg_s)]}
        for c, at in enumerate((4, 5, 6, 8, 10)):
            tasks[at] = [functools.partial(pixel_grad, c)]
        run(cp, first + joint + self_jobs(feed, False), meet, tasks)
        for c in range(PIECES):
            over(c, r.far_s.at[c], r.far_s.at[c]).wait_send()


def reduce_all(world, dp):
    tokens, model = world["df"].shape
    part, tall = model // dp, world["wk"].shape[0] // dp
    hidden, total_rows, width = world["hidden"].shape[1], world["images"].shape[0], world["images"].shape[1]
    jobs = 14
    chunk = total_rows // PIECES
    writes = dict(
        down=(hidden // dp, model), up=(part, hidden), qkv=(part, 3 * model), out=(part, model), norms=(16, model),
        far_norms=(16, model), wide=(tall, model), cross_q=(part // 2, model), cross_o=(part // 2, model),
        image_grad=(total_rows, width // 2),
    )
    hbm = ["hidden", "df", "zb", "du", "att", "da", "entry", "dqkv", "dq", "midb", "dca", "catt", "images", "dkey",
           "dval", "wk", "wimg", "order"]
    vm = pltpu.VMEM
    scratch = dict(
        tile=vm((3, 4, 2, 2, DEEP, TILE), BF), core_in=vm((jobs, 4, 2, DEEP, TILE), BF),
        y_in=vm((jobs, 4, DEEP, TILE), BF), z_in=vm((jobs, 3, DEEP, TILE), BF), final=vm((jobs, DEEP, TILE), F32),
        left_s=vm((2, tokens, model), BF), right_s=vm((2, tokens, hidden // 3), BF), order_s=vm((model, model), BF),
        fk_s=vm((total_rows, model), BF), fv_s=vm((total_rows, model), BF), wk_s=vm((width, model), BF),
        wimg_s=vm((width, model), BF), far_s=vm((PIECES, chunk, width // 2), BF), own_s=vm((2, chunk, width // 2), F32),
        sems=pltpu.SemaphoreType.DMA((128,)), send_sems=pltpu.SemaphoreType.DMA((jobs, 5)),
        recv_sems=pltpu.SemaphoreType.DMA((jobs, 5)),
        far_sends=pltpu.SemaphoreType.DMA((PIECES + 4 * (model // TILE),)),
        far_recvs=pltpu.SemaphoreType.DMA((PIECES + 4 * (model // TILE),)),
    )
    names = ["row_of", "sums"] + hbm + list(writes) + list(scratch)
    got = pl.pallas_call(
        functools.partial(reduce_kernel, names),
        in_specs=[SMEM, VMEM] + [ANY] * len(hbm),
        out_specs=[ANY] * len(writes),
        out_shape=[jax.ShapeDtypeStruct(shape, F32) for shape in writes.values()],
        scratch_shapes=list(scratch.values()),
        compiler_params=pltpu.CompilerParams(vmem_limit_bytes=LIMIT, collective_id=1, has_side_effects=True),
        cost_estimate=pl.CostEstimate(flops=20_000_000_000, bytes_accessed=40_000_000, transcendentals=0),
        name="reduce_all",
    )(world["row_of"], world["sums"], *[world[n] for n in hbm])
    return dict(zip(writes, got))


def reduce_plain(world, dp):
    model, width = world["df"].shape[1], world["images"].shape[1]
    is_text = lax.axis_index("section") == 0
    place = lax.axis_index("dp")

    def total(value):
        return lax.psum_scatter(value, "dp", scatter_dimension=0, tiled=True).astype(F32)

    def by_owner(value):
        own = value.reshape(2, dp, model // (2 * dp), model)
        return jnp.swapaxes(own, 0, 1).reshape(model, model)

    def grad(left, right):
        return total(tn(world[left], world[right]).astype(BF))

    def flat(value):
        value = value[world["row_of"], : world["images"].shape[0] // value.shape[0]]
        return jnp.swapaxes(value, 0, 1).reshape(-1, model)

    def over(value):
        return lax.ppermute(value, "section", [(1, 0)])

    dkey, dval = flat(world["dkey"]), flat(world["dval"])
    pixels = nt(dkey, world["wk"]) + nt(dval, world["wimg"])
    far = over(pixels[:, : width // 2].astype(BF)).astype(F32)
    wide_k, wide_v = (total(tn(world["images"], g).astype(BF)) for g in (dkey, dval))
    cross_q, cross_o = (
        total(by_owner(tn(world[a], world[b]).astype(BF))) for a, b in (("dq", "midb"), ("dca", "catt"))
    )
    own = cross_q.shape[0] // 2
    norms = lax.psum(jnp.sum(world["sums"], (0, 3)).reshape(6, model).at[4:].multiply(jnp.where(is_text, 0.0, 1.0)), "dp")
    del place
    return dict(
        down=grad("hidden", "df"), up=grad("zb", "du"), qkv=grad("entry", "dqkv"), out=grad("att", "da"), norms=norms,
        far_norms=over(norms), wide=jnp.where(is_text, over(wide_k), wide_v),
        cross_q=jnp.where(is_text, over(cross_q[:own]), cross_q[own:]),
        cross_o=jnp.where(is_text, over(cross_o[:own]), cross_o[own:]),
        image_grad=jnp.where(is_text, far, pixels[:, width // 2 :]),
    )


def per_device(
    text_in, cotangent, images, segment_ids, row_image, self_qkv, self_out, ffn_up, ffn_down,
    norm_gain, norm_bias, image_kv, cross_query, cross_out, cross_gain, cross_bias,
):
    tokens, model = text_in.shape
    row_total, length = segment_ids.shape
    patches, width = images.shape[1:]
    hidden_width = ffn_up.shape[2]
    block_rows = row_image.shape[1]
    head_dim = model // HEADS
    pairs = HEADS // 2
    count = tokens // HALVES
    half_rows = row_total // HALVES
    span = 2 * length
    dp = lax.axis_size("dp")
    section = lax.axis_index("section")
    is_text = section == 0
    flag = section.astype(jnp.int32).reshape(1)
    place = lax.axis_index("dp")
    wqkv, wo, w1, w2 = self_qkv[0], self_out[0], ffn_up[0], ffn_down[0]
    gains, biases = norm_gain[0], norm_bias[0]
    cgain, cbias = cross_gain.reshape(1, model), cross_bias.reshape(1, model)

    marks = (segment_ids + segment_ids.shape[1] * (jnp.arange(row_total, dtype=jnp.int32) % 2)[:, None]).reshape(-1, span)
    mask = jnp.where(marks[:, :, None] == jnp.tile(marks, (1, 2))[:, None, :], 0.0, MASKED).astype(F32)
    in_block = jnp.arange(row_total, dtype=jnp.int32) // block_rows * block_rows
    image = row_image.reshape(-1) + in_block
    slots = jnp.arange(block_rows, dtype=jnp.int32)
    row_of = jnp.sum(jnp.where(row_image[:, :, None] == slots, slots[:, None], 0), 1).reshape(-1) + in_block

    def shape(*dims, dtype=BF):
        return jax.ShapeDtypeStruct(dims, dtype)

    flat_rows = row_total * patches
    pixels = jnp.swapaxes(images, 0, 1).reshape(flat_rows, width)
    probs_shape = (count // span * pairs, span, 2 * span)
    world = dict(
        image=image, row_of=row_of, gains=gains, biases=biases, cgain=cgain, cbias=cbias, mask=mask, text=text_in,
        cot=cotangent, images=pixels, wqkv=wqkv, wo=wo, w1=w1, w2=w2, wq=cross_query, wc=cross_out, wimg=image_kv,
    )
    small_f, small_b = ((count, model), F32), ((count, model), BF)
    tall_b, wide_b = ((count, hidden_width), BF), ((count, 3 * model), BF)
    picture_b, pictures_b = ((half_rows, PAD, model), BF), ((row_total, PAD, model), BF)
    scratch = dict(
        wqkv_s=(wqkv.shape, BF), wo_s=(wo.shape, BF), w1_s=(w1.shape, BF), w2_s=(w2.shape, BF),
        wq_s=(cross_query.shape, BF), wc_s=(cross_out.shape, BF), wimg_s=(image_kv.shape, BF),
        wk_s=(image_kv.shape, BF), key_s=pictures_b, val_s=pictures_b, bnd_s=((HALVES, count, model), BF),
        x_s=small_b, back_s=small_b,
    )
    layer_s = dict(
        qkv_s=wide_b, probs_s=(probs_shape, BF), att_s=small_b, y1_s=small_f, mid_s=small_f, zb_s=small_b,
        pre_s=small_f, hid_s=tall_b, slo_s=tall_b, y3_s=small_f, lay_s=small_b, g_s=small_b, midb_s=small_b,
        qc_s=small_f, cprobs_s=((half_rows * pairs, PAD, 2 * length), BF), cat_s=small_f, catb_s=small_b,
        y2_s=small_f, df_s=small_b, dy_s=small_f, dkey_s=picture_b, dval_s=picture_b, dqkv_s=wide_b,
        sum_s=((3, 2, 8, model), F32),
    )
    flat_s = ((model // LANES, flat_rows, LANES), F32)
    first_s = dict(pix_s=((flat_rows, width), BF), flat_s=flat_s)
    tokens_b = shape(tokens, model)
    writes = dict(
        lay=tokens_b, zb=tokens_b, hidden=shape(tokens, hidden_width), att=tokens_b, entry=tokens_b,
        ig=shape(tokens, model, dtype=F32), df=tokens_b, du=shape(tokens, hidden_width), da=tokens_b,
        dqkv=shape(tokens, 3 * model), sums=shape(HALVES, 3, 2, 8, model, dtype=F32), midb=tokens_b, dq=tokens_b,
        catt=tokens_b, dca=tokens_b, dkey=shape(row_total, PAD, model), dval=shape(row_total, PAD, model),
        wk=shape(width, model), y1=shape(HALVES, count, model, dtype=F32),
        y3=shape(HALVES, count, model, dtype=F32), qkv=shape(HALVES, count, 3 * model),
        probs=shape(HALVES, *probs_shape), slope=shape(HALVES, count, hidden_width),
    )
    linear = model * 3 * model + model * model + 2 * model * hidden_width
    reads = (
        ["image"], ["gains", "biases", "mask", "cgain", "cbias"],
        ["text", "cot", "images", "wqkv", "wo", "w1", "w2", "wq", "wc", "wimg"],
    )
    relay(
        world, reads, writes, scratch, (layer_s, first_s),
        functools.partial(relay_kernel, HALVES, span, length, patches), 8 * count * (linear + 2 * model * model),
    )
    new = jnp.arange(model, dtype=jnp.int32)
    own = model // (2 * dp)
    source = new % (2 * own) // own * (model // 2) + new // (2 * own) * own + new % own
    world["order"] = jnp.where(new[:, None] == source, 1.0, 0.0).astype(BF)
    world["row_of"] = row_of
    got = reduce_all(world, dp) if dp == 16 else reduce_plain(world, dp)
    out_rows = model // dp
    cross_rows = out_rows // lax.axis_size("section")
    norm_part = lax.dynamic_slice_in_dim(got["norms"][:4], place * out_rows, out_rows, 1).reshape(2, 2, out_rows)
    cross_part = jnp.where(is_text, got["far_norms"][4:6], got["norms"][4:6])
    cross_part = lax.dynamic_slice_in_dim(cross_part, (section * dp + place) * cross_rows, cross_rows, 1)
    image_grad = jnp.swapaxes(got["image_grad"].reshape(patches, row_total, width // 2), 0, 1)
    return (
        world["lay"][None], world["ig"][None], image_grad, got["qkv"][None], got["out"][None], got["up"][None],
        got["down"][None], norm_part[:, 0][None], norm_part[:, 1][None], got["wide"], got["cross_q"].T,
        got["cross_o"].T, cross_part[0], cross_part[1],
    )


def solution(mesh):
    return jax.shard_map(
        per_device,
        mesh=mesh,
        in_specs=(
            P("dp", None),
            P("dp", None),
            P("dp", None, None),
            P("dp", None),
            P("dp", None),
            P("section", None, None),
            P("section", None, None),
            P("section", None, None),
            P("section", None, None),
            P("section", None, None),
            P("section", None, None),
            P(None, "section"),
            P(),
            P(),
            P(),
            P(),
        ),
        out_specs=(
            P("section", "dp", None),
            P("section", "dp", None),
            P("dp", None, "section"),
            P("section", "dp", None),
            P("section", "dp", None),
            P("section", "dp", None),
            P("section", "dp", None),
            P("section", None, "dp"),
            P("section", None, "dp"),
            P("dp", "section"),
            P(None, ("section", "dp")),
            P(None, ("section", "dp")),
            P(("section", "dp")),
            P(("section", "dp")),
        ),
        check_vma=False,
    )
```

```python
import functools
import math

import jax
import jax.numpy as jnp
import numpy as np
from jax import lax
from jax.experimental import pallas as pl
from jax.experimental.pallas import tpu as pltpu
from jax.sharding import PartitionSpec as P

HEADS = 12
EPSILON = 1e-06
MASKED = -1e30
BF = jnp.bfloat16
F32 = jnp.float32
PAD = 160
LANES = 128
HALVES = 2
CHUNK = 32
LIMIT = 60 * 1024 * 1024
ANY = pl.BlockSpec(memory_space=pl.ANY)
SMEM = pl.BlockSpec(memory_space=pltpu.SMEM)
VMEM = pl.BlockSpec(memory_space=pltpu.VMEM)


def nn(left, right):
    return lax.dot_general(left, right, (((1,), (0,)), ((), ())), preferred_element_type=F32)


def nt(left, right):
    return lax.dot_general(left, right, (((1,), (1,)), ((), ())), preferred_element_type=F32)


def tn(left, right):
    return lax.dot_general(left, right, (((0,), (0,)), ((), ())), preferred_element_type=F32)


class Copy:
    def __init__(self, source, target, sems, number):
        self.parts = source, target, sems, number

    def make(self):
        source, target, sems, number = self.parts
        return pltpu.make_async_copy(source, target, sems.at[number])

    def wait(self):
        self.make().wait()


class Copies:
    def __init__(self, sems):
        self.sems, self.used, self.open = sems, 0, []

    def load(self, source, target):
        copy = Copy(source, target, self.sems, self.used)
        self.used += 1
        copy.make().start()
        return copy

    def store(self, source, target):
        copy = self.load(source, target)
        self.open.append(copy)
        return copy

    def settle(self, copy):
        self.open = [other for other in self.open if other is not copy]
        copy.wait()

    def finish(self):
        for copy in self.open:
            copy.wait()
        self.open = []


def by_rows(count, body):
    for at in range(0, count, CHUNK):
        body(pl.ds(at, CHUNK))


def standard(summed):
    centred = summed - jnp.mean(summed, -1, keepdims=True)
    inv_std = lax.rsqrt(jnp.mean(centred * centred, -1, keepdims=True) + EPSILON)
    return centred * inv_std, inv_std


def fold(value):
    return jnp.sum(value.reshape(value.shape[0] // 8, 8, value.shape[1]), 0)


def norm_back(grad_out, normed, inv_std, gain, sums, slot):
    sums[slot, 0] += fold(grad_out * normed)
    sums[slot, 1] += fold(grad_out)
    grad_normed = grad_out * gain
    return inv_std * (
        grad_normed
        - jnp.mean(grad_normed, -1, keepdims=True)
        - normed * jnp.mean(grad_normed * normed, -1, keepdims=True)
    )


def gelu_both(preact):
    size = jnp.abs(preact)
    bell = jnp.exp(-0.5 * preact * preact)
    t = 1.0 / (1.0 + (0.3275911 * math.sqrt(0.5)) * size)
    series = t * (
        0.5 * 0.254829592
        + t * (-0.5 * 0.284496736 + t * (0.5 * 1.421413741 + t * (-0.5 * 1.453152027 + t * (0.5 * 1.061405429))))
    )
    tail = series * bell
    below = jnp.where(preact >= 0.0, 1.0 - tail, tail)
    return preact * below, below + preact * bell * (1.0 / math.sqrt(2.0 * math.pi))


def head_lanes(width, head_dim):
    lane = lax.broadcasted_iota(jnp.int32, (1, width), 1)
    first = jnp.where(lane < head_dim, 1.0, 0.0)
    return first, 1.0 - first


def lanes(value, low, high):
    return jnp.concatenate([value * low, value * high], 0)


def weights_of(scores):
    grown = [jnp.exp(s - jnp.max(s, 0, keepdims=True)) for s in scores]
    return [(e * (1.0 / jnp.sum(e, 0, keepdims=True))).astype(BF) for e in grown]


def scores_back(weights_b, grad_w):
    weights = [w.astype(F32) for w in weights_b]
    return [(w * (g - jnp.sum(g * w, 0, keepdims=True))).astype(BF) for w, g in zip(weights, grad_w)]


def self_attend(qkv, mask, probs, att, groups, first_group, span, head_dim):
    width = 2 * head_dim
    model = att.shape[1]
    pairs = model // width
    low, high = head_lanes(width, head_dim)
    scale = 1.0 / math.sqrt(head_dim)
    low_b, high_b = (low * scale).astype(BF), (high * scale).astype(BF)
    at = [p * width for p in range(pairs)]

    @pl.loop(0, groups, unroll=4)
    def _(g):
        rows = pl.ds(pl.multiple_of(g * span, span), span)
        bias = mask[first_group + g]
        both = [lanes(qkv[rows, c : c + width], low_b, high_b) for c in at]
        scores = [nt(qkv[rows, model + c : model + c + width], b) + bias for c, b in zip(at, both)]
        weights = weights_of(scores)
        for p, c in enumerate(at):
            probs[g * pairs + p] = weights[p]
            out = tn(weights[p], qkv[rows, 2 * model + c : 2 * model + c + width])
            att[rows, c : c + width] = (out[:span] * low + out[span:] * high).astype(BF)


def self_attend_back(qkv, probs, grad_att, grad_qkv, groups, span, head_dim):
    width = 2 * head_dim
    model = grad_att.shape[1]
    pairs = model // width
    low, high = head_lanes(width, head_dim)
    scale = 1.0 / math.sqrt(head_dim)
    low_s, high_s = low * scale, high * scale
    scaled, plain = (low_s.astype(BF), high_s.astype(BF)), (low.astype(BF), high.astype(BF))
    at = [p * width for p in range(pairs)]

    @pl.loop(0, groups, unroll=4)
    def _(g):
        rows = pl.ds(pl.multiple_of(g * span, span), span)
        both_g = [lanes(grad_att[rows, c : c + width], *plain) for c in at]
        weights = [probs[g * pairs + p] for p in range(pairs)]
        grad_w = [nt(qkv[rows, 2 * model + c : 2 * model + c + width], b) for c, b in zip(at, both_g)]
        grad_s = scores_back(weights, grad_w)
        for p, c in enumerate(at):
            out = tn(grad_s[p], qkv[rows, model + c : model + c + width])
            both_q = lanes(qkv[rows, c : c + width], *scaled)
            grad_qkv[rows, c : c + width] = (out[:span] * low_s + out[span:] * high_s).astype(BF)
            grad_qkv[rows, model + c : model + c + width] = nn(grad_s[p], both_q).astype(BF)
            grad_qkv[rows, 2 * model + c : 2 * model + c + width] = nn(weights[p], both_g[p]).astype(BF)


def cross_attend(queries, keys, vals, image, first_row, probs, out, row_count, length, patches, head_dim):
    width = 2 * head_dim
    pairs = queries.shape[1] // width
    low, high = head_lanes(width, head_dim)
    scale = 1.0 / math.sqrt(head_dim)
    low_s, high_s = low * scale, high * scale
    shown = lax.broadcasted_iota(jnp.int32, (keys.shape[1], 2 * length), 0) < patches
    at = [slice(p * width, p * width + width) for p in range(pairs)]

    @pl.loop(0, row_count, unroll=4)
    def _(r):
        rows = pl.ds(pl.multiple_of(r * length, 8), length)
        picked = image[first_row + r]
        both = [lanes(queries[rows, c], low_s, high_s).astype(BF) for c in at]
        scores = [jnp.where(shown, nt(keys[picked, :, c], b), MASKED) for c, b in zip(at, both)]
        weights = weights_of(scores)
        for p, c in enumerate(at):
            probs[r * pairs + p] = weights[p]
            got = tn(weights[p], vals[picked, :, c])
            out[rows, c] = got[:length] * low + got[length:] * high


def cross_attend_back(
    queries, keys, vals, image, first_row, probs, grad_att, grad_q, grad_k, grad_v, row_count, length, head_dim
):
    width = 2 * head_dim
    pairs = queries.shape[1] // width
    low, high = head_lanes(width, head_dim)
    scale = 1.0 / math.sqrt(head_dim)
    low_s, high_s = low * scale, high * scale
    at = [slice(p * width, p * width + width) for p in range(pairs)]

    @pl.loop(0, row_count, unroll=4)
    def _(r):
        rows = pl.ds(pl.multiple_of(r * length, 8), length)
        picked = image[first_row + r]
        both_g = [lanes(grad_att[rows, c], low, high).astype(BF) for c in at]
        weights = [probs[r * pairs + p] for p in range(pairs)]
        grad_w = [nt(vals[picked, :, c], b) for c, b in zip(at, both_g)]
        grad_s = scores_back(weights, grad_w)
        for p, c in enumerate(at):
            both_q = lanes(queries[rows, c], low_s, high_s).astype(BF)
            got = tn(grad_s[p], keys[picked, :, c])
            grad_q[rows, c] = got[:length] * low_s + got[length:] * high_s
            grad_k[r, :, c] = nn(grad_s[p], both_q).astype(BF)
            grad_v[r, :, c] = nn(weights[p], both_g[p]).astype(BF)


def grow(entry, w_up, preact, hidden, slope):
    tile = preact.shape[1]
    for j in range(hidden.shape[1] // tile):
        cols = slice(j * tile, j * tile + tile)
        preact[...] = nn(entry[...], w_up[:, cols])

        def body(rows):
            value, rise = gelu_both(preact[rows, :])
            hidden[rows, cols] = value.astype(BF)
            slope[rows, cols] = rise.astype(BF)

        by_rows(preact.shape[0], body)


def shrink(branch, w_down, slope, grad_pre):
    tile = branch.shape[1]
    for j in range(slope.shape[1] // tile):
        cols = slice(j * tile, j * tile + tile)
        grad_pre[:, cols] = (nt(branch[...], w_down[cols, :]) * slope[:, cols].astype(F32)).astype(BF)


class Refs:
    def __init__(self, names, refs):
        for name, ref in zip(names, refs):
            setattr(self, name, ref)


def remote(r, number, source, target, device):
    copy = pltpu.make_async_remote_copy(
        src_ref=source, dst_ref=target, send_sem=r.send_sems.at[number], recv_sem=r.recv_sems.at[number],
        device_id=device, device_id_type=pl.DeviceIdType.MESH,
    )
    copy.start()
    return copy


def greet(device):
    pl.semaphore_signal(
        pltpu.get_barrier_semaphore(), inc=1, device_id=device, device_id_type=pl.DeviceIdType.MESH
    )


def greeted(count):
    pl.semaphore_wait(pltpu.get_barrier_semaphore(), count)


def text_forward(r, cp, half, span, out, send):
    count = r.x_s.shape[0]
    own = pl.ds(half * count, count)
    groups = count // span
    text = cp.load(r.text.at[own], r.x_s)
    gets = weights_in(r, cp) if half == 0 else None
    text.wait()
    cp.store(r.x_s, r.entry.at[own])
    if half == 0:
        gets[0].wait()
    r.qkv_s[...] = nn(r.x_s[...], r.wqkv_s[...]).astype(BF)
    cp.store(r.qkv_s, r.qkv.at[half])
    self_attend(r.qkv_s, r.mask, r.probs_s, r.att_s, groups, half * groups, span, r.x_s.shape[1] // HEADS)
    cp.store(r.probs_s, r.probs.at[half])
    cp.store(r.att_s, r.att.at[own])
    if half == 0:
        gets[1].wait()
    r.y1_s[...] = r.x_s[...].astype(F32) + nn(r.att_s[...], r.wo_s[...])
    cp.store(r.y1_s, r.y1.at[half])

    def first(rows):
        value = standard(r.y1_s[rows, :])[0] * r.gains[0:1, :] + r.biases[0:1, :]
        r.mid_s[rows, :] = value
        r.zb_s[rows, :] = value.astype(BF)

    by_rows(count, first)
    cp.store(r.zb_s, r.zb.at[own])
    if half == 0:
        gets[2].wait()
    grow(r.zb_s, r.w1_s, r.pre_s, r.hid_s, r.slo_s)
    cp.store(r.hid_s, r.hidden.at[own])
    cp.store(r.slo_s, r.slope.at[half])
    if half == 0:
        gets[3].wait()
    r.y3_s[...] = r.mid_s[...] + nn(r.hid_s[...], r.w2_s[...])
    cp.store(r.y3_s, r.y3.at[half])

    def second(rows):
        out[rows, :] = (standard(r.y3_s[rows, :])[0] * r.gains[1:2, :] + r.biases[1:2, :]).astype(BF)

    by_rows(count, second)
    sent = send()
    cp.store(out, r.lay.at[own])
    cp.finish()
    return sent


def weights_in(r, cp):
    return [cp.load(a, b) for a, b in ((r.wqkv, r.wqkv_s), (r.wo, r.wo_s), (r.w1, r.w1_s), (r.w2, r.w2_s))]


def text_back(r, cp, half, span, arrived):
    count, model = r.y1_s.shape
    own = pl.ds(half * count, count)
    groups = count // span
    kept = [
        cp.load(a.at[half], b)
        for a, b in ((r.y3, r.y3_s), (r.slope, r.slo_s), (r.y1, r.y1_s), (r.qkv, r.qkv_s), (r.probs, r.probs_s))
    ]
    r.sum_s[...] = jnp.zeros_like(r.sum_s)
    for copy in kept:
        copy.wait()
    arrived()

    def first(rows):
        normed, inv_std = standard(r.y3_s[rows, :])
        value = norm_back(r.bnd_s[half, rows, :].astype(F32), normed, inv_std, r.gains[1:2, :], r.sum_s, 1)
        r.dy_s[rows, :] = value
        r.df_s[rows, :] = value.astype(BF)

    by_rows(count, first)
    df = cp.store(r.df_s, r.df.at[own])
    shrink(r.df_s, r.w2_s, r.slo_s, r.hid_s)
    cp.store(r.hid_s, r.du.at[own])
    r.mid_s[...] = r.dy_s[...] + nt(r.hid_s[...], r.w1_s[...])
    cp.settle(df)

    def second(rows):
        normed, inv_std = standard(r.y1_s[rows, :])
        value = norm_back(r.mid_s[rows, :], normed, inv_std, r.gains[0:1, :], r.sum_s, 0)
        r.dy_s[rows, :] = value
        r.df_s[rows, :] = value.astype(BF)

    by_rows(count, second)
    cp.store(r.df_s, r.da.at[own])
    cp.store(r.sum_s, r.sums.at[half])
    r.att_s[...] = nt(r.df_s[...], r.wo_s[...]).astype(BF)
    self_attend_back(r.qkv_s, r.probs_s, r.att_s, r.dqkv_s, groups, span, model // HEADS)
    cp.store(r.dqkv_s, r.dqkv.at[own])
    r.pre_s[...] = r.dy_s[...] + nt(r.dqkv_s[...], r.wqkv_s[...])
    cp.store(r.pre_s, r.ig.at[own])
    cp.finish()


def join(r, cp, half, span, length, patches, gets, back, arrived, send):
    count, model = r.mid_s.shape
    head_dim = model // HEADS
    own = pl.ds(half * count, count)
    row_count = count // length
    groups = count // span
    pictures = pl.ds(half * row_count, row_count)
    g_cot = cp.load(r.cot.at[own], r.g_s)

    def ready(number):
        if half == 0:
            gets[number].wait()

    r.sum_s[...] = jnp.zeros_like(r.sum_s)
    ready(0)
    arrived()
    entry = r.bnd_s.at[half]
    cp.store(entry, r.entry.at[own])
    r.qkv_s[...] = nn(entry[...], r.wqkv_s[...]).astype(BF)
    self_attend(r.qkv_s, r.mask, r.probs_s, r.att_s, groups, half * groups, span, head_dim)
    att = cp.store(r.att_s, r.att.at[own])
    ready(1)
    r.y1_s[...] = entry[...].astype(F32) + nn(r.att_s[...], r.wo_s[...])

    def first(rows):
        value = standard(r.y1_s[rows, :])[0] * r.gains[0:1, :] + r.biases[0:1, :]
        r.mid_s[rows, :] = value
        r.midb_s[rows, :] = value.astype(BF)

    by_rows(count, first)
    cp.store(r.midb_s, r.midb.at[own])
    ready(4)
    r.qc_s[...] = nn(r.midb_s[...], r.wq_s[...]).astype(BF).astype(F32)
    cross_attend(r.qc_s, r.key_s, r.val_s, r.image, half * row_count, r.cprobs_s, r.cat_s, row_count, length, patches,
                 head_dim)
    r.catb_s[...] = r.cat_s[...].astype(BF)
    catt = cp.store(r.catb_s, r.catt.at[own])
    ready(5)
    r.y2_s[...] = r.mid_s[...] + nn(r.catb_s[...], r.wc_s[...])

    def second(rows):
        value = standard(r.y2_s[rows, :])[0] * r.cgain[...].reshape(1, model) + r.cbias[...].reshape(1, model)
        r.mid_s[rows, :] = value
        r.zb_s[rows, :] = value.astype(BF)

    by_rows(count, second)
    cp.store(r.zb_s, r.zb.at[own])
    ready(2)
    grow(r.zb_s, r.w1_s, r.pre_s, r.hid_s, r.slo_s)
    hidden = cp.store(r.hid_s, r.hidden.at[own])
    ready(3)
    r.y3_s[...] = r.mid_s[...] + nn(r.hid_s[...], r.w2_s[...])
    g_cot.wait()

    def third(rows):
        normed, inv_std = standard(r.y3_s[rows, :])
        r.lay_s[rows, :] = (normed * r.gains[1:2, :] + r.biases[1:2, :]).astype(BF)
        value = norm_back(r.g_s[rows, :].astype(F32), normed, inv_std, r.gains[1:2, :], r.sum_s, 1)
        r.dy_s[rows, :] = value
        r.df_s[rows, :] = value.astype(BF)

    by_rows(count, third)
    cp.store(r.lay_s, r.lay.at[own])
    df = cp.store(r.df_s, r.df.at[own])
    cp.settle(hidden)
    shrink(r.df_s, r.w2_s, r.slo_s, r.hid_s)
    du = cp.store(r.hid_s, r.du.at[own])
    r.mid_s[...] = r.dy_s[...] + nt(r.hid_s[...], r.w1_s[...])
    cp.settle(df)

    def fourth(rows):
        normed, inv_std = standard(r.y2_s[rows, :])
        value = norm_back(r.mid_s[rows, :], normed, inv_std, r.cgain[...].reshape(1, model), r.sum_s, 2)
        r.dy_s[rows, :] = value
        r.df_s[rows, :] = value.astype(BF)

    by_rows(count, fourth)
    dca = cp.store(r.df_s, r.dca.at[own])
    r.cat_s[...] = nt(r.df_s[...], r.wc_s[...]).astype(BF).astype(F32)
    cross_attend_back(r.qc_s, r.key_s, r.val_s, r.image, half * row_count, r.cprobs_s, r.cat_s, r.pre_s, r.dkey_s,
                      r.dval_s, row_count, length, head_dim)
    cp.store(r.dkey_s, r.dkey.at[pictures])
    cp.store(r.dval_s, r.dval.at[pictures])
    cp.settle(catt)
    r.catb_s[...] = r.pre_s[...].astype(BF)
    cp.store(r.catb_s, r.dq.at[own])
    r.mid_s[...] = r.dy_s[...] + nt(r.catb_s[...], r.wq_s[...])
    cp.settle(dca)

    def fifth(rows):
        normed, inv_std = standard(r.y1_s[rows, :])
        value = norm_back(r.mid_s[rows, :], normed, inv_std, r.gains[0:1, :], r.sum_s, 0)
        r.dy_s[rows, :] = value
        r.df_s[rows, :] = value.astype(BF)

    by_rows(count, fifth)
    cp.store(r.df_s, r.da.at[own])
    cp.store(r.sum_s, r.sums.at[half])
    cp.settle(att)
    r.att_s[...] = nt(r.df_s[...], r.wo_s[...]).astype(BF)
    self_attend_back(r.qkv_s, r.probs_s, r.att_s, r.dqkv_s, groups, span, head_dim)
    cp.store(r.dqkv_s, r.dqkv.at[own])
    r.mid_s[...] = r.dy_s[...] + nt(r.dqkv_s[...], r.wqkv_s[...])
    back[...] = r.mid_s[...].astype(BF)
    send()
    cp.store(r.mid_s, r.ig.at[own])
    cp.finish()


PIECES = 5


def project(r, cp, rows, patches, own, source, beside):
    total, width = r.pix_s.shape
    chunk = total // PIECES
    weight = cp.load(r.wimg, r.wimg_s)
    gets = [cp.load(r.images.at[pl.ds(c * chunk, chunk)], r.pix_s.at[pl.ds(c * chunk, chunk)]) for c in range(PIECES)]
    later = weights_in(r, cp) + [cp.load(r.wq, r.wq_s), cp.load(r.wc, r.wc_s)]

    def spread(source, target):
        target[:, patches - 1 : PAD, :] = jnp.zeros((rows, PAD - patches + 1, target.shape[2]), BF)
        for c in range(PIECES):
            if target is r.val_s:
                gets[c].wait()
            at = slice(c * chunk, c * chunk + chunk)
            got = nn(r.pix_s[at, :], source[...])
            for t in range(r.flat_s.shape[0]):
                r.flat_s[t, at, :] = got[:, t * LANES : t * LANES + LANES]
        for i in range(rows):
            for t in range(r.flat_s.shape[0]):
                target[i, :patches, t * LANES : t * LANES + LANES] = r.flat_s[
                    t, pl.ds(i, patches, stride=rows), :
                ].astype(BF)

    weight.wait()
    spread(r.wimg_s, r.val_s)
    expect(r, 0, r.wk_s.at[own], r.wk_s.at[own], source).wait_recv()
    greeted(2)
    swap = remote(r, 1, r.wk_s.at[own], r.wk_s.at[own], beside)
    swap.wait_recv()
    cp.store(r.wk_s, r.wk)
    spread(r.wk_s, r.key_s)
    swap.wait_send()
    return later


def relay_kernel(halves, span, length, patches, names, scopes, *refs):
    r = Refs(names, refs)
    section, place = lax.axis_index("section"), lax.axis_index("dp")
    core = lax.rem(place, jnp.int32(2))
    partner, beside = (1 - section, place), (section, place + 1 - 2 * core)
    half = r.wimg.shape[0] // 2
    own = pl.ds(pl.multiple_of(core * half, half), half)
    layer, first = ({n: pltpu.VMEM(*v) for n, v in scope.items()} for scope in scopes)

    def within(scope, body):
        def call(**own):
            for name, ref in own.items():
                setattr(r, name, ref)
            body()

        pl.run_scoped(call, **scope)

    @pl.when(section == 0)
    def _():
        cp = Copies(r.sems)
        greet(partner)
        greeted(1)

        def body():
            sends = [remote(r, 0, r.wimg.at[own], r.wk_s.at[own], partner)]
            for h in range(halves):
                out = (r.lay_s, r.back_s)[h]
                sends.append(
                    text_forward(r, cp, h, span, out, lambda: remote(r, 2 + h, out, r.bnd_s.at[h], partner))
                )
            for h in range(halves):
                text_back(
                    r, cp, h, span, lambda: expect(r, 2 + h, r.back_s, r.bnd_s.at[h], partner).wait_recv()
                )
            for copy in sends:
                copy.wait_send()

        within(layer, body)

    @pl.when(section == 1)
    def _():
        cp = Copies(r.sems)
        greet(partner)
        greet(beside)
        got = []
        within(first, lambda: got.extend(project(r, cp, r.key_s.shape[0], patches, own, partner, beside)))

        def body():
            for h in range(halves):
                back = (r.back_s, r.x_s)[h]
                join(
                    r, cp, h, span, length, patches, got, back,
                    lambda: expect(r, 2 + h, r.lay_s, r.bnd_s.at[h], partner).wait_recv(),
                    lambda: remote(r, 2 + h, back, r.bnd_s.at[h], partner),
                )

        within(layer, body)
        for h in range(halves):
            expect(r, 2 + h, (r.back_s, r.x_s)[h], r.bnd_s.at[h], partner).wait_send()


def expect(r, number, source, target, device):
    return pltpu.make_async_remote_copy(
        src_ref=source, dst_ref=target, send_sem=r.send_sems.at[number], recv_sem=r.recv_sems.at[number],
        device_id=device, device_id_type=pl.DeviceIdType.MESH,
    )


def relay(world, reads, writes, scratch, scopes, kernel, flops):
    smem, vmem, hbm = reads
    names = smem + vmem + hbm + list(writes) + list(scratch) + ["sems", "send_sems", "recv_sems"]
    got = pl.pallas_call(
        functools.partial(kernel, names, scopes),
        in_specs=[SMEM] * len(smem) + [VMEM] * len(vmem) + [ANY] * len(hbm),
        out_specs=[ANY] * len(writes),
        out_shape=list(writes.values()),
        scratch_shapes=[pltpu.VMEM(shape, dtype) for shape, dtype in scratch.values()]
        + [pltpu.SemaphoreType.DMA((100,)), pltpu.SemaphoreType.DMA((4,)), pltpu.SemaphoreType.DMA((4,))],
        compiler_params=pltpu.CompilerParams(vmem_limit_bytes=LIMIT, collective_id=2, has_side_effects=True),
        cost_estimate=pl.CostEstimate(flops=flops, bytes_accessed=40_000_000, transcendentals=0),
        name="relay",
    )(*[world[n] for n in smem + vmem + hbm])
    world.update(zip(writes, got))


TILE = 256
DEEP = 192


class Job:
    def __init__(self, fill, rows, cols, outs, kind=""):
        self.fill, self.rows, self.cols, self.outs, self.kind = fill, rows, cols, outs, kind
        self.depth = rows * (cols // TILE)


class Feed:
    def __init__(self, cp, lefts, rights):
        self.cp, self.lefts, self.rights = cp, lefts, rights
        self.plan, self.at, self.started = [], 0, 0

    def add(self, left, right):
        here = sum(1 for step in self.plan if step[1] is not None) + (right is not None) - 1
        self.plan.append((left, right, len(self.plan) % 2, here % 2))

    def start(self):
        if self.started < len(self.plan):
            left, right, a, b = self.plan[self.started]
            copies = [self.cp.load(left, self.lefts.at[a])]
            if right is not None:
                copies.append(self.cp.load(right, self.rights.at[b, :, pl.ds(0, right.shape[1])]))
            self.plan[self.started] = (copies, right, a, b)
            self.started += 1

    def take(self):
        if self.started == 0:
            self.start()
        self.start()
        copies, _, a, b = self.plan[self.at]
        for copy in copies:
            copy.wait()
        self.at += 1
        return self.lefts.at[a], self.rights.at[b]


def reduce_kernel(names, *refs):
    r = Refs(names, refs)
    section, place = lax.axis_index("section"), lax.axis_index("dp")
    core, y, z = place % 2, place // 2 % 2, place // 4
    partner = (1 - section, place)
    beside = place + 1 - 2 * core
    across = place + 2 - 4 * y
    along = [place + 4 * (1 - 2 * (z % 2)), place + 4 * (2 - 4 * (z // 2)), place + 4 * (3 - 2 * z)]
    far = [z + 1 - 2 * (z % 2), z + 2 - 4 * (z // 2), 3 - z]
    for other in [beside, across] + along:
        greet((section, other))
    tokens, model = r.df.shape
    part, high, tall = model // 16, r.hidden.shape[1] // 16, r.wk.shape[0] // 16
    total_rows, width = r.images.shape
    row_count = r.dkey.shape[0]
    patches = total_rows // row_count
    chunk = total_rows // PIECES
    vm = pltpu.VMEM

    def send(number, kind, source, target, other):
        copy = pltpu.make_async_remote_copy(
            src_ref=source, dst_ref=target, send_sem=r.send_sems.at[number, kind],
            recv_sem=r.recv_sems.at[number, kind], device_id=(section, other), device_id_type=pl.DeviceIdType.MESH,
        )
        copy.start()
        return copy

    def over(number, source, target):
        return pltpu.make_async_remote_copy(
            src_ref=source, dst_ref=target, send_sem=r.far_sends.at[number], recv_sem=r.far_recvs.at[number],
            device_id=partner, device_id_type=pl.DeviceIdType.MESH,
        )

    def lay_out(slot, got, rows, each=None):
        each = each or rows
        for k in range(got.shape[1] // TILE):
            piece = got[:, k * TILE : k * TILE + TILE].reshape(4, 2, 2, rows, TILE)
            r.tile[slot, :, :, :, k * each : k * each + rows, :] = piece

    def norm_rows(slot, rows, each):
        sums = jnp.sum(r.sums[0] + r.sums[1], 2).reshape(6, model)
        sums = jnp.concatenate([sums, jnp.zeros((10, model), F32)], 0)
        row = lax.broadcasted_iota(jnp.int32, (16, TILE), 0)
        for k in range(model // TILE):
            col = lax.broadcasted_iota(jnp.int32, (16, TILE), 1) + k * TILE
            owner = jnp.where(row < 4, col // part, col % (model // 2) // (part // 2))
            value = sums[:, k * TILE : k * TILE + TILE]
            at = pl.ds(k * each + rows, 16)
            for d in range(16):
                r.tile[slot, d // 4, d // 2 % 2, d % 2, at, :] = jnp.where(owner == d, value, 0.0).astype(BF)

    def product(feed, left, right, cols, rows, norms=False, order=False):
        feed.add(left, right.at[:, cols])

        def fill(slot):
            left_s, right_s = feed.take()
            value = left_s[...]
            if order:
                value = nn(value, r.order_s[...]).astype(BF)
            lay_out(slot, tn(value, right_s[:, : cols.size]).astype(BF), rows, rows + 16 if norms else rows)
            if norms:
                norm_rows(slot, rows, rows + 16)

        return fill

    def stacked(feed, left, right, cols, rows):
        for j in range(4):
            feed.add(left.at[:, pl.ds(j * 4 * rows, 4 * rows)], right.at[:, cols] if j == 0 else None)

        def fill(slot):
            for j in range(4):
                left_s, right_s = feed.take()
                got = tn(left_s[...], right_s[:, : cols.size]).astype(BF)
                r.tile[slot, j, :, :, :rows, :] = got.reshape(2, 2, rows, TILE)

        return fill

    def pictured(cp, flat):
        def fill(slot):
            def body(pix_s):
                cp.load(r.images, pix_s).wait()
                lay_out(slot, tn(pix_s[...], flat[...]).astype(BF), tall)

            pl.run_scoped(body, vm((total_rows, width), BF))

        return fill

    def run(cp, jobs, meet, tasks):
        cores, ys, zs = {}, {}, {}
        total = len(jobs)
        sent = []
        for i in range(total + 4):
            kind = jobs[i].kind if i < total else "none"
            if kind in ("", "give"):
                if i >= 3:
                    cores[i - 3].wait_send()
                slot, deep = i % 3, pl.ds(0, jobs[i].depth)
                jobs[i].fill(slot)
                if i == 0:
                    meet()
                cores[i] = send(i, 0, r.tile.at[slot, :, :, 1 - core, deep], r.core_in.at[i, :, :, deep], beside)
            for task in tasks.get(i, ()):
                task()
            if kind in ("", "give"):
                cores[i].wait_recv()

                @pl.loop(0, 4)
                def _(a):
                    for b in range(2):
                        r.core_in[i, a, b, deep, :] = r.core_in[i, a, b, deep, :] + r.tile[slot, a, b, core, deep, :]

            if i < total:
                deep = pl.ds(0, jobs[i].depth)
                if kind:
                    handed = over(marks[3], r.core_in.at[i, :, :, deep], r.core_in.at[handed_to, :, :, deep])
                if kind == "give":
                    handed.start()
                    sent.append(handed)
                else:
                    if kind == "take":
                        handed.wait_recv()
                    ys[i] = send(i, 1, r.core_in.at[i, :, 1 - y, deep], r.y_in.at[i, :, deep], across)
            j = i - 2
            if 0 <= j < total and jobs[j].kind != "give":
                ys[j].wait_recv()
                deep = pl.ds(0, jobs[j].depth)

                @pl.loop(0, 4)
                def _(a):
                    r.y_in[j, a, deep, :] = r.y_in[j, a, deep, :] + r.core_in[j, a, y, deep, :]

                for step in range(3):
                    zs[j, step] = send(
                        j, 2 + step, r.y_in.at[j, far[step], deep], r.z_in.at[j, step, deep], along[step]
                    )
            j = i - 4
            if 0 <= j < total and jobs[j].kind != "give":
                for step in range(3):
                    zs[j, step].wait_recv()
                deep = pl.ds(0, jobs[j].depth)
                r.final[j, deep, :] = (
                    r.y_in[j, z, deep, :].astype(F32) + r.z_in[j, 0, deep, :].astype(F32)
                ) + (r.z_in[j, 1, deep, :].astype(F32) + r.z_in[j, 2, deep, :].astype(F32))
                each = jobs[j].rows
                for k in range(jobs[j].cols // TILE):
                    for row, rows, target, first, number in jobs[j].outs:
                        source = r.final.at[j, pl.ds(k * each + row, rows)]
                        target = target.at[:, pl.ds(first + k * TILE, TILE)]
                        if number is None:
                            cp.store(source, target)
                        else:
                            sent.append(over(number + k, source, target))
                            sent[-1].start()
        for i in range(total):
            if i >= total - 3 and i in cores or i + 3 < total and i + 3 not in cores:
                cores[i].wait_send()
            if i in ys:
                ys[i].wait_send()
                for step in range(3):
                    zs[i, step].wait_send()
        for copy in sent:
            copy.wait_send()
        cp.finish()

    def ffn_jobs(feed):
        jobs = []
        for at in range(0, model, TILE):
            jobs.append(Job(stacked(feed, r.hidden, r.df, pl.ds(at, TILE), high), high, TILE, [(0, high, r.down, at, None)]))
        wide = DEEP // part * TILE
        for at in range(0, r.hidden.shape[1], wide):
            jobs.append(Job(product(feed, r.zb, r.du, pl.ds(at, wide), part), part, wide, [(0, part, r.up, at, None)]))
        return jobs

    def self_jobs(feed, norms):
        jobs = []
        for at in range(0, 3 * model, model):
            jobs.append(Job(product(feed, r.entry, r.dqkv, pl.ds(at, model), part), part, model,
                            [(0, part, r.qkv, at, None)]))
        outs = [(0, part, r.out, 0, None)] + ([(part, 16, r.norms, 0, None)] if norms else [])
        jobs.append(Job(product(feed, r.att, r.da, pl.ds(0, model), part, norms), part + 16 * norms, model, outs))
        return jobs

    parcels, handed_to = model // TILE, 10
    marks = [PIECES + parcels * n for n in range(4)]

    @pl.when(section == 0)
    def _():
        cp = Copies(r.sems)

        def meet():
            greeted(6)
            greet(partner)

        def widen(c):
            over(c, r.far_s.at[c], r.far_s.at[c]).wait_recv()
            if c > 1:
                cp.settle(stores[c - 2])
            r.own_s[c % 2] = r.far_s[c].astype(F32)
            stores.append(cp.store(r.own_s.at[c % 2], r.image_grad.at[pl.ds(c * chunk, chunk)]))

        feed = Feed(cp, r.left_s, r.right_s)
        jobs, stores = ffn_jobs(feed) + self_jobs(feed, True), []
        jobs.append(Job(None, tall, model, [(0, tall, r.wide, 0, None)], "take"))
        last = len(jobs) + 3
        run(cp, jobs, meet, {last - PIECES + c: [functools.partial(widen, c)] for c in range(PIECES)})
        for first, rows, target in ((marks[0], part // 2, r.cross_q), (marks[1], part // 2, r.cross_o),
                                    (marks[2], 16, r.far_norms)):
            for k in range(parcels):
                piece = target.at[:, pl.ds(k * TILE, TILE)]
                over(first + k, r.final.at[0, pl.ds(0, rows)], piece).wait_recv()

    @pl.when(section == 1)
    def _():
        cp = Copies(r.sems)
        feed = Feed(cp, r.left_s, r.right_s)
        first = ffn_jobs(feed)

        def meet():
            greeted(5)
            greet(partner)

        def flatten(source, flat, weight, weight_s):
            def body(grad_s, flat_s):
                copies = [cp.load(source, grad_s), cp.load(weight, weight_s)]
                if weight is r.wk:
                    copies.append(cp.load(r.order, r.order_s))
                for copy in copies:
                    copy.wait()
                for t in range(model // LANES):
                    lanes_at = slice(t * LANES, t * LANES + LANES)
                    for i in range(row_count):
                        flat_s[t % 2, pl.ds(i, patches, stride=row_count), :] = grad_s[
                            r.row_of[i], :patches, lanes_at
                        ].astype(F32)
                    flat[:, lanes_at] = flat_s[t % 2].astype(BF)

            pl.run_scoped(body, vm(r.dkey.shape, BF), vm((2, total_rows, LANES), F32))

        def pixel_grad(c):
            if c > 1:
                cp.settle(stores[c - 2])
            at, half = slice(c * chunk, c * chunk + chunk), width // 2
            r.far_s[c] = (nt(r.fk_s[at, :], r.wk_s[:half, :]) + nt(r.fv_s[at, :], r.wimg_s[:half, :])).astype(BF)
            if c == 0:
                greeted(1)
            over(c, r.far_s.at[c], r.far_s.at[c]).start()
            r.own_s[c % 2] = nt(r.fk_s[at, :], r.wk_s[half:, :]) + nt(r.fv_s[at, :], r.wimg_s[half:, :])
            stores.append(cp.store(r.own_s.at[c % 2], r.image_grad.at[pl.ds(c * chunk, chunk)]))

        stores = []
        own = part // 2
        joint = [
            Job(product(feed, r.dq, r.midb, pl.ds(0, model), part, False, True), part, model,
                [(0, own, r.cross_q, 0, marks[0]), (own, own, r.cross_q, 0, None)]),
            Job(pictured(cp, r.fk_s), tall, model, [], "give"),
            Job(product(feed, r.dca, r.catt, pl.ds(0, model), part, True, True), part + 16, model,
                [(0, own, r.cross_o, 0, marks[1]), (own, own, r.cross_o, 0, None), (part, 16, r.norms, 0, None),
                 (part, 16, r.far_norms, 0, marks[2])]),
            Job(pictured(cp, r.fv_s), tall, model, [(0, tall, r.wide, 0, None)]),
        ]
        tasks = {1: [lambda: flatten(r.dkey, r.fk_s, r.wk, r.wk_s)], 2: [lambda: flatten(r.dval, r.fv_s, r.wimg, r.wimg_s)]}
        for c, at in enumerate((4, 5, 6, 8, 10)):
            tasks[at] = [functools.partial(pixel_grad, c)]
        run(cp, first + joint + self_jobs(feed, False), meet, tasks)
        for c in range(PIECES):
            over(c, r.far_s.at[c], r.far_s.at[c]).wait_send()


def reduce_all(world, dp):
    tokens, model = world["df"].shape
    part, tall = model // dp, world["wk"].shape[0] // dp
    hidden, total_rows, width = world["hidden"].shape[1], world["images"].shape[0], world["images"].shape[1]
    jobs = 14
    chunk = total_rows // PIECES
    writes = dict(
        down=(hidden // dp, model), up=(part, hidden), qkv=(part, 3 * model), out=(part, model), norms=(16, model),
        far_norms=(16, model), wide=(tall, model), cross_q=(part // 2, model), cross_o=(part // 2, model),
        image_grad=(total_rows, width // 2),
    )
    hbm = ["hidden", "df", "zb", "du", "att", "da", "entry", "dqkv", "dq", "midb", "dca", "catt", "images", "dkey",
           "dval", "wk", "wimg", "order"]
    vm = pltpu.VMEM
    scratch = dict(
        tile=vm((3, 4, 2, 2, DEEP, TILE), BF), core_in=vm((jobs, 4, 2, DEEP, TILE), BF),
        y_in=vm((jobs, 4, DEEP, TILE), BF), z_in=vm((jobs, 3, DEEP, TILE), BF), final=vm((jobs, DEEP, TILE), F32),
        left_s=vm((2, tokens, model), BF), right_s=vm((2, tokens, hidden // 3), BF), order_s=vm((model, model), BF),
        fk_s=vm((total_rows, model), BF), fv_s=vm((total_rows, model), BF), wk_s=vm((width, model), BF),
        wimg_s=vm((width, model), BF), far_s=vm((PIECES, chunk, width // 2), BF), own_s=vm((2, chunk, width // 2), F32),
        sems=pltpu.SemaphoreType.DMA((128,)), send_sems=pltpu.SemaphoreType.DMA((jobs, 5)),
        recv_sems=pltpu.SemaphoreType.DMA((jobs, 5)),
        far_sends=pltpu.SemaphoreType.DMA((PIECES + 4 * (model // TILE),)),
        far_recvs=pltpu.SemaphoreType.DMA((PIECES + 4 * (model // TILE),)),
    )
    names = ["row_of", "sums"] + hbm + list(writes) + list(scratch)
    got = pl.pallas_call(
        functools.partial(reduce_kernel, names),
        in_specs=[SMEM, VMEM] + [ANY] * len(hbm),
        out_specs=[ANY] * len(writes),
        out_shape=[jax.ShapeDtypeStruct(shape, F32) for shape in writes.values()],
        scratch_shapes=list(scratch.values()),
        compiler_params=pltpu.CompilerParams(vmem_limit_bytes=LIMIT, collective_id=1, has_side_effects=True),
        cost_estimate=pl.CostEstimate(flops=20_000_000_000, bytes_accessed=40_000_000, transcendentals=0),
        name="reduce_all",
    )(world["row_of"], world["sums"], *[world[n] for n in hbm])
    return dict(zip(writes, got))


def reduce_plain(world, dp):
    model, width = world["df"].shape[1], world["images"].shape[1]
    is_text = lax.axis_index("section") == 0
    place = lax.axis_index("dp")

    def total(value):
        return lax.psum_scatter(value, "dp", scatter_dimension=0, tiled=True).astype(F32)

    def by_owner(value):
        own = value.reshape(2, dp, model // (2 * dp), model)
        return jnp.swapaxes(own, 0, 1).reshape(model, model)

    def grad(left, right):
        return total(tn(world[left], world[right]).astype(BF))

    def flat(value):
        value = value[world["row_of"], : world["images"].shape[0] // value.shape[0]]
        return jnp.swapaxes(value, 0, 1).reshape(-1, model)

    def over(value):
        return lax.ppermute(value, "section", [(1, 0)])

    dkey, dval = flat(world["dkey"]), flat(world["dval"])
    pixels = nt(dkey, world["wk"]) + nt(dval, world["wimg"])
    far = over(pixels[:, : width // 2].astype(BF)).astype(F32)
    wide_k, wide_v = (total(tn(world["images"], g).astype(BF)) for g in (dkey, dval))
    cross_q, cross_o = (
        total(by_owner(tn(world[a], world[b]).astype(BF))) for a, b in (("dq", "midb"), ("dca", "catt"))
    )
    own = cross_q.shape[0] // 2
    norms = lax.psum(jnp.sum(world["sums"], (0, 3)).reshape(6, model).at[4:].multiply(jnp.where(is_text, 0.0, 1.0)), "dp")
    del place
    return dict(
        down=grad("hidden", "df"), up=grad("zb", "du"), qkv=grad("entry", "dqkv"), out=grad("att", "da"), norms=norms,
        far_norms=over(norms), wide=jnp.where(is_text, over(wide_k), wide_v),
        cross_q=jnp.where(is_text, over(cross_q[:own]), cross_q[own:]),
        cross_o=jnp.where(is_text, over(cross_o[:own]), cross_o[own:]),
        image_grad=jnp.where(is_text, far, pixels[:, width // 2 :]),
    )


def per_device(
    text_in, cotangent, images, segment_ids, row_image, self_qkv, self_out, ffn_up, ffn_down,
    norm_gain, norm_bias, image_kv, cross_query, cross_out, cross_gain, cross_bias,
):
    tokens, model = text_in.shape
    row_total, length = segment_ids.shape
    patches, width = images.shape[1:]
    hidden_width = ffn_up.shape[2]
    block_rows = row_image.shape[1]
    head_dim = model // HEADS
    pairs = HEADS // 2
    count = tokens // HALVES
    half_rows = row_total // HALVES
    span = 2 * length
    dp = lax.axis_size("dp")
    section = lax.axis_index("section")
    is_text = section == 0
    flag = section.astype(jnp.int32).reshape(1)
    place = lax.axis_index("dp")
    wqkv, wo, w1, w2 = self_qkv[0], self_out[0], ffn_up[0], ffn_down[0]
    gains, biases = norm_gain[0], norm_bias[0]
    cgain, cbias = cross_gain, cross_bias

    marks = (segment_ids + segment_ids.shape[1] * (jnp.arange(row_total, dtype=jnp.int32) % 2)[:, None]).reshape(-1, span)
    mask = jnp.where(marks[:, :, None] == jnp.tile(marks, (1, 2))[:, None, :], 0.0, MASKED).astype(F32)
    in_block = jnp.arange(row_total, dtype=jnp.int32) // block_rows * block_rows
    image = row_image.reshape(-1) + in_block
    slots = jnp.arange(block_rows, dtype=jnp.int32)
    row_of = jnp.sum(jnp.where(row_image[:, :, None] == slots, slots[:, None], 0), 1).reshape(-1) + in_block

    def shape(*dims, dtype=BF):
        return jax.ShapeDtypeStruct(dims, dtype)

    flat_rows = row_total * patches
    pixels = jnp.swapaxes(images, 0, 1).reshape(flat_rows, width)
    probs_shape = (count // span * pairs, span, 2 * span)
    world = dict(
        image=image, row_of=row_of, gains=gains, biases=biases, cgain=cgain, cbias=cbias, mask=mask, text=text_in,
        cot=cotangent, images=pixels, wqkv=wqkv, wo=wo, w1=w1, w2=w2, wq=cross_query, wc=cross_out, wimg=image_kv,
    )
    small_f, small_b = ((count, model), F32), ((count, model), BF)
    tall_b, wide_b = ((count, hidden_width), BF), ((count, 3 * model), BF)
    picture_b, pictures_b = ((half_rows, PAD, model), BF), ((row_total, PAD, model), BF)
    scratch = dict(
        wqkv_s=(wqkv.shape, BF), wo_s=(wo.shape, BF), w1_s=(w1.shape, BF), w2_s=(w2.shape, BF),
        wq_s=(cross_query.shape, BF), wc_s=(cross_out.shape, BF), wimg_s=(image_kv.shape, BF),
        wk_s=(image_kv.shape, BF), key_s=pictures_b, val_s=pictures_b, bnd_s=((HALVES, count, model), BF),
        x_s=small_b, back_s=small_b,
    )
    layer_s = dict(
        qkv_s=wide_b, probs_s=(probs_shape, BF), att_s=small_b, y1_s=small_f, mid_s=small_f, zb_s=small_b,
        pre_s=small_f, hid_s=tall_b, slo_s=tall_b, y3_s=small_f, lay_s=small_b, g_s=small_b, midb_s=small_b,
        qc_s=small_f, cprobs_s=((half_rows * pairs, PAD, 2 * length), BF), cat_s=small_f, catb_s=small_b,
        y2_s=small_f, df_s=small_b, dy_s=small_f, dkey_s=picture_b, dval_s=picture_b, dqkv_s=wide_b,
        sum_s=((3, 2, 8, model), F32),
    )
    flat_s = ((model // LANES, flat_rows, LANES), F32)
    first_s = dict(pix_s=((flat_rows, width), BF), flat_s=flat_s)
    tokens_b = shape(tokens, model)
    writes = dict(
        lay=tokens_b, zb=tokens_b, hidden=shape(tokens, hidden_width), att=tokens_b, entry=tokens_b,
        ig=shape(tokens, model, dtype=F32), df=tokens_b, du=shape(tokens, hidden_width), da=tokens_b,
        dqkv=shape(tokens, 3 * model), sums=shape(HALVES, 3, 2, 8, model, dtype=F32), midb=tokens_b, dq=tokens_b,
        catt=tokens_b, dca=tokens_b, dkey=shape(row_total, PAD, model), dval=shape(row_total, PAD, model),
        wk=shape(width, model), y1=shape(HALVES, count, model, dtype=F32),
        y3=shape(HALVES, count, model, dtype=F32), qkv=shape(HALVES, count, 3 * model),
        probs=shape(HALVES, *probs_shape), slope=shape(HALVES, count, hidden_width),
    )
    linear = model * 3 * model + model * model + 2 * model * hidden_width
    reads = (
        ["image"], ["gains", "biases", "mask", "cgain", "cbias"],
        ["text", "cot", "images", "wqkv", "wo", "w1", "w2", "wq", "wc", "wimg"],
    )
    relay(
        world, reads, writes, scratch, (layer_s, first_s),
        functools.partial(relay_kernel, HALVES, span, length, patches), 8 * count * (linear + 2 * model * model),
    )
    new, own = np.arange(model), model // (2 * dp)
    source = new % (2 * own) // own * (model // 2) + new // (2 * own) * own + new % own
    world["order"] = jnp.asarray(new[:, None] == source, BF)
    world["row_of"] = row_of
    got = reduce_all(world, dp) if dp == 16 else reduce_plain(world, dp)
    out_rows = model // dp
    cross_rows = out_rows // lax.axis_size("section")
    norm_part = lax.dynamic_slice_in_dim(got["norms"][:4], place * out_rows, out_rows, 1).reshape(2, 2, out_rows)
    cross_part = jnp.where(is_text, got["far_norms"][4:6], got["norms"][4:6])
    cross_part = lax.dynamic_slice_in_dim(cross_part, (section * dp + place) * cross_rows, cross_rows, 1)
    image_grad = jnp.swapaxes(got["image_grad"].reshape(patches, row_total, width // 2), 0, 1)
    return (
        world["lay"][None], world["ig"][None], image_grad, got["qkv"][None], got["out"][None], got["up"][None],
        got["down"][None], norm_part[:, 0][None], norm_part[:, 1][None], got["wide"], got["cross_q"].T,
        got["cross_o"].T, cross_part[0], cross_part[1],
    )


def solution(mesh):
    return jax.shard_map(
        per_device,
        mesh=mesh,
        in_specs=(
            P("dp", None),
            P("dp", None),
            P("dp", None, None),
            P("dp", None),
            P("dp", None),
            P("section", None, None),
            P("section", None, None),
            P("section", None, None),
            P("section", None, None),
            P("section", None, None),
            P("section", None, None),
            P(None, "section"),
            P(),
            P(),
            P(),
            P(),
        ),
        out_specs=(
            P("section", "dp", None),
            P("section", "dp", None),
            P("dp", None, "section"),
            P("section", "dp", None),
            P("section", "dp", None),
            P("section", "dp", None),
            P("section", "dp", None),
            P("section", None, "dp"),
            P("section", None, "dp"),
            P("dp", "section"),
            P(None, ("section", "dp")),
            P(None, ("section", "dp")),
            P(("section", "dp")),
            P(("section", "dp")),
        ),
        check_vma=False,
    )
```

```python
import functools
import math

import jax
import jax.numpy as jnp
import numpy as np
from jax import lax
from jax.experimental import pallas as pl
from jax.experimental.pallas import tpu as pltpu
from jax.sharding import PartitionSpec as P

HEADS = 12
EPSILON = 1e-06
MASKED = -1e30
BF = jnp.bfloat16
F32 = jnp.float32
PAD = 160
LANES = 128
HALVES = 2
CHUNK = 32
LIMIT = 60 * 1024 * 1024
ANY = pl.BlockSpec(memory_space=pl.ANY)
SMEM = pl.BlockSpec(memory_space=pltpu.SMEM)
VMEM = pl.BlockSpec(memory_space=pltpu.VMEM)


def nn(left, right):
    return lax.dot_general(left, right, (((1,), (0,)), ((), ())), preferred_element_type=F32)


def nt(left, right):
    return lax.dot_general(left, right, (((1,), (1,)), ((), ())), preferred_element_type=F32)


def tn(left, right):
    return lax.dot_general(left, right, (((0,), (0,)), ((), ())), preferred_element_type=F32)


class Copy:
    def __init__(self, source, target, sems, number):
        self.parts = source, target, sems, number

    def make(self):
        source, target, sems, number = self.parts
        return pltpu.make_async_copy(source, target, sems.at[number])

    def wait(self):
        self.make().wait()


class Copies:
    def __init__(self, sems):
        self.sems, self.used, self.open = sems, 0, []

    def load(self, source, target):
        copy = Copy(source, target, self.sems, self.used)
        self.used += 1
        copy.make().start()
        return copy

    def store(self, source, target):
        copy = self.load(source, target)
        self.open.append(copy)
        return copy

    def settle(self, copy):
        self.open = [other for other in self.open if other is not copy]
        copy.wait()

    def finish(self):
        for copy in self.open:
            copy.wait()
        self.open = []


def by_rows(count, body):
    for at in range(0, count, CHUNK):
        body(pl.ds(at, CHUNK))


def standard(summed):
    centred = summed - jnp.mean(summed, -1, keepdims=True)
    inv_std = lax.rsqrt(jnp.mean(centred * centred, -1, keepdims=True) + EPSILON)
    return centred * inv_std, inv_std


def fold(value):
    return jnp.sum(value.reshape(value.shape[0] // 8, 8, value.shape[1]), 0)


def norm_back(grad_out, normed, inv_std, gain, sums, slot):
    sums[slot, 0] += fold(grad_out * normed)
    sums[slot, 1] += fold(grad_out)
    grad_normed = grad_out * gain
    return inv_std * (
        grad_normed
        - jnp.mean(grad_normed, -1, keepdims=True)
        - normed * jnp.mean(grad_normed * normed, -1, keepdims=True)
    )


def gelu_both(preact):
    size = jnp.abs(preact)
    bell = jnp.exp(-0.5 * preact * preact)
    t = 1.0 / (1.0 + (0.3275911 * math.sqrt(0.5)) * size)
    series = t * (
        0.5 * 0.254829592
        + t * (-0.5 * 0.284496736 + t * (0.5 * 1.421413741 + t * (-0.5 * 1.453152027 + t * (0.5 * 1.061405429))))
    )
    tail = series * bell
    below = jnp.where(preact >= 0.0, 1.0 - tail, tail)
    return preact * below, below + preact * bell * (1.0 / math.sqrt(2.0 * math.pi))


def head_lanes(width, head_dim):
    lane = lax.broadcasted_iota(jnp.int32, (1, width), 1)
    first = jnp.where(lane < head_dim, 1.0, 0.0)
    return first, 1.0 - first


def lanes(value, low, high):
    return jnp.concatenate([value * low, value * high], 0)


def weights_of(scores):
    grown = [jnp.exp(s - jnp.max(s, 0, keepdims=True)) for s in scores]
    return [(e * (1.0 / jnp.sum(e, 0, keepdims=True))).astype(BF) for e in grown]


def scores_back(weights_b, grad_w):
    weights = [w.astype(F32) for w in weights_b]
    return [(w * (g - jnp.sum(g * w, 0, keepdims=True))).astype(BF) for w, g in zip(weights, grad_w)]


def self_attend(qkv, mask, probs, att, groups, first_group, span, head_dim):
    width = 2 * head_dim
    model = att.shape[1]
    pairs = model // width
    low, high = head_lanes(width, head_dim)
    scale = 1.0 / math.sqrt(head_dim)
    low_b, high_b = (low * scale).astype(BF), (high * scale).astype(BF)
    at = [p * width for p in range(pairs)]

    @pl.loop(0, groups, unroll=4)
    def _(g):
        rows = pl.ds(pl.multiple_of(g * span, span), span)
        bias = mask[first_group + g]
        both = [lanes(qkv[rows, c : c + width], low_b, high_b) for c in at]
        scores = [nt(qkv[rows, model + c : model + c + width], b) + bias for c, b in zip(at, both)]
        weights = weights_of(scores)
        for p, c in enumerate(at):
            probs[g * pairs + p] = weights[p]
            out = tn(weights[p], qkv[rows, 2 * model + c : 2 * model + c + width])
            att[rows, c : c + width] = (out[:span] * low + out[span:] * high).astype(BF)


def self_attend_back(qkv, probs, grad_att, grad_qkv, groups, span, head_dim):
    width = 2 * head_dim
    model = grad_att.shape[1]
    pairs = model // width
    low, high = head_lanes(width, head_dim)
    scale = 1.0 / math.sqrt(head_dim)
    low_s, high_s = low * scale, high * scale
    scaled, plain = (low_s.astype(BF), high_s.astype(BF)), (low.astype(BF), high.astype(BF))
    at = [p * width for p in range(pairs)]

    @pl.loop(0, groups, unroll=4)
    def _(g):
        rows = pl.ds(pl.multiple_of(g * span, span), span)
        both_g = [lanes(grad_att[rows, c : c + width], *plain) for c in at]
        weights = [probs[g * pairs + p] for p in range(pairs)]
        grad_w = [nt(qkv[rows, 2 * model + c : 2 * model + c + width], b) for c, b in zip(at, both_g)]
        grad_s = scores_back(weights, grad_w)
        for p, c in enumerate(at):
            out = tn(grad_s[p], qkv[rows, model + c : model + c + width])
            both_q = lanes(qkv[rows, c : c + width], *scaled)
            grad_qkv[rows, c : c + width] = (out[:span] * low_s + out[span:] * high_s).astype(BF)
            grad_qkv[rows, model + c : model + c + width] = nn(grad_s[p], both_q).astype(BF)
            grad_qkv[rows, 2 * model + c : 2 * model + c + width] = nn(weights[p], both_g[p]).astype(BF)


def cross_attend(queries, keys, vals, image, first_row, probs, out, row_count, length, patches, head_dim):
    width = 2 * head_dim
    pairs = queries.shape[1] // width
    low, high = head_lanes(width, head_dim)
    scale = 1.0 / math.sqrt(head_dim)
    low_s, high_s = low * scale, high * scale
    shown = lax.broadcasted_iota(jnp.int32, (keys.shape[1], 2 * length), 0) < patches
    at = [slice(p * width, p * width + width) for p in range(pairs)]

    @pl.loop(0, row_count, unroll=4)
    def _(r):
        rows = pl.ds(pl.multiple_of(r * length, 8), length)
        picked = image[first_row + r]
        both = [lanes(queries[rows, c], low_s, high_s).astype(BF) for c in at]
        scores = [jnp.where(shown, nt(keys[picked, :, c], b), MASKED) for c, b in zip(at, both)]
        weights = weights_of(scores)
        for p, c in enumerate(at):
            probs[r * pairs + p] = weights[p]
            got = tn(weights[p], vals[picked, :, c])
            out[rows, c] = got[:length] * low + got[length:] * high


def cross_attend_back(
    queries, keys, vals, image, first_row, probs, grad_att, grad_q, grad_k, grad_v, row_count, length, head_dim
):
    width = 2 * head_dim
    pairs = queries.shape[1] // width
    low, high = head_lanes(width, head_dim)
    scale = 1.0 / math.sqrt(head_dim)
    low_s, high_s = low * scale, high * scale
    at = [slice(p * width, p * width + width) for p in range(pairs)]

    @pl.loop(0, row_count, unroll=4)
    def _(r):
        rows = pl.ds(pl.multiple_of(r * length, 8), length)
        picked = image[first_row + r]
        both_g = [lanes(grad_att[rows, c], low, high).astype(BF) for c in at]
        weights = [probs[r * pairs + p] for p in range(pairs)]
        grad_w = [nt(vals[picked, :, c], b) for c, b in zip(at, both_g)]
        grad_s = scores_back(weights, grad_w)
        for p, c in enumerate(at):
            both_q = lanes(queries[rows, c], low_s, high_s).astype(BF)
            got = tn(grad_s[p], keys[picked, :, c])
            grad_q[rows, c] = got[:length] * low_s + got[length:] * high_s
            grad_k[r, :, c] = nn(grad_s[p], both_q).astype(BF)
            grad_v[r, :, c] = nn(weights[p], both_g[p]).astype(BF)


def grow(entry, w_up, preact, hidden, slope):
    tile = preact.shape[1]
    for j in range(hidden.shape[1] // tile):
        cols = slice(j * tile, j * tile + tile)
        preact[...] = nn(entry[...], w_up[:, cols])

        def body(rows):
            value, rise = gelu_both(preact[rows, :])
            hidden[rows, cols] = value.astype(BF)
            slope[rows, cols] = rise.astype(BF)

        by_rows(preact.shape[0], body)


def shrink(branch, w_down, slope, grad_pre):
    tile = branch.shape[1]
    for j in range(slope.shape[1] // tile):
        cols = slice(j * tile, j * tile + tile)
        grad_pre[:, cols] = (nt(branch[...], w_down[cols, :]) * slope[:, cols].astype(F32)).astype(BF)


class Refs:
    def __init__(self, names, refs):
        for name, ref in zip(names, refs):
            setattr(self, name, ref)


def remote(r, number, source, target, device):
    copy = pltpu.make_async_remote_copy(
        src_ref=source, dst_ref=target, send_sem=r.send_sems.at[number], recv_sem=r.recv_sems.at[number],
        device_id=device, device_id_type=pl.DeviceIdType.MESH,
    )
    copy.start()
    return copy


def greet(device):
    pl.semaphore_signal(
        pltpu.get_barrier_semaphore(), inc=1, device_id=device, device_id_type=pl.DeviceIdType.MESH
    )


def greeted(count):
    pl.semaphore_wait(pltpu.get_barrier_semaphore(), count)


def text_forward(r, cp, half, span, out, send):
    count = r.x_s.shape[0]
    own = pl.ds(half * count, count)
    groups = count // span
    text = cp.load(r.text.at[own], r.x_s)
    gets = weights_in(r, cp) if half == 0 else None
    text.wait()
    cp.store(r.x_s, r.entry.at[own])
    if half == 0:
        gets[0].wait()
    r.qkv_s[...] = nn(r.x_s[...], r.wqkv_s[...]).astype(BF)
    cp.store(r.qkv_s, r.qkv.at[half])
    self_attend(r.qkv_s, r.mask, r.probs_s, r.att_s, groups, half * groups, span, r.x_s.shape[1] // HEADS)
    cp.store(r.probs_s, r.probs.at[half])
    cp.store(r.att_s, r.att.at[own])
    if half == 0:
        gets[1].wait()
    r.y1_s[...] = r.x_s[...].astype(F32) + nn(r.att_s[...], r.wo_s[...])
    cp.store(r.y1_s, r.y1.at[half])

    def first(rows):
        value = standard(r.y1_s[rows, :])[0] * r.gains[0:1, :] + r.biases[0:1, :]
        r.mid_s[rows, :] = value
        r.zb_s[rows, :] = value.astype(BF)

    by_rows(count, first)
    cp.store(r.zb_s, r.zb.at[own])
    if half == 0:
        gets[2].wait()
    grow(r.zb_s, r.w1_s, r.pre_s, r.hid_s, r.slo_s)
    cp.store(r.hid_s, r.hidden.at[own])
    cp.store(r.slo_s, r.slope.at[half])
    if half == 0:
        gets[3].wait()
    r.y3_s[...] = r.mid_s[...] + nn(r.hid_s[...], r.w2_s[...])
    cp.store(r.y3_s, r.y3.at[half])

    def second(rows):
        out[rows, :] = (standard(r.y3_s[rows, :])[0] * r.gains[1:2, :] + r.biases[1:2, :]).astype(BF)

    by_rows(count, second)
    sent = send()
    cp.store(out, r.lay.at[own])
    cp.finish()
    return sent


def weights_in(r, cp):
    return [cp.load(a, b) for a, b in ((r.wqkv, r.wqkv_s), (r.wo, r.wo_s), (r.w1, r.w1_s), (r.w2, r.w2_s))]


def text_back(r, cp, half, span, arrived):
    count, model = r.y1_s.shape
    own = pl.ds(half * count, count)
    groups = count // span
    kept = [
        cp.load(a.at[half], b)
        for a, b in ((r.y3, r.y3_s), (r.slope, r.slo_s), (r.y1, r.y1_s), (r.qkv, r.qkv_s), (r.probs, r.probs_s))
    ]
    r.sum_s[...] = jnp.zeros_like(r.sum_s)
    for copy in kept:
        copy.wait()
    arrived()

    def first(rows):
        normed, inv_std = standard(r.y3_s[rows, :])
        value = norm_back(r.bnd_s[half, rows, :].astype(F32), normed, inv_std, r.gains[1:2, :], r.sum_s, 1)
        r.dy_s[rows, :] = value
        r.df_s[rows, :] = value.astype(BF)

    by_rows(count, first)
    df = cp.store(r.df_s, r.df.at[own])
    shrink(r.df_s, r.w2_s, r.slo_s, r.hid_s)
    cp.store(r.hid_s, r.du.at[own])
    r.mid_s[...] = r.dy_s[...] + nt(r.hid_s[...], r.w1_s[...])
    cp.settle(df)

    def second(rows):
        normed, inv_std = standard(r.y1_s[rows, :])
        value = norm_back(r.mid_s[rows, :], normed, inv_std, r.gains[0:1, :], r.sum_s, 0)
        r.dy_s[rows, :] = value
        r.df_s[rows, :] = value.astype(BF)

    by_rows(count, second)
    cp.store(r.df_s, r.da.at[own])
    cp.store(r.sum_s, r.sums.at[half])
    r.att_s[...] = nt(r.df_s[...], r.wo_s[...]).astype(BF)
    self_attend_back(r.qkv_s, r.probs_s, r.att_s, r.dqkv_s, groups, span, model // HEADS)
    cp.store(r.dqkv_s, r.dqkv.at[own])
    r.pre_s[...] = r.dy_s[...] + nt(r.dqkv_s[...], r.wqkv_s[...])
    cp.store(r.pre_s, r.ig.at[own])
    cp.finish()


def join(r, cp, half, span, length, patches, gets, back, arrived, send):
    count, model = r.mid_s.shape
    head_dim = model // HEADS
    own = pl.ds(half * count, count)
    row_count = count // length
    groups = count // span
    pictures = pl.ds(half * row_count, row_count)
    g_cot = cp.load(r.cot.at[own], r.g_s)

    def ready(number):
        if half == 0:
            gets[number].wait()

    r.sum_s[...] = jnp.zeros_like(r.sum_s)
    ready(0)
    arrived()
    entry = r.bnd_s.at[half]
    cp.store(entry, r.entry.at[own])
    r.qkv_s[...] = nn(entry[...], r.wqkv_s[...]).astype(BF)
    self_attend(r.qkv_s, r.mask, r.probs_s, r.att_s, groups, half * groups, span, head_dim)
    att = cp.store(r.att_s, r.att.at[own])
    ready(1)
    r.y1_s[...] = entry[...].astype(F32) + nn(r.att_s[...], r.wo_s[...])

    def first(rows):
        value = standard(r.y1_s[rows, :])[0] * r.gains[0:1, :] + r.biases[0:1, :]
        r.mid_s[rows, :] = value
        r.midb_s[rows, :] = value.astype(BF)

    by_rows(count, first)
    cp.store(r.midb_s, r.midb.at[own])
    ready(4)
    r.qc_s[...] = nn(r.midb_s[...], r.wq_s[...]).astype(BF).astype(F32)
    cross_attend(r.qc_s, r.key_s, r.val_s, r.image, half * row_count, r.cprobs_s, r.cat_s, row_count, length, patches,
                 head_dim)
    r.catb_s[...] = r.cat_s[...].astype(BF)
    catt = cp.store(r.catb_s, r.catt.at[own])
    ready(5)
    r.y2_s[...] = r.mid_s[...] + nn(r.catb_s[...], r.wc_s[...])

    def second(rows):
        value = standard(r.y2_s[rows, :])[0] * r.cgain[...].reshape(1, model) + r.cbias[...].reshape(1, model)
        r.mid_s[rows, :] = value
        r.zb_s[rows, :] = value.astype(BF)

    by_rows(count, second)
    cp.store(r.zb_s, r.zb.at[own])
    ready(2)
    grow(r.zb_s, r.w1_s, r.pre_s, r.hid_s, r.slo_s)
    hidden = cp.store(r.hid_s, r.hidden.at[own])
    ready(3)
    r.y3_s[...] = r.mid_s[...] + nn(r.hid_s[...], r.w2_s[...])
    g_cot.wait()

    def third(rows):
        normed, inv_std = standard(r.y3_s[rows, :])
        r.lay_s[rows, :] = (normed * r.gains[1:2, :] + r.biases[1:2, :]).astype(BF)
        value = norm_back(r.g_s[rows, :].astype(F32), normed, inv_std, r.gains[1:2, :], r.sum_s, 1)
        r.dy_s[rows, :] = value
        r.df_s[rows, :] = value.astype(BF)

    by_rows(count, third)
    cp.store(r.lay_s, r.lay.at[own])
    df = cp.store(r.df_s, r.df.at[own])
    cp.settle(hidden)
    shrink(r.df_s, r.w2_s, r.slo_s, r.hid_s)
    du = cp.store(r.hid_s, r.du.at[own])
    r.mid_s[...] = r.dy_s[...] + nt(r.hid_s[...], r.w1_s[...])
    cp.settle(df)

    def fourth(rows):
        normed, inv_std = standard(r.y2_s[rows, :])
        value = norm_back(r.mid_s[rows, :], normed, inv_std, r.cgain[...].reshape(1, model), r.sum_s, 2)
        r.dy_s[rows, :] = value
        r.df_s[rows, :] = value.astype(BF)

    by_rows(count, fourth)
    dca = cp.store(r.df_s, r.dca.at[own])
    r.cat_s[...] = nt(r.df_s[...], r.wc_s[...]).astype(BF).astype(F32)
    cross_attend_back(r.qc_s, r.key_s, r.val_s, r.image, half * row_count, r.cprobs_s, r.cat_s, r.pre_s, r.dkey_s,
                      r.dval_s, row_count, length, head_dim)
    cp.store(r.dkey_s, r.dkey.at[pictures])
    cp.store(r.dval_s, r.dval.at[pictures])
    cp.settle(catt)
    r.catb_s[...] = r.pre_s[...].astype(BF)
    cp.store(r.catb_s, r.dq.at[own])
    r.mid_s[...] = r.dy_s[...] + nt(r.catb_s[...], r.wq_s[...])
    cp.settle(dca)

    def fifth(rows):
        normed, inv_std = standard(r.y1_s[rows, :])
        value = norm_back(r.mid_s[rows, :], normed, inv_std, r.gains[0:1, :], r.sum_s, 0)
        r.dy_s[rows, :] = value
        r.df_s[rows, :] = value.astype(BF)

    by_rows(count, fifth)
    cp.store(r.df_s, r.da.at[own])
    cp.store(r.sum_s, r.sums.at[half])
    cp.settle(att)
    r.att_s[...] = nt(r.df_s[...], r.wo_s[...]).astype(BF)
    self_attend_back(r.qkv_s, r.probs_s, r.att_s, r.dqkv_s, groups, span, head_dim)
    cp.store(r.dqkv_s, r.dqkv.at[own])
    r.mid_s[...] = r.dy_s[...] + nt(r.dqkv_s[...], r.wqkv_s[...])
    back[...] = r.mid_s[...].astype(BF)
    send()
    cp.store(r.mid_s, r.ig.at[own])
    cp.finish()


PIECES = 5


def project(r, cp, rows, patches, own, source, beside):
    total, width = r.pix_s.shape
    chunk = total // PIECES
    weight = cp.load(r.wimg, r.wimg_s)
    gets = [cp.load(r.images.at[pl.ds(c * chunk, chunk)], r.pix_s.at[pl.ds(c * chunk, chunk)]) for c in range(PIECES)]
    later = weights_in(r, cp) + [cp.load(r.wq, r.wq_s), cp.load(r.wc, r.wc_s)]

    def spread(source, target):
        target[:, patches - 1 : PAD, :] = jnp.zeros((rows, PAD - patches + 1, target.shape[2]), BF)
        for c in range(PIECES):
            if target is r.val_s:
                gets[c].wait()
            at = slice(c * chunk, c * chunk + chunk)
            got = nn(r.pix_s[at, :], source[...])
            for t in range(r.flat_s.shape[0]):
                r.flat_s[t, at, :] = got[:, t * LANES : t * LANES + LANES]
        for i in range(rows):
            for t in range(r.flat_s.shape[0]):
                target[i, :patches, t * LANES : t * LANES + LANES] = r.flat_s[
                    t, pl.ds(i, patches, stride=rows), :
                ].astype(BF)

    weight.wait()
    spread(r.wimg_s, r.val_s)
    expect(r, 0, r.wk_s.at[own], r.wk_s.at[own], source).wait_recv()
    greeted(2)
    swap = remote(r, 1, r.wk_s.at[own], r.wk_s.at[own], beside)
    swap.wait_recv()
    cp.store(r.wk_s, r.wk)
    spread(r.wk_s, r.key_s)
    swap.wait_send()
    return later


def relay_kernel(halves, span, length, patches, names, scopes, *refs):
    r = Refs(names, refs)
    section, place = lax.axis_index("section"), lax.axis_index("dp")
    core = lax.rem(place, jnp.int32(2))
    partner, beside = (1 - section, place), (section, place + 1 - 2 * core)
    half = r.wimg.shape[0] // 2
    own = pl.ds(pl.multiple_of(core * half, half), half)
    layer, first = ({n: pltpu.VMEM(*v) for n, v in scope.items()} for scope in scopes)

    def within(scope, body):
        def call(**own):
            for name, ref in own.items():
                setattr(r, name, ref)
            body()

        pl.run_scoped(call, **scope)

    @pl.when(section == 0)
    def _():
        cp = Copies(r.sems)
        greet(partner)
        greeted(1)

        def body():
            sends = [remote(r, 0, r.wimg.at[own], r.wk_s.at[own], partner)]
            for h in range(halves):
                out = (r.lay_s, r.back_s)[h]
                sends.append(
                    text_forward(r, cp, h, span, out, lambda: remote(r, 2 + h, out, r.bnd_s.at[h], partner))
                )
            for h in range(halves):
                text_back(
                    r, cp, h, span, lambda: expect(r, 2 + h, r.back_s, r.bnd_s.at[h], partner).wait_recv()
                )
            for copy in sends:
                copy.wait_send()

        within(layer, body)

    @pl.when(section == 1)
    def _():
        cp = Copies(r.sems)
        greet(partner)
        greet(beside)
        got = []
        within(first, lambda: got.extend(project(r, cp, r.key_s.shape[0], patches, own, partner, beside)))

        def body():
            for h in range(halves):
                back = (r.back_s, r.x_s)[h]
                join(
                    r, cp, h, span, length, patches, got, back,
                    lambda: expect(r, 2 + h, r.lay_s, r.bnd_s.at[h], partner).wait_recv(),
                    lambda: remote(r, 2 + h, back, r.bnd_s.at[h], partner),
                )

        within(layer, body)
        for h in range(halves):
            expect(r, 2 + h, (r.back_s, r.x_s)[h], r.bnd_s.at[h], partner).wait_send()


def expect(r, number, source, target, device):
    return pltpu.make_async_remote_copy(
        src_ref=source, dst_ref=target, send_sem=r.send_sems.at[number], recv_sem=r.recv_sems.at[number],
        device_id=device, device_id_type=pl.DeviceIdType.MESH,
    )


def relay(world, reads, writes, scratch, scopes, kernel, flops):
    smem, vmem, hbm = reads
    names = smem + vmem + hbm + list(writes) + list(scratch) + ["sems", "send_sems", "recv_sems"]
    got = pl.pallas_call(
        functools.partial(kernel, names, scopes),
        in_specs=[SMEM] * len(smem) + [VMEM] * len(vmem) + [ANY] * len(hbm),
        out_specs=[ANY] * len(writes),
        out_shape=list(writes.values()),
        scratch_shapes=[pltpu.VMEM(shape, dtype) for shape, dtype in scratch.values()]
        + [pltpu.SemaphoreType.DMA((100,)), pltpu.SemaphoreType.DMA((4,)), pltpu.SemaphoreType.DMA((4,))],
        compiler_params=pltpu.CompilerParams(vmem_limit_bytes=LIMIT, collective_id=2, has_side_effects=True),
        cost_estimate=pl.CostEstimate(flops=flops, bytes_accessed=40_000_000, transcendentals=0),
        name="relay",
    )(*[world[n] for n in smem + vmem + hbm])
    world.update(zip(writes, got))


TILE = 256
DEEP = 192


class Job:
    def __init__(self, fill, rows, cols, outs, kind=""):
        self.fill, self.rows, self.cols, self.outs, self.kind = fill, rows, cols, outs, kind
        self.depth = rows * (cols // TILE)


class Feed:
    def __init__(self, cp, lefts, rights):
        self.cp, self.lefts, self.rights = cp, lefts, rights
        self.plan, self.at, self.started = [], 0, 0

    def add(self, left, right):
        here = sum(1 for step in self.plan if step[1] is not None) + (right is not None) - 1
        self.plan.append((left, right, len(self.plan) % 2, here % 2))

    def start(self):
        if self.started < len(self.plan):
            left, right, a, b = self.plan[self.started]
            copies = [self.cp.load(left, self.lefts.at[a])]
            if right is not None:
                copies.append(self.cp.load(right, self.rights.at[b, :, pl.ds(0, right.shape[1])]))
            self.plan[self.started] = (copies, right, a, b)
            self.started += 1

    def take(self):
        if self.started == 0:
            self.start()
        self.start()
        copies, _, a, b = self.plan[self.at]
        for copy in copies:
            copy.wait()
        self.at += 1
        return self.lefts.at[a], self.rights.at[b]


def reduce_kernel(names, *refs):
    r = Refs(names, refs)
    section, place = lax.axis_index("section"), lax.axis_index("dp")
    core, y, z = place % 2, place // 2 % 2, place // 4
    partner = (1 - section, place)
    beside = place + 1 - 2 * core
    across = place + 2 - 4 * y
    along = [place + 4 * (1 - 2 * (z % 2)), place + 4 * (2 - 4 * (z // 2)), place + 4 * (3 - 2 * z)]
    far = [z + 1 - 2 * (z % 2), z + 2 - 4 * (z // 2), 3 - z]
    for other in [beside, across] + along:
        greet((section, other))
    tokens, model = r.df.shape
    part, high, tall = model // 16, r.hidden.shape[1] // 16, r.wk.shape[0] // 16
    total_rows, width = r.images.shape
    row_count = r.dkey.shape[0]
    patches = total_rows // row_count
    chunk = total_rows // PIECES
    vm = pltpu.VMEM

    def send(number, kind, source, target, other):
        copy = pltpu.make_async_remote_copy(
            src_ref=source, dst_ref=target, send_sem=r.send_sems.at[number, kind],
            recv_sem=r.recv_sems.at[number, kind], device_id=(section, other), device_id_type=pl.DeviceIdType.MESH,
        )
        copy.start()
        return copy

    def over(number, source, target):
        return pltpu.make_async_remote_copy(
            src_ref=source, dst_ref=target, send_sem=r.far_sends.at[number], recv_sem=r.far_recvs.at[number],
            device_id=partner, device_id_type=pl.DeviceIdType.MESH,
        )

    def lay_out(slot, got, rows, each=None):
        each = each or rows
        for k in range(got.shape[1] // TILE):
            piece = got[:, k * TILE : k * TILE + TILE].reshape(4, 2, 2, rows, TILE)
            r.tile[slot, :, :, :, k * each : k * each + rows, :] = piece

    def norm_rows(slot, rows, each):
        sums = jnp.sum(r.sums[0] + r.sums[1], 2).reshape(6, model)
        sums = jnp.concatenate([sums, jnp.zeros((10, model), F32)], 0)
        row = lax.broadcasted_iota(jnp.int32, (16, TILE), 0)
        for k in range(model // TILE):
            col = lax.broadcasted_iota(jnp.int32, (16, TILE), 1) + k * TILE
            owner = jnp.where(row < 4, col // part, col % (model // 2) // (part // 2))
            value = sums[:, k * TILE : k * TILE + TILE]
            at = pl.ds(k * each + rows, 16)
            for d in range(16):
                r.tile[slot, d // 4, d // 2 % 2, d % 2, at, :] = jnp.where(owner == d, value, 0.0).astype(BF)

    def product(feed, left, right, cols, rows, norms=False, order=False):
        feed.add(left, right.at[:, cols])

        def fill(slot):
            left_s, right_s = feed.take()
            value = left_s[...]
            if order:
                value = nn(value, r.order_s[...]).astype(BF)
            lay_out(slot, tn(value, right_s[:, : cols.size]).astype(BF), rows, rows + 16 if norms else rows)
            if norms:
                norm_rows(slot, rows, rows + 16)

        return fill

    def stacked(feed, left, right, cols, rows):
        for j in range(4):
            feed.add(left.at[:, pl.ds(j * 4 * rows, 4 * rows)], right.at[:, cols] if j == 0 else None)

        def fill(slot):
            for j in range(4):
                left_s, right_s = feed.take()
                got = tn(left_s[...], right_s[:, : cols.size]).astype(BF)
                r.tile[slot, j, :, :, :rows, :] = got.reshape(2, 2, rows, TILE)

        return fill

    def pictured(cp, flat):
        def fill(slot):
            def body(pix_s):
                cp.load(r.images, pix_s).wait()
                lay_out(slot, tn(pix_s[...], flat[...]).astype(BF), tall)

            pl.run_scoped(body, vm((total_rows, width), BF))

        return fill

    def run(cp, jobs, meet, tasks):
        cores, ys, zs = {}, {}, {}
        total = len(jobs)
        sent = []
        for i in range(total + 4):
            kind = jobs[i].kind if i < total else "none"
            if i < total and i - 3 in cores:
                cores[i - 3].wait_send()
            if kind in ("", "give"):
                slot, deep = i % 3, pl.ds(0, jobs[i].depth)
                jobs[i].fill(slot)
                if i == 0:
                    meet()
                cores[i] = send(i, 0, r.tile.at[slot, :, :, 1 - core, deep], r.core_in.at[i, :, :, deep], beside)
            for task in tasks.get(i, ()):
                task()
            if kind in ("", "give"):
                cores[i].wait_recv()

                @pl.loop(0, 4)
                def _(a):
                    for b in range(2):
                        r.core_in[i, a, b, deep, :] = r.core_in[i, a, b, deep, :] + r.tile[slot, a, b, core, deep, :]

            if i < total:
                deep = pl.ds(0, jobs[i].depth)
                if kind:
                    handed = over(marks[3], r.core_in.at[i, :, :, deep], r.core_in.at[handed_to, :, :, deep])
                if kind == "give":
                    handed.start()
                    sent.append(handed)
                else:
                    if kind == "take":
                        handed.wait_recv()
                    ys[i] = send(i, 1, r.core_in.at[i, :, 1 - y, deep], r.y_in.at[i, :, deep], across)
            j = i - 2
            if 0 <= j < total and jobs[j].kind != "give":
                ys[j].wait_recv()
                deep = pl.ds(0, jobs[j].depth)

                @pl.loop(0, 4)
                def _(a):
                    r.y_in[j, a, deep, :] = r.y_in[j, a, deep, :] + r.core_in[j, a, y, deep, :]

                for step in range(3):
                    zs[j, step] = send(
                        j, 2 + step, r.y_in.at[j, far[step], deep], r.z_in.at[j, step, deep], along[step]
                    )
            j = i - 4
            if 0 <= j < total and jobs[j].kind != "give":
                for step in range(3):
                    zs[j, step].wait_recv()
                deep = pl.ds(0, jobs[j].depth)
                r.final[j, deep, :] = (
                    r.y_in[j, z, deep, :].astype(F32) + r.z_in[j, 0, deep, :].astype(F32)
                ) + (r.z_in[j, 1, deep, :].astype(F32) + r.z_in[j, 2, deep, :].astype(F32))
                each = jobs[j].rows
                for k in range(jobs[j].cols // TILE):
                    for row, rows, target, first, number in jobs[j].outs:
                        source = r.final.at[j, pl.ds(k * each + row, rows)]
                        target = target.at[:, pl.ds(first + k * TILE, TILE)]
                        if number is None:
                            cp.store(source, target)
                        else:
                            sent.append(over(number + k, source, target))
                            sent[-1].start()
        for i in range(total):
            if i >= total - 3 and i in cores:
                cores[i].wait_send()
            if i in ys:
                ys[i].wait_send()
                for step in range(3):
                    zs[i, step].wait_send()
        for copy in sent:
            copy.wait_send()
        cp.finish()

    def ffn_jobs(feed):
        jobs = []
        for at in range(0, model, TILE):
            jobs.append(Job(stacked(feed, r.hidden, r.df, pl.ds(at, TILE), high), high, TILE, [(0, high, r.down, at, None)]))
        wide = DEEP // part * TILE
        for at in range(0, r.hidden.shape[1], wide):
            jobs.append(Job(product(feed, r.zb, r.du, pl.ds(at, wide), part), part, wide, [(0, part, r.up, at, None)]))
        return jobs

    def self_jobs(feed, norms):
        outs = [(0, part, r.out, 0, None)] + ([(part, 16, r.norms, 0, None)] if norms else [])
        jobs = [Job(product(feed, r.att, r.da, pl.ds(0, model), part, norms), part + 16 * norms, model, outs)]
        at = 0
        for wide in (model, model, 2 * TILE, TILE):
            jobs.append(Job(product(feed, r.entry, r.dqkv, pl.ds(at, wide), part), part, wide,
                            [(0, part, r.qkv, at, None)]))
            at += wide
        return jobs

    parcels, handed_to = model // TILE, 7
    marks = [PIECES + parcels * n for n in range(4)]

    @pl.when(section == 0)
    def _():
        cp = Copies(r.sems)

        def meet():
            greeted(6)
            greet(partner)

        def widen(c):
            over(c, r.far_s.at[c], r.far_s.at[c]).wait_recv()
            if c > 1:
                cp.settle(stores[c - 2])
            r.own_s[c % 2] = r.far_s[c].astype(F32)
            stores.append(cp.store(r.own_s.at[c % 2], r.image_grad.at[pl.ds(c * chunk, chunk)]))

        feed = Feed(cp, r.left_s, r.right_s)
        jobs, stores = ffn_jobs(feed) + self_jobs(feed, True), []
        jobs.insert(handed_to, Job(None, tall, model, [(0, tall, r.wide, 0, None)], "take"))
        last = len(jobs) + 3
        run(cp, jobs, meet, {last - PIECES + c: [functools.partial(widen, c)] for c in range(PIECES)})
        for first, rows, target in ((marks[0], part // 2, r.cross_q), (marks[1], part // 2, r.cross_o),
                                    (marks[2], 16, r.far_norms)):
            for k in range(parcels):
                piece = target.at[:, pl.ds(k * TILE, TILE)]
                over(first + k, r.final.at[0, pl.ds(0, rows)], piece).wait_recv()

    @pl.when(section == 1)
    def _():
        cp = Copies(r.sems)
        feed = Feed(cp, r.left_s, r.right_s)
        first = ffn_jobs(feed)

        def meet():
            greeted(5)
            greet(partner)

        def flatten(source, flat, weight, weight_s):
            def body(grad_s, flat_s):
                copies = [cp.load(source, grad_s), cp.load(weight, weight_s)]
                if weight is r.wk:
                    copies.append(cp.load(r.order, r.order_s))
                for copy in copies:
                    copy.wait()
                for t in range(model // LANES):
                    lanes_at = slice(t * LANES, t * LANES + LANES)
                    for i in range(row_count):
                        flat_s[t % 2, pl.ds(i, patches, stride=row_count), :] = grad_s[
                            r.row_of[i], :patches, lanes_at
                        ].astype(F32)
                    flat[:, lanes_at] = flat_s[t % 2].astype(BF)

            pl.run_scoped(body, vm(r.dkey.shape, BF), vm((2, total_rows, LANES), F32))

        def pixel_grad(c):
            if c > 1:
                cp.settle(stores[c - 2])
            at, half = slice(c * chunk, c * chunk + chunk), width // 2
            r.far_s[c] = (nt(r.fk_s[at, :], r.wk_s[:half, :]) + nt(r.fv_s[at, :], r.wimg_s[:half, :])).astype(BF)
            if c == 0:
                greeted(1)
            over(c, r.far_s.at[c], r.far_s.at[c]).start()
            r.own_s[c % 2] = nt(r.fk_s[at, :], r.wk_s[half:, :]) + nt(r.fv_s[at, :], r.wimg_s[half:, :])
            stores.append(cp.store(r.own_s.at[c % 2], r.image_grad.at[pl.ds(c * chunk, chunk)]))

        stores = []
        own = part // 2
        joint = [
            Job(product(feed, r.dq, r.midb, pl.ds(0, model), part, False, True), part, model,
                [(0, own, r.cross_q, 0, marks[0]), (own, own, r.cross_q, 0, None)]),
            Job(pictured(cp, r.fk_s), tall, model, [], "give"),
            Job(product(feed, r.dca, r.catt, pl.ds(0, model), part, True, True), part + 16, model,
                [(0, own, r.cross_o, 0, marks[1]), (own, own, r.cross_o, 0, None), (part, 16, r.norms, 0, None),
                 (part, 16, r.far_norms, 0, marks[2])]),
            Job(pictured(cp, r.fv_s), tall, model, [(0, tall, r.wide, 0, None)]),
        ]
        tasks = {1: [lambda: flatten(r.dkey, r.fk_s, r.wk, r.wk_s)], 2: [lambda: flatten(r.dval, r.fv_s, r.wimg, r.wimg_s)]}
        for c, at in enumerate((4, 5, 6, 8, 10)):
            tasks[at] = [functools.partial(pixel_grad, c)]
        run(cp, first + joint + self_jobs(feed, False), meet, tasks)
        for c in range(PIECES):
            over(c, r.far_s.at[c], r.far_s.at[c]).wait_send()


def reduce_all(world, dp):
    tokens, model = world["df"].shape
    part, tall = model // dp, world["wk"].shape[0] // dp
    hidden, total_rows, width = world["hidden"].shape[1], world["images"].shape[0], world["images"].shape[1]
    jobs = 15
    chunk = total_rows // PIECES
    writes = dict(
        down=(hidden // dp, model), up=(part, hidden), qkv=(part, 3 * model), out=(part, model), norms=(16, model),
        far_norms=(16, model), wide=(tall, model), cross_q=(part // 2, model), cross_o=(part // 2, model),
        image_grad=(total_rows, width // 2),
    )
    hbm = ["hidden", "df", "zb", "du", "att", "da", "entry", "dqkv", "dq", "midb", "dca", "catt", "images", "dkey",
           "dval", "wk", "wimg", "order"]
    vm = pltpu.VMEM
    scratch = dict(
        tile=vm((3, 4, 2, 2, DEEP, TILE), BF), core_in=vm((jobs, 4, 2, DEEP, TILE), BF),
        y_in=vm((jobs, 4, DEEP, TILE), BF), z_in=vm((jobs, 3, DEEP, TILE), BF), final=vm((jobs, DEEP, TILE), F32),
        left_s=vm((2, tokens, model), BF), right_s=vm((2, tokens, hidden // 3), BF), order_s=vm((model, model), BF),
        fk_s=vm((total_rows, model), BF), fv_s=vm((total_rows, model), BF), wk_s=vm((width, model), BF),
        wimg_s=vm((width, model), BF), far_s=vm((PIECES, chunk, width // 2), BF), own_s=vm((2, chunk, width // 2), F32),
        sems=pltpu.SemaphoreType.DMA((128,)), send_sems=pltpu.SemaphoreType.DMA((jobs, 5)),
        recv_sems=pltpu.SemaphoreType.DMA((jobs, 5)),
        far_sends=pltpu.SemaphoreType.DMA((PIECES + 4 * (model // TILE),)),
        far_recvs=pltpu.SemaphoreType.DMA((PIECES + 4 * (model // TILE),)),
    )
    names = ["row_of", "sums"] + hbm + list(writes) + list(scratch)
    got = pl.pallas_call(
        functools.partial(reduce_kernel, names),
        in_specs=[SMEM, VMEM] + [ANY] * len(hbm),
        out_specs=[ANY] * len(writes),
        out_shape=[jax.ShapeDtypeStruct(shape, F32) for shape in writes.values()],
        scratch_shapes=list(scratch.values()),
        compiler_params=pltpu.CompilerParams(vmem_limit_bytes=LIMIT, collective_id=1, has_side_effects=True),
        cost_estimate=pl.CostEstimate(flops=20_000_000_000, bytes_accessed=40_000_000, transcendentals=0),
        name="reduce_all",
    )(world["row_of"], world["sums"], *[world[n] for n in hbm])
    return dict(zip(writes, got))


def reduce_plain(world, dp):
    model, width = world["df"].shape[1], world["images"].shape[1]
    is_text = lax.axis_index("section") == 0
    place = lax.axis_index("dp")

    def total(value):
        return lax.psum_scatter(value, "dp", scatter_dimension=0, tiled=True).astype(F32)

    def by_owner(value):
        own = value.reshape(2, dp, model // (2 * dp), model)
        return jnp.swapaxes(own, 0, 1).reshape(model, model)

    def grad(left, right):
        return total(tn(world[left], world[right]).astype(BF))

    def flat(value):
        value = value[world["row_of"], : world["images"].shape[0] // value.shape[0]]
        return jnp.swapaxes(value, 0, 1).reshape(-1, model)

    def over(value):
        return lax.ppermute(value, "section", [(1, 0)])

    dkey, dval = flat(world["dkey"]), flat(world["dval"])
    pixels = nt(dkey, world["wk"]) + nt(dval, world["wimg"])
    far = over(pixels[:, : width // 2].astype(BF)).astype(F32)
    wide_k, wide_v = (total(tn(world["images"], g).astype(BF)) for g in (dkey, dval))
    cross_q, cross_o = (
        total(by_owner(tn(world[a], world[b]).astype(BF))) for a, b in (("dq", "midb"), ("dca", "catt"))
    )
    own = cross_q.shape[0] // 2
    norms = lax.psum(jnp.sum(world["sums"], (0, 3)).reshape(6, model).at[4:].multiply(jnp.where(is_text, 0.0, 1.0)), "dp")
    del place
    return dict(
        down=grad("hidden", "df"), up=grad("zb", "du"), qkv=grad("entry", "dqkv"), out=grad("att", "da"), norms=norms,
        far_norms=over(norms), wide=jnp.where(is_text, over(wide_k), wide_v),
        cross_q=jnp.where(is_text, over(cross_q[:own]), cross_q[own:]),
        cross_o=jnp.where(is_text, over(cross_o[:own]), cross_o[own:]),
        image_grad=jnp.where(is_text, far, pixels[:, width // 2 :]),
    )


def per_device(
    text_in, cotangent, images, segment_ids, row_image, self_qkv, self_out, ffn_up, ffn_down,
    norm_gain, norm_bias, image_kv, cross_query, cross_out, cross_gain, cross_bias,
):
    tokens, model = text_in.shape
    row_total, length = segment_ids.shape
    patches, width = images.shape[1:]
    hidden_width = ffn_up.shape[2]
    block_rows = row_image.shape[1]
    head_dim = model // HEADS
    pairs = HEADS // 2
    count = tokens // HALVES
    half_rows = row_total // HALVES
    span = 2 * length
    dp = lax.axis_size("dp")
    section = lax.axis_index("section")
    is_text = section == 0
    flag = section.astype(jnp.int32).reshape(1)
    place = lax.axis_index("dp")
    wqkv, wo, w1, w2 = self_qkv[0], self_out[0], ffn_up[0], ffn_down[0]
    gains, biases = norm_gain[0], norm_bias[0]
    cgain, cbias = cross_gain, cross_bias

    marks = (segment_ids + segment_ids.shape[1] * (jnp.arange(row_total, dtype=jnp.int32) % 2)[:, None]).reshape(-1, span)
    mask = jnp.where(marks[:, :, None] == jnp.tile(marks, (1, 2))[:, None, :], 0.0, MASKED).astype(F32)
    in_block = jnp.arange(row_total, dtype=jnp.int32) // block_rows * block_rows
    image = row_image.reshape(-1) + in_block
    slots = jnp.arange(block_rows, dtype=jnp.int32)
    row_of = jnp.sum(jnp.where(row_image[:, :, None] == slots, slots[:, None], 0), 1).reshape(-1) + in_block

    def shape(*dims, dtype=BF):
        return jax.ShapeDtypeStruct(dims, dtype)

    flat_rows = row_total * patches
    pixels = jnp.swapaxes(images, 0, 1).reshape(flat_rows, width)
    probs_shape = (count // span * pairs, span, 2 * span)
    world = dict(
        image=image, row_of=row_of, gains=gains, biases=biases, cgain=cgain, cbias=cbias, mask=mask, text=text_in,
        cot=cotangent, images=pixels, wqkv=wqkv, wo=wo, w1=w1, w2=w2, wq=cross_query, wc=cross_out, wimg=image_kv,
    )
    small_f, small_b = ((count, model), F32), ((count, model), BF)
    tall_b, wide_b = ((count, hidden_width), BF), ((count, 3 * model), BF)
    picture_b, pictures_b = ((half_rows, PAD, model), BF), ((row_total, PAD, model), BF)
    scratch = dict(
        wqkv_s=(wqkv.shape, BF), wo_s=(wo.shape, BF), w1_s=(w1.shape, BF), w2_s=(w2.shape, BF),
        wq_s=(cross_query.shape, BF), wc_s=(cross_out.shape, BF), wimg_s=(image_kv.shape, BF),
        wk_s=(image_kv.shape, BF), key_s=pictures_b, val_s=pictures_b, bnd_s=((HALVES, count, model), BF),
        x_s=small_b, back_s=small_b,
    )
    layer_s = dict(
        qkv_s=wide_b, probs_s=(probs_shape, BF), att_s=small_b, y1_s=small_f, mid_s=small_f, zb_s=small_b,
        pre_s=small_f, hid_s=tall_b, slo_s=tall_b, y3_s=small_f, lay_s=small_b, g_s=small_b, midb_s=small_b,
        qc_s=small_f, cprobs_s=((half_rows * pairs, PAD, 2 * length), BF), cat_s=small_f, catb_s=small_b,
        y2_s=small_f, df_s=small_b, dy_s=small_f, dkey_s=picture_b, dval_s=picture_b, dqkv_s=wide_b,
        sum_s=((3, 2, 8, model), F32),
    )
    flat_s = ((model // LANES, flat_rows, LANES), F32)
    first_s = dict(pix_s=((flat_rows, width), BF), flat_s=flat_s)
    tokens_b = shape(tokens, model)
    writes = dict(
        lay=tokens_b, zb=tokens_b, hidden=shape(tokens, hidden_width), att=tokens_b, entry=tokens_b,
        ig=shape(tokens, model, dtype=F32), df=tokens_b, du=shape(tokens, hidden_width), da=tokens_b,
        dqkv=shape(tokens, 3 * model), sums=shape(HALVES, 3, 2, 8, model, dtype=F32), midb=tokens_b, dq=tokens_b,
        catt=tokens_b, dca=tokens_b, dkey=shape(row_total, PAD, model), dval=shape(row_total, PAD, model),
        wk=shape(width, model), y1=shape(HALVES, count, model, dtype=F32),
        y3=shape(HALVES, count, model, dtype=F32), qkv=shape(HALVES, count, 3 * model),
        probs=shape(HALVES, *probs_shape), slope=shape(HALVES, count, hidden_width),
    )
    linear = model * 3 * model + model * model + 2 * model * hidden_width
    reads = (
        ["image"], ["gains", "biases", "mask", "cgain", "cbias"],
        ["text", "cot", "images", "wqkv", "wo", "w1", "w2", "wq", "wc", "wimg"],
    )
    relay(
        world, reads, writes, scratch, (layer_s, first_s),
        functools.partial(relay_kernel, HALVES, span, length, patches), 8 * count * (linear + 2 * model * model),
    )
    new, own = np.arange(model), model // (2 * dp)
    source = new % (2 * own) // own * (model // 2) + new // (2 * own) * own + new % own
    world["order"] = jnp.asarray(new[:, None] == source, BF)
    world["row_of"] = row_of
    got = reduce_all(world, dp) if dp == 16 else reduce_plain(world, dp)
    out_rows = model // dp
    cross_rows = out_rows // lax.axis_size("section")
    norm_part = lax.dynamic_slice_in_dim(got["norms"][:4], place * out_rows, out_rows, 1).reshape(2, 2, out_rows)
    cross_part = jnp.where(is_text, got["far_norms"][4:6], got["norms"][4:6])
    cross_part = lax.dynamic_slice_in_dim(cross_part, (section * dp + place) * cross_rows, cross_rows, 1)
    image_grad = jnp.swapaxes(got["image_grad"].reshape(patches, row_total, width // 2), 0, 1)
    return (
        world["lay"][None], world["ig"][None], image_grad, got["qkv"][None], got["out"][None], got["up"][None],
        got["down"][None], norm_part[:, 0][None], norm_part[:, 1][None], got["wide"], got["cross_q"].T,
        got["cross_o"].T, cross_part[0], cross_part[1],
    )


def solution(mesh):
    return jax.shard_map(
        per_device,
        mesh=mesh,
        in_specs=(
            P("dp", None),
            P("dp", None),
            P("dp", None, None),
            P("dp", None),
            P("dp", None),
            P("section", None, None),
            P("section", None, None),
            P("section", None, None),
            P("section", None, None),
            P("section", None, None),
            P("section", None, None),
            P(None, "section"),
            P(),
            P(),
            P(),
            P(),
        ),
        out_specs=(
            P("section", "dp", None),
            P("section", "dp", None),
            P("dp", None, "section"),
            P("section", "dp", None),
            P("section", "dp", None),
            P("section", "dp", None),
            P("section", "dp", None),
            P("section", None, "dp"),
            P("section", None, "dp"),
            P("dp", "section"),
            P(None, ("section", "dp")),
            P(None, ("section", "dp")),
            P(("section", "dp")),
            P(("section", "dp")),
        ),
        check_vma=False,
    )
```
